32 devices in a mesh: inst: 2 (over x), dom: 16 (over z, y, core).
Axes of the slice: x: 2, y: 2, z: 4, core: 2. Of those that a mesh axis runs over, the one named last changes fastest.
Arguments:
- initial_state: bfloat16 [8, 256, 320], P('inst', 'dom'), may hold values from -6 to 6
- forcing: bfloat16 [8, 256, 320], P('inst', 'dom'), may hold values from -6 to 6
- diagonal_blocks: bfloat16 [256, 320, 320], P('dom'), may hold values from -0.3125 to 0.3125
- flux_jacobian: bfloat16 [256, 2400], P('dom'), may hold values from -0.5 to 0.5
- send_list: int32 [16, 4, 8], P('dom'), may hold values from 0 to 96, as said below
- source_index: int32 [256, 6], P('dom'), may hold values from 0 to 128, as said below
- frequency: float32 [1], replicated, may hold values from 0.5 to 2
Outputs:
- final_state: bfloat16 [8, 256, 320], P('inst', 'dom')
- final_residual: float32 [8, 256, 320], P('inst', 'dom')
The draws below stay inside these ranges and needn't reach their ends.
Inputs may be any that keep to these rules, and one draw needn't show every extreme that they name: `send_list`: entry [p, k, c] is a face-block 6 e + f of partition p (its element e, face f) that partition p sends to partition p + o_k; the value 6 * 16 marks an empty slot, and used slots come first in each row. Slots toward partitions outside the mesh are empty. No partition sends more than 8 face-blocks to one neighbour, and in every draw some partition sends exactly 8. `source_index`: values under 6 * 16 name a face-block of the element's own partition; 96 + k * 8 + c names slot c of what partition p + o_k sends toward offset -o_k; the largest value marks a boundary face without neighbour. Every used slot sent to a partition is named by exactly one face of that partition.
All inputs are finite; a program needn't handle non-finite values.
Results may differ from the reference program's by a relative error of at most 0.014.
Values may be sent and summed in bfloat16 or wider, within the bound.
No kernel may reach another device: no remote copies, remote signals or barrier semaphores. Data moves between devices by JAX's collectives and lax.ppermute only.
A program may use at most 64 MiB of HBM per device.

```python
import math
import jax
import jax.numpy as jnp
import numpy as np
from jax import lax

FIELDS = 5
ORDER = 3
NODES = 64
FPTS = 16
NI = 8
ELEM_DEV = 16
REACH = 2
CAP = 8
ITERS = 2
NE = 256
N_DOM = 16


def draw_topology(key):
    base = jax.random.fold_in(key, 11)
    key_counts, key_faces, key_order, key_local, key_bound = jax.random.split(base, 5)
    face_count = 6 * ELEM_DEV
    slots = 2 * REACH
    offsets = jnp.concatenate([jnp.arange(-REACH, 0), jnp.arange(1, REACH + 1)]).astype(jnp.int32)
    part_ids = jnp.arange(N_DOM, dtype=jnp.int32)[:, None]
    targets = part_ids + offsets[None, :]
    usable = (targets >= 0) & (targets < N_DOM)
    counts = jax.random.randint(key_counts, (N_DOM, slots), 1, CAP + 1)
    counts = jnp.where(offsets[None, :] == 1, CAP, counts)
    counts = jnp.where(usable, counts, 0)
    chosen = jax.random.randint(key_faces, (N_DOM, slots, CAP), 0, face_count)
    live = jnp.arange(CAP)[None, None, :] < counts[:, :, None]
    send_list = jnp.where(live, chosen, face_count).astype(jnp.int32)
    sender = jnp.clip(targets, 0, N_DOM - 1)
    mirrored = counts[sender, slots - 1 - jnp.arange(slots)[None, :]]
    arriving = jnp.where(usable, mirrored, 0)
    live_in = (jnp.arange(CAP)[None, None, :] < arriving[:, :, None]).reshape(N_DOM, slots * CAP)
    order_keys = jax.random.split(key_order, N_DOM)
    orders = jax.vmap(lambda single: jax.random.permutation(single, face_count))(order_keys)
    ranks = jnp.argsort(orders, axis=1).astype(jnp.int32)
    fallback = jax.random.randint(key_local, (N_DOM, face_count), 0, face_count)
    boundary = jax.random.randint(key_bound, (N_DOM, face_count), 0, 8) == 0
    boundary = boundary | (ranks == face_count - 1)
    empty_row = face_count + slots * CAP
    fallback = jnp.where(boundary, empty_row, fallback)
    remote_ok = ranks < slots * CAP
    remote_live = jnp.take_along_axis(live_in, jnp.clip(ranks, 0, slots * CAP - 1), axis=1)
    source_index = jnp.where(remote_ok & remote_live, face_count + ranks, fallback)
    return (send_list, source_index.reshape(N_DOM * ELEM_DEV, 6).astype(jnp.int32))


def draw_send_list(key, part):
    return draw_topology(key)[0]


def draw_source_index(key, part):
    return draw_topology(key)[1]


def shard_levels(key, shape, shards, least, top_value):
    factor_of, own = 1.0, jax.random.fold_in(key, 6)
    for dim, shards_of in shards:
        heights = jnp.exp(jax.random.uniform(jax.random.fold_in(own, dim), (shards_of,), jnp.float32, least / len(shards), top_value / len(shards)))
        factor_of = factor_of * jnp.repeat(heights, shape[dim] // shards_of).reshape([-1 if axis == dim else 1 for axis in range(len(shape))])
    return factor_of


def centred(stream_key, extent, width, bound, pieces=(), kind=jnp.bfloat16):
    drawn = jax.random.normal(stream_key, extent, jnp.float32) * width
    if len(pieces) > 0:
        drawn = shard_levels(stream_key, extent, pieces, -0.22, 0.18) * drawn
    return jnp.clip(drawn, min=-bound, max=bound).astype(kind)


def setup_inputs(seed: int = 0) -> dict:
    streams_of = jax.random.split(jax.random.key(seed), 8)
    return {
        "initial_state": centred(streams_of[0], (NI, NE, FIELDS * NODES), 1.0, 6.0, ((0, 2), (1, 16))),
        "forcing": centred(streams_of[1], (NI, NE, FIELDS * NODES), 1.0, 6.0, ((0, 2), (1, 16))),
        "diagonal_blocks": centred(streams_of[2], (NE, FIELDS * NODES, FIELDS * NODES), (FIELDS * NODES) ** -0.5, 0.3125, ((0, 16),)),
        "flux_jacobian": centred(streams_of[3], (NE, 6 * FIELDS * FIELDS * FPTS), 0.08, 0.5, ((0, 16),)),
        "send_list": draw_send_list(jax.random.fold_in(streams_of[7], 71), 0),
        "source_index": draw_source_index(jax.random.fold_in(streams_of[7], 71), 0),
        "frequency": jnp.clip(jnp.exp(jax.random.uniform(streams_of[6], (1,), jnp.float32, math.log(0.5), math.log(2.0))), 0.5, 2.0),
    }


pseudo_step = 0.5
dissipation = 0.25


def gauss_legendre(count):
    points = []
    weights = []
    for i in range(count):
        where = math.cos(math.pi * (i + 0.75) / (count + 0.5))
        for sweep in range(100):
            before = 1.0
            value = where
            for j in range(2, count + 1):
                after = ((2 * j - 1) * where * value - (j - 1) * before) / j
                before = value
                value = after
            if count == 1:
                before = 1.0
                value = where
            slope = count * (where * value - before) / (where * where - 1.0)
            where = where - value / slope
        before = 1.0
        value = where
        for j in range(2, count + 1):
            after = ((2 * j - 1) * where * value - (j - 1) * before) / j
            before = value
            value = after
        slope = count * (where * value - before) / (where * where - 1.0)
        points.append(where)
        weights.append(2.0 / ((1.0 - where * where) * slope * slope))
    return np.array(points[::-1]), np.array(weights[::-1])


def lagrange_at(points, where):
    values = np.ones(points.shape[0])
    for i in range(points.shape[0]):
        for j in range(points.shape[0]):
            if j != i:
                values[i] = values[i] * (where - points[j]) / (points[i] - points[j])
    return values


def tables(order, count):
    points, weights = gauss_legendre(order + 1)
    at_minus = lagrange_at(points, -1.0)
    at_plus = lagrange_at(points, 1.0)
    per_side = order + 1
    node_count = per_side ** 3
    face_points = per_side ** 2
    trace_table = np.zeros((node_count, 6 * face_points))
    lift_table = np.zeros((node_count, 6 * face_points))
    for k in range(per_side):
        for j in range(per_side):
            for i in range(per_side):
                node = i + per_side * j + per_side * per_side * k
                entries = [(0, at_minus[i], j + per_side * k, weights[i]),
                           (1, at_plus[i], j + per_side * k, weights[i]),
                           (2, at_minus[j], i + per_side * k, weights[j]),
                           (3, at_plus[j], i + per_side * k, weights[j]),
                           (4, at_minus[k], i + per_side * j, weights[k]),
                           (5, at_plus[k], i + per_side * j, weights[k])]
                for face_index, factor, point, weight in entries:
                    trace_table[node, face_index * face_points + point] = factor
                    lift_table[node, face_index * face_points + point] = factor / weight
    spectral = np.zeros((count, count))
    second = np.zeros((count, count))
    for t in range(count):
        for s in range(count):
            if t != s:
                spectral[t, s] = 0.5 * (-1.0) ** (t - s + 1) / math.tan(math.pi * (t - s) / count)
                second[t, s] = -0.5 * (-1.0) ** (t - s) / math.sin(math.pi * (t - s) / count) ** 2
            else:
                second[t, s] = -(count * count + 2.0) / 12.0
    return trace_table, lift_table, spectral, second


def reference(initial_state, forcing, diagonal_blocks, flux_jacobian, send_list, source_index, frequency):
    trace_np, lift_np, spectral_np, second_np = tables(ORDER, NI)
    trace_table = jnp.asarray(trace_np, jnp.float32)
    lift_table = jnp.asarray(lift_np, jnp.float32).reshape(NODES, 6, FPTS)
    coupler = frequency[0] * jnp.asarray(spectral_np, jnp.float32) - dissipation * jnp.asarray(second_np, jnp.float32)
    face_count = 6 * ELEM_DEV
    slots = 2 * REACH
    offsets = np.concatenate([np.arange(-REACH, 0), np.arange(1, REACH + 1)])
    offset_table = jnp.asarray(offsets, jnp.int32)
    part_ids = jnp.arange(N_DOM, dtype=jnp.int32)[:, None]
    local_source = source_index.reshape(N_DOM, face_count)
    remote_slot = local_source - face_count
    from_local = local_source < face_count
    from_remote = (remote_slot >= 0) & (remote_slot < slots * CAP)
    clipped = jnp.clip(remote_slot, 0, slots * CAP - 1)
    slot_group = clipped // CAP
    slot_place = clipped % CAP
    sender = part_ids + offset_table[slot_group]
    usable = from_remote & (sender >= 0) & (sender < N_DOM)
    sender_safe = jnp.clip(sender, 0, N_DOM - 1)
    sent_face = send_list[sender_safe, slots - 1 - slot_group, slot_place]
    usable = usable & (sent_face < face_count)
    zero_row = N_DOM * face_count
    global_row = jnp.where(from_local, part_ids * face_count + local_source,
                           jnp.where(usable, sender_safe * face_count + sent_face, zero_row))
    global_row = global_row.reshape(NE * 6).astype(jnp.int32)
    flux_blocks = flux_jacobian.reshape(NE, 6, FIELDS, FIELDS, FPTS).astype(jnp.float32)
    blocks_wide = diagonal_blocks.astype(jnp.float32)
    forcing_wide = forcing.astype(jnp.float32)
    current = initial_state
    residual = jnp.zeros(forcing.shape, jnp.float32)
    for iteration in range(ITERS):
        current_wide = current.astype(jnp.float32)
        traces = jnp.einsum('iecn,nm->iecm', current_wide.reshape(NI, NE, FIELDS, NODES), trace_table,
                            precision=lax.Precision.HIGHEST).astype(jnp.bfloat16)
        face_rows = traces.reshape(NI, NE, FIELDS, 6, FPTS).transpose(1, 3, 0, 2, 4).reshape(NE * 6, NI * FIELDS * FPTS)
        face_pool = jnp.concatenate([face_rows, jnp.zeros((1, NI * FIELDS * FPTS), jnp.bfloat16)], 0)
        picked = face_pool[global_row].reshape(NE, 6, NI, FIELDS, FPTS).astype(jnp.float32)
        normal_flux = jnp.einsum('efcdq,efidq->eifcq', flux_blocks, picked, precision=lax.Precision.HIGHEST)
        lifted = jnp.einsum('eifcq,nfq->iecn', normal_flux, lift_table, precision=lax.Precision.HIGHEST)
        lifted = lifted.reshape(NI, NE, FIELDS * NODES)
        coupling = jnp.einsum('ts,sem->tem', coupler, current_wide,
                              precision=lax.Precision.HIGHEST).astype(jnp.bfloat16)
        diagonal_term = jnp.einsum('iem,emn->ien', current_wide, blocks_wide, precision=lax.Precision.HIGHEST)
        residual = diagonal_term + lifted + coupling.astype(jnp.float32) - forcing_wide
        current = (current_wide - pseudo_step * residual).astype(jnp.bfloat16)
    return current, residual
```

```python
import functools
import math

import jax
import jax.numpy as jnp
import numpy as np
from jax import lax
from jax.experimental import pallas as pl
from jax.experimental.pallas import tpu as pltpu
from jax.sharding import PartitionSpec as P

FIELDS = 5
ORDER = 3
NODES = 64
FPTS = 16
NI = 8
REACH = 2
ITERS = 2


pseudo_step = 0.5
dissipation = 0.25


def gauss_legendre(count):
    points = []
    weights = []
    for i in range(count):
        where = math.cos(math.pi * (i + 0.75) / (count + 0.5))
        for sweep in range(100):
            before = 1.0
            value = where
            for j in range(2, count + 1):
                after = ((2 * j - 1) * where * value - (j - 1) * before) / j
                before = value
                value = after
            slope = count * (where * value - before) / (where * where - 1.0)
            where = where - value / slope
        before = 1.0
        value = where
        for j in range(2, count + 1):
            after = ((2 * j - 1) * where * value - (j - 1) * before) / j
            before = value
            value = after
        slope = count * (where * value - before) / (where * where - 1.0)
        points.append(where)
        weights.append(2.0 / ((1.0 - where * where) * slope * slope))
    return (np.array(points[::-1]), np.array(weights[::-1]))


def lagrange_at(points, where):
    values = np.ones(points.shape[0])
    for i in range(points.shape[0]):
        for j in range(points.shape[0]):
            if j != i:
                values[i] = values[i] * (where - points[j]) / (points[i] - points[j])
    return values


def tables(order, count):
    points, weights = gauss_legendre(order + 1)
    at_minus = lagrange_at(points, -1.0)
    at_plus = lagrange_at(points, 1.0)
    per_side = order + 1
    node_count = per_side**3
    face_points = per_side**2
    trace_table = np.zeros((node_count, 6 * face_points))
    lift_table = np.zeros((node_count, 6 * face_points))
    for k in range(per_side):
        for j in range(per_side):
            for i in range(per_side):
                node = i + per_side * j + per_side * per_side * k
                entries = [
                    (0, at_minus[i], j + per_side * k, weights[i]),
                    (1, at_plus[i], j + per_side * k, weights[i]),
                    (2, at_minus[j], i + per_side * k, weights[j]),
                    (3, at_plus[j], i + per_side * k, weights[j]),
                    (4, at_minus[k], i + per_side * j, weights[k]),
                    (5, at_plus[k], i + per_side * j, weights[k]),
                ]
                for face_index, factor, point, weight in entries:
                    trace_table[node, face_index * face_points + point] = factor
                    lift_table[node, face_index * face_points + point] = factor / weight
    spectral = np.zeros((count, count))
    second = np.zeros((count, count))
    for t in range(count):
        for s in range(count):
            if t != s:
                spectral[t, s] = 0.5 * (-1.0) ** (t - s + 1) / math.tan(math.pi * (t - s) / count)
                second[t, s] = -0.5 * (-1.0) ** (t - s) / math.sin(math.pi * (t - s) / count) ** 2
            else:
                second[t, s] = -(count * count + 2.0) / 12.0
    return (trace_table, lift_table, spectral, second)


LANE = 128
WIDE = FIELDS * NODES
FACES = 6
VMEM_LIMIT = 16 * 1024 * 1024
BF16 = jnp.bfloat16
F32 = jnp.float32
OFFSETS = list(range(-REACH, 0)) + list(range(1, REACH + 1))
SWAP_ORDER = (3, 1, 2, 0)


def wide_tables():
    trace_np, lift_np, spectral_np, second_np = tables(ORDER, NI)
    trace_wide = np.zeros((WIDE, FACES * LANE))
    lift_wide = np.zeros((FACES * LANE, WIDE))
    for c in range(FIELDS):
        rows = slice(c * NODES, (c + 1) * NODES)
        for f in range(FACES):
            cols = slice(f * LANE + c * FPTS, f * LANE + (c + 1) * FPTS)
            face = slice(f * FPTS, (f + 1) * FPTS)
            trace_wide[rows, cols] = trace_np[:, face]
            lift_wide[cols, rows] = lift_np[:, face].T
    return trace_wide, lift_wide, spectral_np[:, 0], second_np[:, 0]


def iotas(shape):
    return [lax.broadcasted_iota(jnp.int32, shape, axis) for axis in range(2)]


def one_hot(mask):
    return jnp.where(mask, 1.0, 0.0).astype(BF16)


def spread_table():
    row, col = iotas((LANE, FIELDS * LANE))
    inside = col % LANE < FIELDS * FPTS
    return one_hot(inside & (row == col // LANE * FPTS + col % FPTS))


def order_table():
    row, col = iotas((FIELDS * FIELDS * FPTS, FIELDS * LANE))
    place = col % LANE
    source = place // FPTS * FIELDS * FPTS + col // LANE * FPTS + col % FPTS
    return one_hot((place < FIELDS * FPTS) & (row == source))


def trace_pool(state, trace_wide, insts, elems):
    wide = jnp.dot(state, trace_wide, preferred_element_type=F32).astype(BF16)
    by_inst = []
    for t in range(insts):
        rows = wide[t * elems : (t + 1) * elems]
        by_inst.append(
            jnp.concatenate([rows[:, f * LANE : (f + 1) * LANE] for f in range(FACES)], 0)
        )
    return jnp.concatenate(by_inst, 1)


def swap_routes(ranks, parts):
    near = [[(p, p + 1) for p in range(first, parts - 1, 2)] for first in range(2)]
    far = [
        [(p + i, p + i + 2) for p in range(first, parts - 3, 4) for i in range(2)]
        for first in (0, 2)
    ]
    routes = []
    for pairs in near + far:
        met = {p for pair in pairs for p in pair}
        alone = [p for p in range(parts) if p not in met]
        swaps = [(r * parts + p, r * parts + q) for r in range(ranks) for p, q in pairs]
        swaps += [(r * parts + p, (r ^ 1) * parts + p) for r in range(0, ranks, 2) for p in alone]
        routes.append(swaps + [(q, p) for p, q in swaps])
    return routes


def by_swap(place, by_offset):
    two_down, one_down, one_up, two_up = by_offset
    even = place % 2 == 0
    low = place // 2 % 2 == 0
    return [
        jnp.where(even, one_up, one_down),
        jnp.where(even, one_down, one_up),
        jnp.where(low, two_up, two_down),
        jnp.where(low, two_down, two_up),
    ]


def by_offset(place, blocks):
    even = place % 2 == 0
    low = place // 2 % 2 == 0
    return [
        jnp.where(low, blocks[3], blocks[2]),
        jnp.where(even, blocks[1], blocks[0]),
        jnp.where(even, blocks[0], blocks[1]),
        jnp.where(low, blocks[2], blocks[3]),
    ]


def fill_outgoing(pool, send, out_refs, place, elems):
    slots, capacity = send.shape
    rows, cols = iotas((FACES * elems, slots * capacity))
    ids = FACES * (rows % elems) + rows // elems
    wanted = jnp.concatenate([send[k : k + 1] for k in range(slots)], 1)
    out = lax.dot_general(
        one_hot(ids == wanted), pool, (((0,), (0,)), ((), ())), preferred_element_type=F32
    )
    blocks = by_swap(place, [out[k * capacity : (k + 1) * capacity] for k in range(slots)])
    for block, ref in zip(blocks, out_refs):
        ref[...] = block.astype(BF16)


def diagonal(states, diag, wide_ref, prod_ref, insts, elems):
    tall = insts * elems
    width = diag.shape[1]
    cuts = [(j, j * LANE, min((j + 1) * LANE, width)) for j in range(pl.cdiv(width, LANE))]
    for t in range(insts):
        rows = states[t].astype(F32)
        for j, low, high in cuts:
            first = j * tall + t * elems
            wide_ref[first : first + elems, 0 : high - low] = rows[:, low:high]
    for e in range(elems):
        rows = jnp.concatenate(
            [wide_ref[pl.ds(j * tall + e, insts, stride=elems), :] for j, low, high in cuts], 1
        )
        product = jnp.dot(rows[:, 0:width].astype(BF16), diag[e], preferred_element_type=F32)
        for j, low, high in cuts:
            chunk = product[:, low:high]
            if high - low < LANE:
                chunk = jnp.concatenate([chunk, jnp.zeros((insts, LANE - high + low), F32)], 1)
            prod_ref[pl.ds(j * tall + e, insts, stride=elems), :] = chunk
    return [
        jnp.concatenate(
            [
                prod_ref[j * tall + t * elems : j * tall + (t + 1) * elems, 0 : high - low]
                for j, low, high in cuts
            ],
            1,
        )
        for t in range(insts)
    ]


def flux_order(rows, order):
    per_face = FIELDS * FIELDS * FPTS
    by_face = jnp.concatenate(
        [rows[:, f * per_face : (f + 1) * per_face] for f in range(FACES)], 0
    )
    return jnp.dot(by_face, order, preferred_element_type=F32).astype(BF16)


def source_table(sources, elems, slots):
    faces = FACES * elems
    columns = lax.broadcasted_iota(jnp.int32, (elems, faces + slots), 1)
    ids = jnp.where(columns < faces, FACES * (columns % elems) + columns // elems, columns)
    hot = [jnp.where(sources[:, f : f + 1] == ids, 1.0, 0.0) for f in range(FACES)]
    return jnp.concatenate(hot, 0).astype(BF16)


def table_kernel(spread_ref, order_ref):
    spread_ref[...] = spread_table()
    order_ref[...] = order_table()


def first_kernel(place_ref, order_ref, state_ref, trace_ref, send_ref, flux_ref, source_ref,
                 flux_out_ref, hot_ref, pool_ref, *out_refs):
    insts, elems, width = state_ref.shape
    state = state_ref[...].reshape(insts * elems, width)
    pool = trace_pool(state, trace_ref[...], insts, elems)
    pool_ref[...] = pool
    fill_outgoing(pool, send_ref[0], out_refs, place_ref[0], elems)
    hot_ref[...] = source_table(source_ref[...].T, elems, send_ref.shape[1] * send_ref.shape[2])
    flux_out_ref[...] = flux_order(flux_ref[...], order_ref[...])


def base_kernel(state_ref, diag_ref, forcing_ref, base_ref, wide_ref, prod_ref):
    insts, elems, width = state_ref.shape
    states = [state_ref[t] for t in range(insts)]
    products = diagonal(states, diag_ref, wide_ref, prod_ref, insts, elems)
    for t in range(insts):
        base_ref[t] = products[t] - forcing_ref[t].astype(F32)


def step_kernel(parts, ranks, last, spectral, second, *refs):
    place_ref, freq_ref, spread_ref = refs[:3]
    got_refs = {swap: refs[3 + i] for i, swap in enumerate(SWAP_ORDER)}
    got_refs = [got_refs[swap] for swap in range(len(OFFSETS))]
    refs = refs[3 + len(OFFSETS) :]
    states = refs[:ranks]
    pool_ref, refs = refs[ranks], refs[ranks + 1 :]
    base_ref, hot_ref, flux_ref, lift_ref = refs[:4]
    if last:
        final_ref, residual_ref = refs[4:]
    else:
        trace_ref, send_ref, next_ref, next_pool_ref = refs[4:8]
        out_refs = refs[8:]
    insts, elems, width = states[0].shape
    place = place_ref[0]
    faces = FACES * elems

    freq = freq_ref[...]
    entries = [freq * float(spectral[d]) - dissipation * float(second[d]) for d in range(NI)]

    arrived = by_offset(place, [ref[...].astype(F32) for ref in got_refs])
    for k, offset in enumerate(OFFSETS):
        exists = (place + offset >= 0) & (place + offset < parts)
        arrived[k] = jnp.where(exists, arrived[k], jnp.zeros_like(arrived[k]))
    pool = jnp.concatenate([pool_ref[...], jnp.concatenate(arrived, 0).astype(BF16)], 0)
    picked = jnp.dot(hot_ref[...], pool, preferred_element_type=F32).astype(BF16)
    stacked = jnp.concatenate([picked[:, t * LANE : (t + 1) * LANE] for t in range(insts)], 0)
    wide = jnp.dot(stacked, spread_ref[...], preferred_element_type=F32)

    flux = flux_ref[...].astype(F32)
    normal = []
    for t in range(insts):
        rows = wide[t * faces : (t + 1) * faces]
        summed = flux[:, 0:LANE] * rows[:, 0:LANE]
        for d in range(1, FIELDS):
            summed += flux[:, d * LANE : (d + 1) * LANE] * rows[:, d * LANE : (d + 1) * LANE]
        summed = summed.astype(BF16)
        normal.append(
            jnp.concatenate([summed[f * elems : (f + 1) * elems] for f in range(FACES)], 1)
        )
    lifted = jnp.dot(jnp.concatenate(normal, 0), lift_ref[...], preferred_element_type=F32)

    fresh = []
    for t in range(insts):
        summed = jnp.zeros((elems, width), F32)
        for rank in range(ranks):
            for s in range(insts):
                summed += entries[(t - s - rank * insts) % NI] * states[rank][s].astype(F32)
        residual = (
            base_ref[t] + lifted[t * elems : (t + 1) * elems] + summed.astype(BF16).astype(F32)
        )
        moved = (states[0][t].astype(F32) - pseudo_step * residual).astype(BF16)
        if last:
            final_ref[t] = moved
            residual_ref[t] = residual
        else:
            next_ref[t] = moved
            fresh.append(moved)
    if not last:
        pool = trace_pool(jnp.concatenate(fresh, 0), trace_ref[...], insts, elems)
        next_pool_ref[...] = pool
        fill_outgoing(pool, send_ref[0], out_refs, place, elems)


def on_device(
    initial_state, forcing, diagonal_blocks, flux_jacobian, send_list, source_index, frequency
):
    insts, elems, width = initial_state.shape
    parts = lax.axis_size("dom")
    ranks = lax.axis_size("inst")
    slots, capacity = send_list.shape[1:]
    faces = FACES * elems
    trace_np, lift_np, spectral, second = wide_tables()
    trace_wide = jnp.asarray(trace_np, BF16)
    lift_wide = jnp.asarray(lift_np, BF16)
    place = lax.axis_index("dom").reshape(1)
    sources = source_index.T
    routes = swap_routes(ranks, parts)

    smem = pl.BlockSpec(memory_space=pltpu.SMEM)
    vmem = pl.BlockSpec(memory_space=pltpu.VMEM)
    params = pltpu.CompilerParams(vmem_limit_bytes=VMEM_LIMIT)

    def like(array):
        return jax.ShapeDtypeStruct(array.shape, array.dtype)

    wide_shape = jax.ShapeDtypeStruct(initial_state.shape, F32)
    pool_shape = jax.ShapeDtypeStruct((faces, insts * LANE), BF16)
    out_shapes = [jax.ShapeDtypeStruct((capacity, insts * LANE), BF16)] * slots
    flux_shape = jax.ShapeDtypeStruct((faces, FIELDS * LANE), BF16)
    hot_shape = jax.ShapeDtypeStruct((faces, faces + slots * capacity), BF16)

    def exchange(state, outgoing):
        got = [lax.ppermute(outgoing[swap], ("inst", "dom"), routes[swap]) for swap in SWAP_ORDER]
        states = [state]
        for rank in range(1, ranks):
            route = [((i + rank) % ranks, i) for i in range(ranks)]
            states.append(lax.ppermute(state, "inst", route))
        return states, got

    def own_terms(state, diag, force):
        return pl.pallas_call(
            base_kernel,
            out_shape=wide_shape,
            in_specs=[vmem] * 3,
            out_specs=vmem,
            scratch_shapes=[pltpu.VMEM((pl.cdiv(width, LANE) * insts * elems, LANE), F32)] * 2,
            compiler_params=params,
            cost_estimate=pl.CostEstimate(
                flops=2 * insts * diagonal_blocks.size,
                bytes_accessed=2 * diagonal_blocks.size,
                transcendentals=0,
            ),
            name="own_terms",
        )(state, diag, force)

    freq = frequency.reshape(1, 1)
    spread, order = pl.pallas_call(
        table_kernel,
        out_shape=[
            jax.ShapeDtypeStruct((LANE, FIELDS * LANE), BF16),
            jax.ShapeDtypeStruct((FIELDS * FIELDS * FPTS, FIELDS * LANE), BF16),
        ],
        out_specs=[vmem] * 2,
        compiler_params=params,
        cost_estimate=pl.CostEstimate(flops=10**10, bytes_accessed=10**6, transcendentals=0),
        name="tables",
    )()
    flux, hot, pool, *outgoing = pl.pallas_call(
        first_kernel,
        out_shape=[flux_shape, hot_shape, pool_shape] + out_shapes,
        in_specs=[smem] + [vmem] * 6,
        out_specs=[vmem] * (3 + len(out_shapes)),
        compiler_params=params,
        cost_estimate=pl.CostEstimate(flops=10**10, bytes_accessed=10**6, transcendentals=0),
        name="first_traces",
    )(place, order, initial_state, trace_wide, send_list, flux_jacobian, sources)
    state, trace, send = initial_state, trace_wide, send_list
    force, lift, diag = forcing, lift_wide, diagonal_blocks
    states, got = exchange(state, outgoing)
    base = own_terms(state, diag, force)
    state, pool, *outgoing = pl.pallas_call(
        functools.partial(step_kernel, parts, ranks, False, spectral, second),
        out_shape=[like(initial_state), pool_shape] + out_shapes,
        in_specs=[smem] + [vmem] * (ranks + slots + 9),
        out_specs=[vmem] * (2 + len(out_shapes)),
        compiler_params=params,
        name="first_step",
    )(place, freq, spread, *got, *states, pool, base, hot, flux, lift, trace, send)
    states, got = exchange(state, outgoing)
    base = own_terms(state, diag, force)
    return pl.pallas_call(
        functools.partial(step_kernel, parts, ranks, True, spectral, second),
        out_shape=[like(initial_state), wide_shape],
        in_specs=[smem] + [vmem] * (ranks + slots + 7),
        out_specs=[vmem] * 2,
        compiler_params=params,
        name="last_step",
    )(place, freq, spread, *got, *states, pool, base, hot, flux, lift)


def solution(mesh):
    return jax.shard_map(
        on_device,
        mesh=mesh,
        in_specs=(
            P("inst", "dom", None),
            P("inst", "dom", None),
            P("dom", None, None),
            P("dom", None),
            P("dom", None, None),
            P("dom", None),
            P(),
        ),
        out_specs=(P("inst", "dom", None), P("inst", "dom", None)),
        check_vma=False,
    )
```

```python
import functools
import math

import jax
import jax.numpy as jnp
import numpy as np
from jax import lax
from jax.experimental import pallas as pl
from jax.experimental.pallas import tpu as pltpu
from jax.sharding import PartitionSpec as P

FIELDS = 5
ORDER = 3
NODES = 64
FPTS = 16
NI = 8
REACH = 2
ITERS = 2


pseudo_step = 0.5
dissipation = 0.25


def gauss_legendre(count):
    points = []
    weights = []
    for i in range(count):
        where = math.cos(math.pi * (i + 0.75) / (count + 0.5))
        for sweep in range(100):
            before = 1.0
            value = where
            for j in range(2, count + 1):
                after = ((2 * j - 1) * where * value - (j - 1) * before) / j
                before = value
                value = after
            slope = count * (where * value - before) / (where * where - 1.0)
            where = where - value / slope
        before = 1.0
        value = where
        for j in range(2, count + 1):
            after = ((2 * j - 1) * where * value - (j - 1) * before) / j
            before = value
            value = after
        slope = count * (where * value - before) / (where * where - 1.0)
        points.append(where)
        weights.append(2.0 / ((1.0 - where * where) * slope * slope))
    return (np.array(points[::-1]), np.array(weights[::-1]))


def lagrange_at(points, where):
    values = np.ones(points.shape[0])
    for i in range(points.shape[0]):
        for j in range(points.shape[0]):
            if j != i:
                values[i] = values[i] * (where - points[j]) / (points[i] - points[j])
    return values


def tables(order, count):
    points, weights = gauss_legendre(order + 1)
    at_minus = lagrange_at(points, -1.0)
    at_plus = lagrange_at(points, 1.0)
    per_side = order + 1
    node_count = per_side**3
    face_points = per_side**2
    trace_table = np.zeros((node_count, 6 * face_points))
    lift_table = np.zeros((node_count, 6 * face_points))
    for k in range(per_side):
        for j in range(per_side):
            for i in range(per_side):
                node = i + per_side * j + per_side * per_side * k
                entries = [
                    (0, at_minus[i], j + per_side * k, weights[i]),
                    (1, at_plus[i], j + per_side * k, weights[i]),
                    (2, at_minus[j], i + per_side * k, weights[j]),
                    (3, at_plus[j], i + per_side * k, weights[j]),
                    (4, at_minus[k], i + per_side * j, weights[k]),
                    (5, at_plus[k], i + per_side * j, weights[k]),
                ]
                for face_index, factor, point, weight in entries:
                    trace_table[node, face_index * face_points + point] = factor
                    lift_table[node, face_index * face_points + point] = factor / weight
    spectral = np.zeros((count, count))
    second = np.zeros((count, count))
    for t in range(count):
        for s in range(count):
            if t != s:
                spectral[t, s] = 0.5 * (-1.0) ** (t - s + 1) / math.tan(math.pi * (t - s) / count)
                second[t, s] = -0.5 * (-1.0) ** (t - s) / math.sin(math.pi * (t - s) / count) ** 2
            else:
                second[t, s] = -(count * count + 2.0) / 12.0
    return (trace_table, lift_table, spectral, second)


LANE = 128
WIDE = FIELDS * NODES
FACES = 6
VMEM_LIMIT = 16 * 1024 * 1024
BF16 = jnp.bfloat16
F32 = jnp.float32
OFFSETS = list(range(-REACH, 0)) + list(range(1, REACH + 1))
SWAP_ORDER = (3, 1, 2, 0)


def wide_tables():
    trace_np, lift_np, spectral_np, second_np = tables(ORDER, NI)
    trace_wide = np.zeros((WIDE, FACES * LANE))
    lift_wide = np.zeros((FACES * LANE, WIDE))
    for c in range(FIELDS):
        rows = slice(c * NODES, (c + 1) * NODES)
        for f in range(FACES):
            cols = slice(f * LANE + c * FPTS, f * LANE + (c + 1) * FPTS)
            face = slice(f * FPTS, (f + 1) * FPTS)
            trace_wide[rows, cols] = trace_np[:, face]
            lift_wide[cols, rows] = lift_np[:, face].T
    return trace_wide, lift_wide, spectral_np[:, 0], second_np[:, 0]


def iotas(shape):
    return [lax.broadcasted_iota(jnp.int32, shape, axis) for axis in range(2)]


def one_hot(mask):
    return jnp.where(mask, 1.0, 0.0).astype(BF16)


def spread_table():
    row, col = iotas((LANE, FIELDS * LANE))
    inside = col % LANE < FIELDS * FPTS
    return one_hot(inside & (row == col // LANE * FPTS + col % FPTS))


def order_table():
    row, col = iotas((FIELDS * FIELDS * FPTS, FIELDS * LANE))
    place = col % LANE
    source = place // FPTS * FIELDS * FPTS + col // LANE * FPTS + col % FPTS
    return one_hot((place < FIELDS * FPTS) & (row == source))


def trace_pool(state, trace_wide, insts, elems):
    wide = jnp.dot(state, trace_wide, preferred_element_type=F32).astype(BF16)
    by_inst = []
    for t in range(insts):
        rows = wide[t * elems : (t + 1) * elems]
        by_inst.append(
            jnp.concatenate([rows[:, f * LANE : (f + 1) * LANE] for f in range(FACES)], 0)
        )
    return jnp.concatenate(by_inst, 1)


def swap_routes(ranks, parts):
    near = [[(p, p + 1) for p in range(first, parts - 1, 2)] for first in range(2)]
    far = [
        [(p + i, p + i + 2) for p in range(first, parts - 3, 4) for i in range(2)]
        for first in (0, 2)
    ]
    routes = []
    for pairs in near + far:
        met = {p for pair in pairs for p in pair}
        alone = [p for p in range(parts) if p not in met]
        swaps = [(r * parts + p, r * parts + q) for r in range(ranks) for p, q in pairs]
        swaps += [(r * parts + p, (r ^ 1) * parts + p) for r in range(0, ranks, 2) for p in alone]
        routes.append(swaps + [(q, p) for p, q in swaps])
    return routes


def by_swap(place, by_offset):
    two_down, one_down, one_up, two_up = by_offset
    even = place % 2 == 0
    low = place // 2 % 2 == 0
    return [
        jnp.where(even, one_up, one_down),
        jnp.where(even, one_down, one_up),
        jnp.where(low, two_up, two_down),
        jnp.where(low, two_down, two_up),
    ]


def by_offset(place, blocks):
    even = place % 2 == 0
    low = place // 2 % 2 == 0
    return [
        jnp.where(low, blocks[3], blocks[2]),
        jnp.where(even, blocks[1], blocks[0]),
        jnp.where(even, blocks[0], blocks[1]),
        jnp.where(low, blocks[2], blocks[3]),
    ]


def fill_outgoing(pool, send, out_refs, place, elems):
    slots, capacity = send.shape
    rows, cols = iotas((FACES * elems, slots * capacity))
    ids = FACES * (rows % elems) + rows // elems
    wanted = jnp.concatenate([send[k : k + 1] for k in range(slots)], 1)
    out = lax.dot_general(
        one_hot(ids == wanted), pool, (((0,), (0,)), ((), ())), preferred_element_type=F32
    )
    blocks = by_swap(place, [out[k * capacity : (k + 1) * capacity] for k in range(slots)])
    for block, ref in zip(blocks, out_refs):
        ref[...] = block.astype(BF16)


def diagonal(states, diag, wide_ref, prod_ref, insts, elems):
    tall = insts * elems
    width = diag.shape[1]
    cuts = [(j, j * LANE, min((j + 1) * LANE, width)) for j in range(pl.cdiv(width, LANE))]
    for t in range(insts):
        rows = states[t].astype(F32)
        for j, low, high in cuts:
            first = j * tall + t * elems
            wide_ref[first : first + elems, 0 : high - low] = rows[:, low:high]
    for e in range(elems):
        rows = jnp.concatenate(
            [wide_ref[pl.ds(j * tall + e, insts, stride=elems), :] for j, low, high in cuts], 1
        )
        product = jnp.dot(rows[:, 0:width].astype(BF16), diag[e], preferred_element_type=F32)
        for j, low, high in cuts:
            chunk = product[:, low:high]
            if high - low < LANE:
                chunk = jnp.concatenate([chunk, jnp.zeros((insts, LANE - high + low), F32)], 1)
            prod_ref[pl.ds(j * tall + e, insts, stride=elems), :] = chunk
    return [
        jnp.concatenate(
            [
                prod_ref[j * tall + t * elems : j * tall + (t + 1) * elems, 0 : high - low]
                for j, low, high in cuts
            ],
            1,
        )
        for t in range(insts)
    ]


def flux_order(rows, order):
    per_face = FIELDS * FIELDS * FPTS
    by_face = jnp.concatenate(
        [rows[:, f * per_face : (f + 1) * per_face] for f in range(FACES)], 0
    )
    return jnp.dot(by_face, order, preferred_element_type=F32).astype(BF16)


def source_table(sources, elems, slots):
    faces = FACES * elems
    columns = lax.broadcasted_iota(jnp.int32, (elems, faces + slots), 1)
    ids = jnp.where(columns < faces, FACES * (columns % elems) + columns // elems, columns)
    hot = [jnp.where(sources[:, f : f + 1] == ids, 1.0, 0.0) for f in range(FACES)]
    return jnp.concatenate(hot, 0).astype(BF16)


def table_kernel(spread_ref, order_ref):
    spread_ref[...] = spread_table()
    order_ref[...] = order_table()


def first_kernel(spectral, second, place_ref, freq_ref, order_ref, state_ref, trace_ref, send_ref, flux_ref, source_ref,
                 flux_out_ref, hot_ref, entry_ref, pool_ref, *out_refs):
    insts, elems, width = state_ref.shape
    state = state_ref[...].reshape(insts * elems, width)
    pool = trace_pool(state, trace_ref[...], insts, elems)
    pool_ref[...] = pool
    fill_outgoing(pool, send_ref[0], out_refs, place_ref[0], elems)
    hot_ref[...] = source_table(source_ref[...].T, elems, send_ref.shape[1] * send_ref.shape[2])
    flux_out_ref[...] = flux_order(flux_ref[...], order_ref[...])
    freq = freq_ref[0]
    for d in range(NI):
        entry = freq * float(spectral[d]) - dissipation * float(second[d])
        entry_ref[d : d + 1, :] = jnp.full((1, width), entry, F32)


def base_kernel(state_ref, diag_ref, forcing_ref, base_ref, wide_ref, prod_ref):
    insts, elems, width = state_ref.shape
    states = [state_ref[t] for t in range(insts)]
    products = diagonal(states, diag_ref, wide_ref, prod_ref, insts, elems)
    for t in range(insts):
        base_ref[t] = products[t] - forcing_ref[t].astype(F32)


def step_kernel(parts, ranks, last, *refs):
    place_ref, entry_ref, spread_ref = refs[:3]
    got_refs = {swap: refs[3 + i] for i, swap in enumerate(SWAP_ORDER)}
    got_refs = [got_refs[swap] for swap in range(len(OFFSETS))]
    refs = refs[3 + len(OFFSETS) :]
    states = refs[:ranks]
    pool_ref, refs = refs[ranks], refs[ranks + 1 :]
    base_ref, hot_ref, flux_ref, lift_ref = refs[:4]
    if last:
        final_ref, residual_ref = refs[4:]
    else:
        trace_ref, send_ref, next_ref, next_pool_ref = refs[4:8]
        out_refs = refs[8:]
    insts, elems, width = states[0].shape
    place = place_ref[0]
    faces = FACES * elems

    entries = [entry_ref[d : d + 1, :] for d in range(NI)]

    arrived = by_offset(place, [ref[...].astype(F32) for ref in got_refs])
    for k, offset in enumerate(OFFSETS):
        exists = (place + offset >= 0) & (place + offset < parts)
        arrived[k] = jnp.where(exists, arrived[k], jnp.zeros_like(arrived[k]))
    pool = jnp.concatenate([pool_ref[...], jnp.concatenate(arrived, 0).astype(BF16)], 0)
    picked = jnp.dot(hot_ref[...], pool, preferred_element_type=F32).astype(BF16)
    stacked = jnp.concatenate([picked[:, t * LANE : (t + 1) * LANE] for t in range(insts)], 0)
    wide = jnp.dot(stacked, spread_ref[...], preferred_element_type=F32)

    flux = flux_ref[...].astype(F32)
    normal = []
    for t in range(insts):
        rows = wide[t * faces : (t + 1) * faces]
        summed = flux[:, 0:LANE] * rows[:, 0:LANE]
        for d in range(1, FIELDS):
            summed += flux[:, d * LANE : (d + 1) * LANE] * rows[:, d * LANE : (d + 1) * LANE]
        summed = summed.astype(BF16)
        normal.append(
            jnp.concatenate([summed[f * elems : (f + 1) * elems] for f in range(FACES)], 1)
        )
    lifted = jnp.dot(jnp.concatenate(normal, 0), lift_ref[...], preferred_element_type=F32)

    fresh = []
    for t in range(insts):
        summed = jnp.zeros((elems, width), F32)
        for rank in range(ranks):
            for s in range(insts):
                summed += entries[(t - s - rank * insts) % NI] * states[rank][s].astype(F32)
        residual = (
            base_ref[t] + lifted[t * elems : (t + 1) * elems] + summed.astype(BF16).astype(F32)
        )
        moved = (states[0][t].astype(F32) - pseudo_step * residual).astype(BF16)
        if last:
            final_ref[t] = moved
            residual_ref[t] = residual
        else:
            next_ref[t] = moved
            fresh.append(moved)
    if not last:
        pool = trace_pool(jnp.concatenate(fresh, 0), trace_ref[...], insts, elems)
        next_pool_ref[...] = pool
        fill_outgoing(pool, send_ref[0], out_refs, place, elems)


def on_device(
    initial_state, forcing, diagonal_blocks, flux_jacobian, send_list, source_index, frequency
):
    insts, elems, width = initial_state.shape
    parts = lax.axis_size("dom")
    ranks = lax.axis_size("inst")
    slots, capacity = send_list.shape[1:]
    faces = FACES * elems
    trace_np, lift_np, spectral, second = wide_tables()
    trace_wide = jnp.asarray(trace_np, BF16)
    lift_wide = jnp.asarray(lift_np, BF16)
    place = lax.axis_index("dom").reshape(1)
    sources = source_index.T
    routes = swap_routes(ranks, parts)

    smem = pl.BlockSpec(memory_space=pltpu.SMEM)
    vmem = pl.BlockSpec(memory_space=pltpu.VMEM)
    params = pltpu.CompilerParams(vmem_limit_bytes=VMEM_LIMIT)

    def like(array):
        return jax.ShapeDtypeStruct(array.shape, array.dtype)

    wide_shape = jax.ShapeDtypeStruct(initial_state.shape, F32)
    pool_shape = jax.ShapeDtypeStruct((faces, insts * LANE), BF16)
    out_shapes = [jax.ShapeDtypeStruct((capacity, insts * LANE), BF16)] * slots
    flux_shape = jax.ShapeDtypeStruct((faces, FIELDS * LANE), BF16)
    entry_shape = jax.ShapeDtypeStruct((NI, width), F32)
    hot_shape = jax.ShapeDtypeStruct((faces, faces + slots * capacity), BF16)

    def exchange(state, outgoing):
        got = [lax.ppermute(outgoing[swap], ("inst", "dom"), routes[swap]) for swap in SWAP_ORDER]
        states = [state]
        for rank in range(1, ranks):
            route = [((i + rank) % ranks, i) for i in range(ranks)]
            states.append(lax.ppermute(state, "inst", route))
        return states, got

    def own_terms(state, diag, force):
        return pl.pallas_call(
            base_kernel,
            out_shape=wide_shape,
            in_specs=[vmem] * 3,
            out_specs=vmem,
            scratch_shapes=[pltpu.VMEM((pl.cdiv(width, LANE) * insts * elems, LANE), F32)] * 2,
            compiler_params=params,
            cost_estimate=pl.CostEstimate(
                flops=2 * insts * diagonal_blocks.size,
                bytes_accessed=2 * diagonal_blocks.size,
                transcendentals=0,
            ),
            name="own_terms",
        )(state, diag, force)

    spread, order = pl.pallas_call(
        table_kernel,
        out_shape=[
            jax.ShapeDtypeStruct((LANE, FIELDS * LANE), BF16),
            jax.ShapeDtypeStruct((FIELDS * FIELDS * FPTS, FIELDS * LANE), BF16),
        ],
        out_specs=[vmem] * 2,
        compiler_params=params,
        cost_estimate=pl.CostEstimate(flops=10**10, bytes_accessed=10**6, transcendentals=0),
        name="tables",
    )()
    flux, hot, entries, pool, *outgoing = pl.pallas_call(
        functools.partial(first_kernel, spectral, second),
        out_shape=[flux_shape, hot_shape, entry_shape, pool_shape] + out_shapes,
        in_specs=[smem] * 2 + [vmem] * 6,
        out_specs=[vmem] * (4 + len(out_shapes)),
        compiler_params=params,
        cost_estimate=pl.CostEstimate(flops=10**10, bytes_accessed=10**6, transcendentals=0),
        name="first_traces",
    )(place, frequency, order, initial_state, trace_wide, send_list, flux_jacobian, sources)
    state, trace, send = initial_state, trace_wide, send_list
    force, lift, diag = forcing, lift_wide, diagonal_blocks
    states, got = exchange(state, outgoing)
    base = own_terms(state, diag, force)
    state, pool, *outgoing = pl.pallas_call(
        functools.partial(step_kernel, parts, ranks, False),
        out_shape=[like(initial_state), pool_shape] + out_shapes,
        in_specs=[smem] + [vmem] * (ranks + slots + 9),
        out_specs=[vmem] * (2 + len(out_shapes)),
        compiler_params=params,
        name="first_step",
    )(place, entries, spread, *got, *states, pool, base, hot, flux, lift, trace, send)
    states, got = exchange(state, outgoing)
    base = own_terms(state, diag, force)
    return pl.pallas_call(
        functools.partial(step_kernel, parts, ranks, True),
        out_shape=[like(initial_state), wide_shape],
        in_specs=[smem] + [vmem] * (ranks + slots + 7),
        out_specs=[vmem] * 2,
        compiler_params=params,
        name="last_step",
    )(place, entries, spread, *got, *states, pool, base, hot, flux, lift)


def solution(mesh):
    return jax.shard_map(
        on_device,
        mesh=mesh,
        in_specs=(
            P("inst", "dom", None),
            P("inst", "dom", None),
            P("dom", None, None),
            P("dom", None),
            P("dom", None, None),
            P("dom", None),
            P(),
        ),
        out_specs=(P("inst", "dom", None), P("inst", "dom", None)),
        check_vma=False,
    )
```

```python
import functools
import math

import jax
import jax.numpy as jnp
import numpy as np
from jax import lax
from jax.experimental import pallas as pl
from jax.experimental.pallas import tpu as pltpu
from jax.sharding import PartitionSpec as P

FIELDS = 5
ORDER = 3
NODES = 64
FPTS = 16
NI = 8
REACH = 2
ITERS = 2


pseudo_step = 0.5
dissipation = 0.25


def gauss_legendre(count):
    points = []
    weights = []
    for i in range(count):
        where = math.cos(math.pi * (i + 0.75) / (count + 0.5))
        for sweep in range(100):
            before = 1.0
            value = where
            for j in range(2, count + 1):
                after = ((2 * j - 1) * where * value - (j - 1) * before) / j
                before = value
                value = after
            slope = count * (where * value - before) / (where * where - 1.0)
            where = where - value / slope
        before = 1.0
        value = where
        for j in range(2, count + 1):
            after = ((2 * j - 1) * where * value - (j - 1) * before) / j
            before = value
            value = after
        slope = count * (where * value - before) / (where * where - 1.0)
        points.append(where)
        weights.append(2.0 / ((1.0 - where * where) * slope * slope))
    return (np.array(points[::-1]), np.array(weights[::-1]))


def lagrange_at(points, where):
    values = np.ones(points.shape[0])
    for i in range(points.shape[0]):
        for j in range(points.shape[0]):
            if j != i:
                values[i] = values[i] * (where - points[j]) / (points[i] - points[j])
    return values


def tables(order, count):
    points, weights = gauss_legendre(order + 1)
    at_minus = lagrange_at(points, -1.0)
    at_plus = lagrange_at(points, 1.0)
    per_side = order + 1
    node_count = per_side**3
    face_points = per_side**2
    trace_table = np.zeros((node_count, 6 * face_points))
    lift_table = np.zeros((node_count, 6 * face_points))
    for k in range(per_side):
        for j in range(per_side):
            for i in range(per_side):
                node = i + per_side * j + per_side * per_side * k
                entries = [
                    (0, at_minus[i], j + per_side * k, weights[i]),
                    (1, at_plus[i], j + per_side * k, weights[i]),
                    (2, at_minus[j], i + per_side * k, weights[j]),
                    (3, at_plus[j], i + per_side * k, weights[j]),
                    (4, at_minus[k], i + per_side * j, weights[k]),
                    (5, at_plus[k], i + per_side * j, weights[k]),
                ]
                for face_index, factor, point, weight in entries:
                    trace_table[node, face_index * face_points + point] = factor
                    lift_table[node, face_index * face_points + point] = factor / weight
    spectral = np.zeros((count, count))
    second = np.zeros((count, count))
    for t in range(count):
        for s in range(count):
            if t != s:
                spectral[t, s] = 0.5 * (-1.0) ** (t - s + 1) / math.tan(math.pi * (t - s) / count)
                second[t, s] = -0.5 * (-1.0) ** (t - s) / math.sin(math.pi * (t - s) / count) ** 2
            else:
                second[t, s] = -(count * count + 2.0) / 12.0
    return (trace_table, lift_table, spectral, second)


LANE = 128
WIDE = FIELDS * NODES
FACES = 6
VMEM_LIMIT = 16 * 1024 * 1024
BF16 = jnp.bfloat16
F32 = jnp.float32
OFFSETS = list(range(-REACH, 0)) + list(range(1, REACH + 1))
SWAP_ORDER = (3, 1, 2, 0)


def wide_tables():
    trace_np, lift_np, spectral_np, second_np = tables(ORDER, NI)
    trace_wide = np.zeros((WIDE, FACES * LANE))
    lift_wide = np.zeros((FACES * LANE, WIDE))
    for c in range(FIELDS):
        rows = slice(c * NODES, (c + 1) * NODES)
        for f in range(FACES):
            cols = slice(f * LANE + c * FPTS, f * LANE + (c + 1) * FPTS)
            face = slice(f * FPTS, (f + 1) * FPTS)
            trace_wide[rows, cols] = trace_np[:, face]
            lift_wide[cols, rows] = lift_np[:, face].T
    return trace_wide, lift_wide, spectral_np[:, 0], second_np[:, 0]


def iotas(shape):
    return [lax.broadcasted_iota(jnp.int32, shape, axis) for axis in range(2)]


def one_hot(mask):
    return jnp.where(mask, 1.0, 0.0).astype(BF16)


def spread_table():
    row, col = iotas((LANE, FIELDS * LANE))
    inside = col % LANE < FIELDS * FPTS
    return one_hot(inside & (row == col // LANE * FPTS + col % FPTS))


def order_table():
    row, col = iotas((FIELDS * FIELDS * FPTS, FIELDS * LANE))
    place = col % LANE
    source = place // FPTS * FIELDS * FPTS + col // LANE * FPTS + col % FPTS
    return one_hot((place < FIELDS * FPTS) & (row == source))


def trace_pool(state, trace_wide, insts, elems):
    wide = jnp.dot(state, trace_wide, preferred_element_type=F32).astype(BF16)
    by_inst = []
    for t in range(insts):
        rows = wide[t * elems : (t + 1) * elems]
        by_inst.append(
            jnp.concatenate([rows[:, f * LANE : (f + 1) * LANE] for f in range(FACES)], 0)
        )
    return jnp.concatenate(by_inst, 1)


def swap_routes(ranks, parts):
    near = [[(p, p + 1) for p in range(first, parts - 1, 2)] for first in range(2)]
    far = [
        [(p + i, p + i + 2) for p in range(first, parts - 3, 4) for i in range(2)]
        for first in (0, 2)
    ]
    routes = []
    for pairs in near + far:
        met = {p for pair in pairs for p in pair}
        alone = [p for p in range(parts) if p not in met]
        swaps = [(r * parts + p, r * parts + q) for r in range(ranks) for p, q in pairs]
        swaps += [(r * parts + p, (r ^ 1) * parts + p) for r in range(0, ranks, 2) for p in alone]
        routes.append(swaps + [(q, p) for p, q in swaps])
    return routes


def by_swap(place, by_offset):
    two_down, one_down, one_up, two_up = by_offset
    even = place % 2 == 0
    low = place // 2 % 2 == 0
    return [
        jnp.where(even, one_up, one_down),
        jnp.where(even, one_down, one_up),
        jnp.where(low, two_up, two_down),
        jnp.where(low, two_down, two_up),
    ]


def by_offset(place, blocks):
    even = place % 2 == 0
    low = place // 2 % 2 == 0
    return [
        jnp.where(low, blocks[3], blocks[2]),
        jnp.where(even, blocks[1], blocks[0]),
        jnp.where(even, blocks[0], blocks[1]),
        jnp.where(low, blocks[2], blocks[3]),
    ]


def fill_outgoing(pool, send, out_refs, place, elems):
    slots, capacity = send.shape
    rows, cols = iotas((FACES * elems, slots * capacity))
    ids = FACES * (rows % elems) + rows // elems
    wanted = jnp.concatenate([send[k : k + 1] for k in range(slots)], 1)
    out = lax.dot_general(
        one_hot(ids == wanted), pool, (((0,), (0,)), ((), ())), preferred_element_type=F32
    )
    blocks = by_swap(place, [out[k * capacity : (k + 1) * capacity] for k in range(slots)])
    for block, ref in zip(blocks, out_refs):
        ref[...] = block.astype(BF16)


def diagonal(states, diag, wide_ref, prod_ref, insts, elems):
    tall = insts * elems
    width = diag.shape[1]
    cuts = [(j, j * LANE, min((j + 1) * LANE, width)) for j in range(pl.cdiv(width, LANE))]
    for t in range(insts):
        rows = states[t].astype(F32)
        for j, low, high in cuts:
            first = j * tall + t * elems
            wide_ref[first : first + elems, 0 : high - low] = rows[:, low:high]
    for e in range(elems):
        rows = jnp.concatenate(
            [wide_ref[pl.ds(j * tall + e, insts, stride=elems), :] for j, low, high in cuts], 1
        )
        product = jnp.dot(rows[:, 0:width].astype(BF16), diag[e], preferred_element_type=F32)
        for j, low, high in cuts:
            chunk = product[:, low:high]
            if high - low < LANE:
                chunk = jnp.concatenate([chunk, jnp.zeros((insts, LANE - high + low), F32)], 1)
            prod_ref[pl.ds(j * tall + e, insts, stride=elems), :] = chunk
    return [
        jnp.concatenate(
            [
                prod_ref[j * tall + t * elems : j * tall + (t + 1) * elems, 0 : high - low]
                for j, low, high in cuts
            ],
            1,
        )
        for t in range(insts)
    ]


def flux_order(rows, order):
    per_face = FIELDS * FIELDS * FPTS
    by_face = jnp.concatenate(
        [rows[:, f * per_face : (f + 1) * per_face] for f in range(FACES)], 0
    )
    return jnp.dot(by_face, order, preferred_element_type=F32).astype(BF16)


def source_table(sources, elems, slots):
    faces = FACES * elems
    columns = lax.broadcasted_iota(jnp.int32, (elems, faces + slots), 1)
    ids = jnp.where(columns < faces, FACES * (columns % elems) + columns // elems, columns)
    hot = [jnp.where(sources[:, f : f + 1] == ids, 1.0, 0.0) for f in range(FACES)]
    return jnp.concatenate(hot, 0).astype(BF16)


def face_flux(picked, flux, spread, insts):
    count = picked.shape[0]
    stacked = jnp.concatenate([picked[:, t * LANE : (t + 1) * LANE] for t in range(insts)], 0)
    wide = jnp.dot(stacked, spread, preferred_element_type=F32)
    normal = []
    for t in range(insts):
        rows = wide[t * count : (t + 1) * count]
        summed = flux[:, 0:LANE] * rows[:, 0:LANE]
        for d in range(1, FIELDS):
            summed += flux[:, d * LANE : (d + 1) * LANE] * rows[:, d * LANE : (d + 1) * LANE]
        normal.append(summed.astype(BF16))
    return normal


def lift_faces(normal, lift, elems):
    rows = [
        jnp.concatenate([n[f * elems : (f + 1) * elems] for f in range(FACES)], 1) for n in normal
    ]
    return jnp.dot(jnp.concatenate(rows, 0), lift, preferred_element_type=F32)


def coupler_kernel(spectral, second, freq_ref, spread_ref, entry_ref):
    freq = freq_ref[0]
    for d in range(NI):
        entry = freq * float(spectral[d]) - dissipation * float(second[d])
        entry_ref[d : d + 1, :] = jnp.full((1, entry_ref.shape[1]), entry, F32)


def couple(entry_ref, states, t, rank, insts):
    summed = None
    for s in range(insts):
        d = (t - s - rank * insts) % NI
        term = entry_ref[d : d + 1, :] * states[s].astype(F32)
        summed = term if summed is None else summed + term
    return summed


def rotated(flux):
    place = lax.broadcasted_iota(jnp.int32, (flux.shape[0], LANE), 1) // FPTS
    blocks = []
    for k in range(LANE // FPTS):
        block = jnp.zeros((flux.shape[0], LANE), F32)
        for d in range(FIELDS):
            met = place == (d + k) % (LANE // FPTS)
            block = jnp.where(met, flux[:, d * LANE : (d + 1) * LANE], block)
        blocks.append(block)
    return jnp.concatenate(blocks, 1)


def slot_normal(blocks, factors, insts):
    count = blocks.shape[0]
    stacked = jnp.concatenate([blocks[:, t * LANE : (t + 1) * LANE] for t in range(insts)], 0)
    summed = [None] * insts
    for k in range(LANE // FPTS):
        turned = stacked if k == 0 else pltpu.roll(stacked, k * FPTS, 1)
        for t in range(insts):
            term = factors[:, k * LANE : (k + 1) * LANE] * turned[t * count : (t + 1) * count]
            summed[t] = term if k == 0 else summed[t] + term
    return [rows.astype(BF16) for rows in summed]


def table_kernel(spread_ref, order_ref):
    spread_ref[...] = spread_table()
    order_ref[...] = order_table()


def first_kernel(place_ref, order_ref, state_ref, trace_ref, send_ref, flux_ref, source_ref,
                 flux_out_ref, hot_ref, pool_ref, *out_refs):
    insts, elems, width = state_ref.shape
    state = state_ref[...].reshape(insts * elems, width)
    pool = trace_pool(state, trace_ref[...], insts, elems)
    pool_ref[...] = pool
    fill_outgoing(pool, send_ref[0], out_refs, place_ref[0], elems)
    slots = send_ref.shape[1] * send_ref.shape[2]
    hot_ref[...] = source_table(source_ref[...].T, elems, slots)
    flux_out_ref[...] = flux_order(flux_ref[...], order_ref[...])


def base_kernel(state_ref, diag_ref, forcing_ref, base_ref, wide_ref, prod_ref):
    insts, elems, width = state_ref.shape
    states = [state_ref[t] for t in range(insts)]
    products = diagonal(states, diag_ref, wide_ref, prod_ref, insts, elems)
    for t in range(insts):
        base_ref[t] = products[t] - forcing_ref[t].astype(F32)


def last_base_kernel(state_ref, diag_ref, forcing_ref, pool_ref, hot_ref, flux_ref, spread_ref,
                     lift_ref, entry_ref, base_ref, part_ref, factor_ref, wide_ref, prod_ref):
    insts, elems, width = state_ref.shape
    flux = flux_ref[...]
    hot = hot_ref[...]
    faces = pool_ref.shape[0]
    factors = lax.dot_general(hot, flux, (((0,), (0,)), ((), ())), preferred_element_type=F32)
    factor_ref[...] = rotated(factors[faces:])
    empty = jnp.zeros((hot.shape[1] - faces, pool_ref.shape[1]), BF16)
    pool = jnp.concatenate([pool_ref[...], empty], 0)
    picked = jnp.dot(hot, pool, preferred_element_type=F32).astype(BF16)
    normal = face_flux(picked, flux.astype(F32), spread_ref[...], insts)
    lifted = lift_faces(normal, lift_ref[...], elems)
    states = [state_ref[t] for t in range(insts)]
    products = diagonal(states, diag_ref, wide_ref, prod_ref, insts, elems)
    for t in range(insts):
        base_ref[t] = (
            products[t] + lifted[t * elems : (t + 1) * elems] - forcing_ref[t].astype(F32)
        )
        part_ref[t] = couple(entry_ref, states, t, 0, insts)


def received(parts, place, got_refs):
    got_refs = {swap: got_refs[i] for i, swap in enumerate(SWAP_ORDER)}
    arrived = by_offset(
        place, [got_refs[swap][...].astype(F32) for swap in range(len(OFFSETS))]
    )
    for k, offset in enumerate(OFFSETS):
        exists = (place + offset >= 0) & (place + offset < parts)
        arrived[k] = jnp.where(exists, arrived[k], jnp.zeros_like(arrived[k]))
    return jnp.concatenate(arrived, 0)


def step_kernel(parts, ranks, *refs):
    place_ref, entry_ref, spread_ref = refs[:3]
    got_refs, refs = refs[3 : 3 + len(OFFSETS)], refs[3 + len(OFFSETS) :]
    states, refs = refs[:ranks], refs[ranks:]
    (pool_ref, base_ref, hot_ref, flux_ref, lift_ref, trace_ref, send_ref,
     next_ref, next_pool_ref) = refs[:9]
    out_refs = refs[9:]
    insts, elems, width = states[0].shape
    place = place_ref[0]
    blocks = received(parts, place, got_refs).astype(BF16)
    pool = jnp.concatenate([pool_ref[...], blocks], 0)
    picked = jnp.dot(hot_ref[...], pool, preferred_element_type=F32).astype(BF16)
    normal = face_flux(picked, flux_ref[...].astype(F32), spread_ref[...], insts)
    lifted = lift_faces(normal, lift_ref[...], elems)
    fresh = []
    for t in range(insts):
        summed = couple(entry_ref, states[0], t, 0, insts)
        for rank in range(1, ranks):
            summed += couple(entry_ref, states[rank], t, rank, insts)
        residual = (
            base_ref[t] + lifted[t * elems : (t + 1) * elems] + summed.astype(BF16).astype(F32)
        )
        moved = (states[0][t].astype(F32) - pseudo_step * residual).astype(BF16)
        next_ref[t] = moved
        fresh.append(moved)
    pool = trace_pool(jnp.concatenate(fresh, 0), trace_ref[...], insts, elems)
    next_pool_ref[...] = pool
    fill_outgoing(pool, send_ref[0], out_refs, place, elems)


def last_kernel(parts, ranks, *refs):
    place_ref, entry_ref = refs[:2]
    got_refs, refs = refs[2 : 2 + len(OFFSETS)], refs[2 + len(OFFSETS) :]
    states, refs = refs[:ranks], refs[ranks:]
    (base_ref, part_ref, hot_ref, factor_ref, lift_ref, final_hbm, residual_hbm,
     final_ref, residual_ref, sems) = refs
    insts, elems, width = states[0].shape
    blocks = received(parts, place_ref[0], got_refs)
    normal = slot_normal(blocks, factor_ref[...], insts)
    empty = jnp.zeros((FACES * elems, insts * LANE), BF16)
    rows = jnp.concatenate([empty, jnp.concatenate(normal, 1)], 0)
    spots = jnp.dot(hot_ref[...], rows, preferred_element_type=F32).astype(BF16)
    lifted = lift_faces(
        [spots[:, t * LANE : (t + 1) * LANE] for t in range(insts)], lift_ref[...], elems
    )
    copies = []
    for t in range(insts):
        summed = part_ref[t]
        for rank in range(1, ranks):
            summed += couple(entry_ref, states[rank], t, rank, insts)
        residual = (
            base_ref[t] + lifted[t * elems : (t + 1) * elems] + summed.astype(BF16).astype(F32)
        )
        residual_ref[t] = residual
        final_ref[t] = (states[0][t].astype(F32) - pseudo_step * residual).astype(BF16)
        copies += [
            pltpu.make_async_copy(residual_ref.at[t], residual_hbm.at[t], sems.at[0, t]),
            pltpu.make_async_copy(final_ref.at[t], final_hbm.at[t], sems.at[1, t]),
        ]
        copies[-2].start()
        copies[-1].start()
    for copy in copies:
        copy.wait()


def on_device(
    initial_state, forcing, diagonal_blocks, flux_jacobian, send_list, source_index, frequency
):
    insts, elems, width = initial_state.shape
    parts = lax.axis_size("dom")
    ranks = lax.axis_size("inst")
    slots, capacity = send_list.shape[1:]
    faces = FACES * elems
    trace_np, lift_np, spectral, second = wide_tables()
    trace_wide = jnp.asarray(trace_np, BF16)
    lift_wide = jnp.asarray(lift_np, BF16)
    place = lax.axis_index("dom").reshape(1)
    sources = source_index.T
    routes = swap_routes(ranks, parts)

    smem = pl.BlockSpec(memory_space=pltpu.SMEM)
    vmem = pl.BlockSpec(memory_space=pltpu.VMEM)
    params = pltpu.CompilerParams(vmem_limit_bytes=VMEM_LIMIT)

    def like(array):
        return jax.ShapeDtypeStruct(array.shape, array.dtype)

    wide_shape = jax.ShapeDtypeStruct(initial_state.shape, F32)
    pool_shape = jax.ShapeDtypeStruct((faces, insts * LANE), BF16)
    out_shapes = [jax.ShapeDtypeStruct((capacity, insts * LANE), BF16)] * slots
    flux_shape = jax.ShapeDtypeStruct((faces, FIELDS * LANE), BF16)
    hot_shape = jax.ShapeDtypeStruct((faces, faces + slots * capacity), BF16)
    factor_shape = jax.ShapeDtypeStruct((slots * capacity, LANE // FPTS * LANE), F32)

    def exchange(state, outgoing):
        got = [lax.ppermute(outgoing[swap], ("inst", "dom"), routes[swap]) for swap in SWAP_ORDER]
        states = [state]
        for rank in range(1, ranks):
            route = [((i + rank) % ranks, i) for i in range(ranks)]
            states.append(lax.ppermute(state, "inst", route))
        return states, got

    chunks = [pltpu.VMEM((pl.cdiv(width, LANE) * insts * elems, LANE), F32)] * 2
    diag_cost = pl.CostEstimate(
        flops=2 * insts * diagonal_blocks.size, bytes_accessed=2 * diagonal_blocks.size,
        transcendentals=0,
    )
    spread, order = pl.pallas_call(
        table_kernel,
        out_shape=[
            jax.ShapeDtypeStruct((LANE, FIELDS * LANE), BF16),
            jax.ShapeDtypeStruct((FIELDS * FIELDS * FPTS, FIELDS * LANE), BF16),
        ],
        out_specs=[vmem] * 2,
        compiler_params=params,
        cost_estimate=pl.CostEstimate(flops=10**10, bytes_accessed=10**6, transcendentals=0),
        name="tables",
    )()
    freq, _ = lax.optimization_barrier((frequency, spread))
    entries = pl.pallas_call(
        functools.partial(coupler_kernel, spectral, second),
        out_shape=jax.ShapeDtypeStruct((NI, width), F32),
        in_specs=[smem, vmem],
        out_specs=vmem,
        compiler_params=params,
        name="couplers",
    )(freq, spread)
    flux, hot, pool, *outgoing = pl.pallas_call(
        first_kernel,
        out_shape=[flux_shape, hot_shape, pool_shape] + out_shapes,
        in_specs=[smem] + [vmem] * 6,
        out_specs=[vmem] * (3 + len(out_shapes)),
        compiler_params=params,
        cost_estimate=pl.CostEstimate(flops=10**10, bytes_accessed=10**6, transcendentals=0),
        name="first_traces",
    )(place, order, initial_state, trace_wide, send_list, flux_jacobian, sources)
    state, _ = lax.optimization_barrier((initial_state, entries))
    states, got = exchange(state, outgoing)
    base = pl.pallas_call(
        base_kernel,
        out_shape=wide_shape,
        in_specs=[vmem] * 3,
        out_specs=vmem,
        scratch_shapes=chunks,
        compiler_params=params,
        cost_estimate=diag_cost,
        name="own_terms",
    )(state, diagonal_blocks, forcing)
    state, pool, *outgoing = pl.pallas_call(
        functools.partial(step_kernel, parts, ranks),
        out_shape=[like(initial_state), pool_shape] + out_shapes,
        in_specs=[smem] + [vmem] * (ranks + slots + 9),
        out_specs=[vmem] * (2 + len(out_shapes)),
        compiler_params=params,
        name="first_step",
    )(place, entries, spread, *got, *states, pool, base, hot, flux, lift_wide, trace_wide,
      send_list)
    states, got = exchange(state, outgoing)
    base, part, factors = pl.pallas_call(
        last_base_kernel,
        out_shape=[wide_shape] * 2 + [factor_shape],
        in_specs=[vmem] * 9,
        out_specs=[vmem] * 3,
        scratch_shapes=chunks,
        compiler_params=params,
        cost_estimate=diag_cost,
        name="last_own_terms",
    )(state, diagonal_blocks, forcing, pool, hot, flux, spread, lift_wide, entries)
    return pl.pallas_call(
        functools.partial(last_kernel, parts, ranks),
        out_shape=[like(initial_state), wide_shape],
        in_specs=[smem] + [vmem] * (ranks + slots + 6),
        out_specs=[pl.BlockSpec(memory_space=pl.ANY)] * 2,
        scratch_shapes=[
            pltpu.VMEM(initial_state.shape, BF16),
            pltpu.VMEM(initial_state.shape, F32),
            pltpu.SemaphoreType.DMA((2, insts)),
        ],
        compiler_params=params,
        name="last_step",
    )(place, entries, *got, *states, base, part, hot, factors, lift_wide)


def solution(mesh):
    return jax.shard_map(
        on_device,
        mesh=mesh,
        in_specs=(
            P("inst", "dom", None),
            P("inst", "dom", None),
            P("dom", None, None),
            P("dom", None),
            P("dom", None, None),
            P("dom", None),
            P(),
        ),
        out_specs=(P("inst", "dom", None), P("inst", "dom", None)),
        check_vma=False,
    )
```

```python
import functools
import math

import jax
import jax.numpy as jnp
import numpy as np
from jax import lax
from jax.experimental import pallas as pl
from jax.experimental.pallas import tpu as pltpu
from jax.sharding import PartitionSpec as P

FIELDS = 5
ORDER = 3
NODES = 64
FPTS = 16
NI = 8
REACH = 2
ITERS = 2


pseudo_step = 0.5
dissipation = 0.25


def gauss_legendre(count):
    points = []
    weights = []
    for i in range(count):
        where = math.cos(math.pi * (i + 0.75) / (count + 0.5))
        for sweep in range(100):
            before = 1.0
            value = where
            for j in range(2, count + 1):
                after = ((2 * j - 1) * where * value - (j - 1) * before) / j
                before = value
                value = after
            slope = count * (where * value - before) / (where * where - 1.0)
            where = where - value / slope
        before = 1.0
        value = where
        for j in range(2, count + 1):
            after = ((2 * j - 1) * where * value - (j - 1) * before) / j
            before = value
            value = after
        slope = count * (where * value - before) / (where * where - 1.0)
        points.append(where)
        weights.append(2.0 / ((1.0 - where * where) * slope * slope))
    return (np.array(points[::-1]), np.array(weights[::-1]))


def lagrange_at(points, where):
    values = np.ones(points.shape[0])
    for i in range(points.shape[0]):
        for j in range(points.shape[0]):
            if j != i:
                values[i] = values[i] * (where - points[j]) / (points[i] - points[j])
    return values


def tables(order, count):
    points, weights = gauss_legendre(order + 1)
    at_minus = lagrange_at(points, -1.0)
    at_plus = lagrange_at(points, 1.0)
    per_side = order + 1
    node_count = per_side**3
    face_points = per_side**2
    trace_table = np.zeros((node_count, 6 * face_points))
    lift_table = np.zeros((node_count, 6 * face_points))
    for k in range(per_side):
        for j in range(per_side):
            for i in range(per_side):
                node = i + per_side * j + per_side * per_side * k
                entries = [
                    (0, at_minus[i], j + per_side * k, weights[i]),
                    (1, at_plus[i], j + per_side * k, weights[i]),
                    (2, at_minus[j], i + per_side * k, weights[j]),
                    (3, at_plus[j], i + per_side * k, weights[j]),
                    (4, at_minus[k], i + per_side * j, weights[k]),
                    (5, at_plus[k], i + per_side * j, weights[k]),
                ]
                for face_index, factor, point, weight in entries:
                    trace_table[node, face_index * face_points + point] = factor
                    lift_table[node, face_index * face_points + point] = factor / weight
    spectral = np.zeros((count, count))
    second = np.zeros((count, count))
    for t in range(count):
        for s in range(count):
            if t != s:
                spectral[t, s] = 0.5 * (-1.0) ** (t - s + 1) / math.tan(math.pi * (t - s) / count)
                second[t, s] = -0.5 * (-1.0) ** (t - s) / math.sin(math.pi * (t - s) / count) ** 2
            else:
                second[t, s] = -(count * count + 2.0) / 12.0
    return (trace_table, lift_table, spectral, second)


LANE = 128
WIDE = FIELDS * NODES
FACES = 6
VMEM_LIMIT = 16 * 1024 * 1024
BF16 = jnp.bfloat16
F32 = jnp.float32
OFFSETS = list(range(-REACH, 0)) + list(range(1, REACH + 1))
SWAP_ORDER = (3, 1, 2, 0)


def wide_tables():
    trace_np, lift_np, spectral_np, second_np = tables(ORDER, NI)
    trace_wide = np.zeros((WIDE, FACES * LANE))
    lift_wide = np.zeros((FACES * LANE, WIDE))
    for c in range(FIELDS):
        rows = slice(c * NODES, (c + 1) * NODES)
        for f in range(FACES):
            cols = slice(f * LANE + c * FPTS, f * LANE + (c + 1) * FPTS)
            face = slice(f * FPTS, (f + 1) * FPTS)
            trace_wide[rows, cols] = trace_np[:, face]
            lift_wide[cols, rows] = lift_np[:, face].T
    return trace_wide, lift_wide, spectral_np[:, 0], second_np[:, 0]


def iotas(shape):
    return [lax.broadcasted_iota(jnp.int32, shape, axis) for axis in range(2)]


def one_hot(mask):
    return jnp.where(mask, 1.0, 0.0).astype(BF16)


def spread_table():
    row, col = iotas((LANE, FIELDS * LANE))
    inside = col % LANE < FIELDS * FPTS
    return one_hot(inside & (row == col // LANE * FPTS + col % FPTS))


def order_table():
    row, col = iotas((FIELDS * FIELDS * FPTS, FIELDS * LANE))
    place = col % LANE
    source = place // FPTS * FIELDS * FPTS + col // LANE * FPTS + col % FPTS
    return one_hot((place < FIELDS * FPTS) & (row == source))


def trace_pool(state, trace_wide, insts, elems):
    wide = jnp.dot(state, trace_wide, preferred_element_type=F32).astype(BF16)
    by_inst = []
    for t in range(insts):
        rows = wide[t * elems : (t + 1) * elems]
        by_inst.append(
            jnp.concatenate([rows[:, f * LANE : (f + 1) * LANE] for f in range(FACES)], 0)
        )
    return jnp.concatenate(by_inst, 1)


def swap_routes(ranks, parts):
    near = [[(p, p + 1) for p in range(first, parts - 1, 2)] for first in range(2)]
    far = [
        [(p + i, p + i + 2) for p in range(first, parts - 3, 4) for i in range(2)]
        for first in (0, 2)
    ]
    routes = []
    for pairs in near + far:
        met = {p for pair in pairs for p in pair}
        alone = [p for p in range(parts) if p not in met]
        swaps = [(r * parts + p, r * parts + q) for r in range(ranks) for p, q in pairs]
        swaps += [(r * parts + p, (r ^ 1) * parts + p) for r in range(0, ranks, 2) for p in alone]
        routes.append(swaps + [(q, p) for p, q in swaps])
    return routes


def by_swap(place, by_offset):
    two_down, one_down, one_up, two_up = by_offset
    even = place % 2 == 0
    low = place // 2 % 2 == 0
    return [
        jnp.where(even, one_up, one_down),
        jnp.where(even, one_down, one_up),
        jnp.where(low, two_up, two_down),
        jnp.where(low, two_down, two_up),
    ]


def by_offset(place, blocks):
    even = place % 2 == 0
    low = place // 2 % 2 == 0
    return [
        jnp.where(low, blocks[3], blocks[2]),
        jnp.where(even, blocks[1], blocks[0]),
        jnp.where(even, blocks[0], blocks[1]),
        jnp.where(low, blocks[2], blocks[3]),
    ]


def fill_outgoing(pool, send, out_refs, place, elems):
    slots, capacity = send.shape
    rows, cols = iotas((FACES * elems, slots * capacity))
    ids = FACES * (rows % elems) + rows // elems
    wanted = jnp.concatenate([send[k : k + 1] for k in range(slots)], 1)
    out = lax.dot_general(
        one_hot(ids == wanted), pool, (((0,), (0,)), ((), ())), preferred_element_type=F32
    )
    blocks = by_swap(place, [out[k * capacity : (k + 1) * capacity] for k in range(slots)])
    for block, ref in zip(blocks, out_refs):
        ref[...] = block.astype(BF16)


def diagonal(states, diag, wide_ref, prod_ref, insts, elems):
    tall = insts * elems
    width = diag.shape[1]
    cuts = [(j, j * LANE, min((j + 1) * LANE, width)) for j in range(pl.cdiv(width, LANE))]
    for t in range(insts):
        rows = states[t].astype(F32)
        for j, low, high in cuts:
            first = j * tall + t * elems
            wide_ref[first : first + elems, 0 : high - low] = rows[:, low:high]
    for e in range(elems):
        rows = jnp.concatenate(
            [wide_ref[pl.ds(j * tall + e, insts, stride=elems), :] for j, low, high in cuts], 1
        )
        product = jnp.dot(rows[:, 0:width].astype(BF16), diag[e], preferred_element_type=F32)
        for j, low, high in cuts:
            chunk = product[:, low:high]
            if high - low < LANE:
                chunk = jnp.concatenate([chunk, jnp.zeros((insts, LANE - high + low), F32)], 1)
            prod_ref[pl.ds(j * tall + e, insts, stride=elems), :] = chunk
    return [
        jnp.concatenate(
            [
                prod_ref[j * tall + t * elems : j * tall + (t + 1) * elems, 0 : high - low]
                for j, low, high in cuts
            ],
            1,
        )
        for t in range(insts)
    ]


def flux_order(rows, order):
    per_face = FIELDS * FIELDS * FPTS
    by_face = jnp.concatenate(
        [rows[:, f * per_face : (f + 1) * per_face] for f in range(FACES)], 0
    )
    return jnp.dot(by_face, order, preferred_element_type=F32).astype(BF16)


def source_table(sources, elems, slots):
    faces = FACES * elems
    columns = lax.broadcasted_iota(jnp.int32, (elems, faces + slots), 1)
    ids = jnp.where(columns < faces, FACES * (columns % elems) + columns // elems, columns)
    hot = [jnp.where(sources[:, f : f + 1] == ids, 1.0, 0.0) for f in range(FACES)]
    return jnp.concatenate(hot, 0).astype(BF16)


def face_flux(picked, flux, spread, insts):
    count = picked.shape[0]
    stacked = jnp.concatenate([picked[:, t * LANE : (t + 1) * LANE] for t in range(insts)], 0)
    wide = jnp.dot(stacked, spread, preferred_element_type=F32)
    normal = []
    for t in range(insts):
        rows = wide[t * count : (t + 1) * count]
        summed = flux[:, 0:LANE] * rows[:, 0:LANE]
        for d in range(1, FIELDS):
            summed += flux[:, d * LANE : (d + 1) * LANE] * rows[:, d * LANE : (d + 1) * LANE]
        normal.append(summed.astype(BF16))
    return normal


def lift_faces(normal, lift, elems):
    rows = [
        jnp.concatenate([n[f * elems : (f + 1) * elems] for f in range(FACES)], 1) for n in normal
    ]
    return jnp.dot(jnp.concatenate(rows, 0), lift, preferred_element_type=F32)


def couple(entry_ref, states, t, shift, insts):
    summed = None
    for s in range(insts):
        d = (t - s + shift * insts) % NI
        term = entry_ref[d : d + 1, :] * states[s].astype(F32)
        summed = term if summed is None else summed + term
    return summed


def rotated(flux):
    place = lax.broadcasted_iota(jnp.int32, (flux.shape[0], LANE), 1) // FPTS
    blocks = []
    for k in range(LANE // FPTS):
        block = jnp.zeros((flux.shape[0], LANE), F32)
        for d in range(FIELDS):
            met = place == (d + k) % (LANE // FPTS)
            block = jnp.where(met, flux[:, d * LANE : (d + 1) * LANE], block)
        blocks.append(block)
    return jnp.concatenate(blocks, 1)


def slot_normal(blocks, factors, insts):
    count = blocks.shape[0]
    stacked = jnp.concatenate([blocks[:, t * LANE : (t + 1) * LANE] for t in range(insts)], 0)
    summed = [None] * insts
    for k in range(LANE // FPTS):
        turned = stacked if k == 0 else pltpu.roll(stacked, k * FPTS, 1)
        for t in range(insts):
            term = factors[:, k * LANE : (k + 1) * LANE] * turned[t * count : (t + 1) * count]
            summed[t] = term if k == 0 else summed[t] + term
    return [rows.astype(BF16) for rows in summed]


def table_kernel(spread_ref, order_ref):
    spread_ref[...] = spread_table()
    order_ref[...] = order_table()


def first_kernel(spectral, second, place_ref, freq_ref, order_ref, state_ref, trace_ref, send_ref, flux_ref, source_ref,
                 flux_out_ref, hot_ref, entry_ref, pool_ref, *out_refs):
    insts, elems, width = state_ref.shape
    state = state_ref[...].reshape(insts * elems, width)
    pool = trace_pool(state, trace_ref[...], insts, elems)
    pool_ref[...] = pool
    fill_outgoing(pool, send_ref[0], out_refs, place_ref[0], elems)
    slots = send_ref.shape[1] * send_ref.shape[2]
    hot_ref[...] = source_table(source_ref[...].T, elems, slots)
    flux_out_ref[...] = flux_order(flux_ref[...], order_ref[...])
    freq = freq_ref[0]
    for d in range(NI):
        entry = freq * float(spectral[d]) - dissipation * float(second[d])
        entry_ref[d : d + 1, :] = jnp.full((1, width), entry, F32)


def base_kernel(state_ref, diag_ref, forcing_ref, entry_ref, base_ref, wide_ref, prod_ref):
    insts, elems, width = state_ref.shape
    states = [state_ref[t] for t in range(insts)]
    products = diagonal(states, diag_ref, wide_ref, prod_ref, insts, elems)
    for t in range(insts):
        own = couple(entry_ref, states, t, 0, insts)
        base_ref[t] = products[t] + own - forcing_ref[t].astype(F32)


def message_rows(insts, elems, slots):
    per_row = pl.cdiv(WIDE, LANE)
    tall = insts * elems
    return tall, 2 * tall, 2 * tall + pl.cdiv(insts, per_row) * slots


def fill_message(message_ref, states, partial, blocks, insts, elems):
    slots = blocks.shape[0]
    per_row = pl.cdiv(WIDE, LANE)
    first, second, last = message_rows(insts, elems, slots)
    message_ref[...] = jnp.zeros_like(message_ref)
    for t in range(insts):
        message_ref[t * elems : (t + 1) * elems, 0:WIDE] = states[t]
        message_ref[first + t * elems : first + (t + 1) * elems, 0:WIDE] = partial[t]
        low, at = second + t // per_row * slots, t % per_row * LANE
        message_ref[low : low + slots, at : at + LANE] = blocks[:, t * LANE : (t + 1) * LANE]


def from_message(message_ref, insts, elems, slots):
    per_row = pl.cdiv(WIDE, LANE)
    first, second, last = message_rows(insts, elems, slots)
    states = [message_ref[t * elems : (t + 1) * elems, 0:WIDE] for t in range(insts)]
    partial = [
        message_ref[first + t * elems : first + (t + 1) * elems, 0:WIDE] for t in range(insts)
    ]
    blocks = []
    for t in range(insts):
        low, at = second + t // per_row * slots, t % per_row * LANE
        blocks.append(message_ref[low : low + slots, at : at + LANE])
    return states, partial, blocks


def last_base_kernel(ranks, partial_ref, first_ref, *refs):
    messages, refs = refs[: ranks - 1], refs[ranks - 1 :]
    (diag_ref, forcing_ref, trace_ref, hot_ref, flux_ref, spread_ref, lift_ref, entry_ref,
     state_ref, base_ref, factor_ref, mend_ref, wide_ref, prod_ref) = refs
    insts, elems, width = first_ref.shape
    flux = flux_ref[...]
    hot = hot_ref[...]
    faces = hot.shape[0]
    slots = hot.shape[1] - faces

    firsts = [[first_ref[t] for t in range(insts)]]
    partials = [[partial_ref[t] for t in range(insts)]]
    traces = [None]
    for message_ref in messages:
        states, partial, blocks = from_message(message_ref, insts, elems, slots)
        firsts.append(states)
        partials.append(partial)
        traces.append(blocks)
    states = []
    for k in range(ranks):
        of_rank = []
        for t in range(insts):
            state = partials[k][t].astype(F32)
            for j in range(ranks):
                if j != k:
                    state -= pseudo_step * couple(entry_ref, firsts[j], t, k - j, insts)
            of_rank.append(state.astype(BF16))
        states.append(of_rank)
    for t in range(insts):
        state_ref[t] = states[0][t]
    for t in range(insts):
        mend = jnp.zeros((slots, LANE), F32)
        for k in range(1, ranks):
            for s in range(insts):
                d = (t - s - k * insts) % NI
                mend -= pseudo_step * entry_ref[d : d + 1, 0:LANE] * traces[k][s].astype(F32)
        mend_ref[:, t * LANE : (t + 1) * LANE] = mend

    pool = trace_pool(jnp.concatenate(states[0], 0), trace_ref[...], insts, elems)
    factors = lax.dot_general(hot, flux, (((0,), (0,)), ((), ())), preferred_element_type=F32)
    factor_ref[...] = rotated(factors[faces:])
    empty = jnp.zeros((slots, insts * LANE), BF16)
    pool = jnp.concatenate([pool, empty], 0)
    picked = jnp.dot(hot, pool, preferred_element_type=F32).astype(BF16)
    normal = face_flux(picked, flux.astype(F32), spread_ref[...], insts)
    lifted = lift_faces(normal, lift_ref[...], elems)
    products = diagonal(states[0], diag_ref, wide_ref, prod_ref, insts, elems)
    for t in range(insts):
        coupling = couple(entry_ref, states[0], t, 0, insts)
        for k in range(1, ranks):
            coupling += couple(entry_ref, states[k], t, -k, insts)
        base_ref[t] = (
            products[t]
            + lifted[t * elems : (t + 1) * elems]
            + coupling.astype(BF16).astype(F32)
            - forcing_ref[t].astype(F32)
        )


def received(parts, place, got_refs):
    got_refs = {swap: got_refs[i] for i, swap in enumerate(SWAP_ORDER)}
    arrived = by_offset(
        place, [got_refs[swap][...].astype(F32) for swap in range(len(OFFSETS))]
    )
    for k, offset in enumerate(OFFSETS):
        exists = (place + offset >= 0) & (place + offset < parts)
        arrived[k] = jnp.where(exists, arrived[k], jnp.zeros_like(arrived[k]))
    return jnp.concatenate(arrived, 0)


def step_kernel(parts, place_ref, spread_ref, *refs):
    got_refs, refs = refs[: len(OFFSETS)], refs[len(OFFSETS) :]
    (state_ref, pool_ref, base_ref, hot_ref, flux_ref, lift_ref, trace_ref, send_ref,
     partial_ref, message_ref, *out_refs) = refs
    insts, elems, width = state_ref.shape
    place = place_ref[0]
    blocks = received(parts, place, got_refs).astype(BF16)
    pool = jnp.concatenate([pool_ref[...], blocks], 0)
    picked = jnp.dot(hot_ref[...], pool, preferred_element_type=F32).astype(BF16)
    normal = face_flux(picked, flux_ref[...].astype(F32), spread_ref[...], insts)
    lifted = lift_faces(normal, lift_ref[...], elems)
    fresh = []
    for t in range(insts):
        residual = base_ref[t] + lifted[t * elems : (t + 1) * elems]
        moved = state_ref[t].astype(F32) - pseudo_step * residual
        partial_ref[t] = moved
        fresh.append(moved.astype(BF16))
    fill_message(message_ref, [state_ref[t] for t in range(insts)], fresh, blocks, insts, elems)
    pool = trace_pool(jnp.concatenate(fresh, 0), trace_ref[...], insts, elems)
    fill_outgoing(pool, send_ref[0], out_refs, place, elems)


def last_kernel(parts, place_ref, *refs):
    got_refs, refs = refs[: len(OFFSETS)], refs[len(OFFSETS) :]
    (state_ref, base_ref, hot_ref, factor_ref, mend_ref, lift_ref, final_hbm, residual_hbm,
     final_ref, residual_ref, sems) = refs
    insts, elems, width = state_ref.shape
    blocks = received(parts, place_ref[0], got_refs) + mend_ref[...]
    normal = slot_normal(blocks, factor_ref[...], insts)
    empty = jnp.zeros((FACES * elems, insts * LANE), BF16)
    rows = jnp.concatenate([empty, jnp.concatenate(normal, 1)], 0)
    spots = jnp.dot(hot_ref[...], rows, preferred_element_type=F32).astype(BF16)
    lifted = lift_faces(
        [spots[:, t * LANE : (t + 1) * LANE] for t in range(insts)], lift_ref[...], elems
    )
    copies = []
    for t in range(insts):
        residual = base_ref[t] + lifted[t * elems : (t + 1) * elems]
        residual_ref[t] = residual
        final_ref[t] = (state_ref[t].astype(F32) - pseudo_step * residual).astype(BF16)
        copies += [
            pltpu.make_async_copy(residual_ref.at[t], residual_hbm.at[t], sems.at[0, t]),
            pltpu.make_async_copy(final_ref.at[t], final_hbm.at[t], sems.at[1, t]),
        ]
        copies[-2].start()
        copies[-1].start()
    for copy in copies:
        copy.wait()


def on_device(
    initial_state, forcing, diagonal_blocks, flux_jacobian, send_list, source_index, frequency
):
    insts, elems, width = initial_state.shape
    parts = lax.axis_size("dom")
    ranks = lax.axis_size("inst")
    slots, capacity = send_list.shape[1:]
    faces = FACES * elems
    trace_np, lift_np, spectral, second = wide_tables()
    trace_wide = jnp.asarray(trace_np, BF16)
    lift_wide = jnp.asarray(lift_np, BF16)
    place = lax.axis_index("dom").reshape(1)
    sources = source_index.T
    routes = swap_routes(ranks, parts)

    smem = pl.BlockSpec(memory_space=pltpu.SMEM)
    vmem = pl.BlockSpec(memory_space=pltpu.VMEM)
    params = pltpu.CompilerParams(vmem_limit_bytes=VMEM_LIMIT)

    def like(array):
        return jax.ShapeDtypeStruct(array.shape, array.dtype)

    wide_shape = jax.ShapeDtypeStruct(initial_state.shape, F32)
    pool_shape = jax.ShapeDtypeStruct((faces, insts * LANE), BF16)
    out_shapes = [jax.ShapeDtypeStruct((capacity, insts * LANE), BF16)] * slots
    flux_shape = jax.ShapeDtypeStruct((faces, FIELDS * LANE), BF16)
    hot_shape = jax.ShapeDtypeStruct((faces, faces + slots * capacity), BF16)
    factor_shape = jax.ShapeDtypeStruct((slots * capacity, LANE // FPTS * LANE), F32)

    def exchange(outgoing):
        return [
            lax.ppermute(outgoing[swap], ("inst", "dom"), routes[swap]) for swap in SWAP_ORDER
        ]

    entry_shape = jax.ShapeDtypeStruct((NI, width), F32)
    mend_shape = jax.ShapeDtypeStruct((slots * capacity, insts * LANE), F32)
    message_shape = jax.ShapeDtypeStruct(
        (message_rows(insts, elems, slots * capacity)[-1], pl.cdiv(width, LANE) * LANE), BF16
    )
    chunks = [pltpu.VMEM((pl.cdiv(width, LANE) * insts * elems, LANE), F32)] * 2
    diag_cost = pl.CostEstimate(
        flops=2 * insts * diagonal_blocks.size, bytes_accessed=2 * diagonal_blocks.size,
        transcendentals=0,
    )
    spread, order = pl.pallas_call(
        table_kernel,
        out_shape=[
            jax.ShapeDtypeStruct((LANE, FIELDS * LANE), BF16),
            jax.ShapeDtypeStruct((FIELDS * FIELDS * FPTS, FIELDS * LANE), BF16),
        ],
        out_specs=[vmem] * 2,
        compiler_params=params,
        cost_estimate=pl.CostEstimate(flops=10**10, bytes_accessed=10**6, transcendentals=0),
        name="tables",
    )()
    freq, _ = lax.optimization_barrier((frequency, spread))
    flux, hot, entries, pool, *outgoing = pl.pallas_call(
        functools.partial(first_kernel, spectral, second),
        out_shape=[flux_shape, hot_shape, entry_shape, pool_shape] + out_shapes,
        in_specs=[smem] * 2 + [vmem] * 6,
        out_specs=[vmem] * (4 + len(out_shapes)),
        compiler_params=params,
        cost_estimate=pl.CostEstimate(flops=10**10, bytes_accessed=10**6, transcendentals=0),
        name="first_traces",
    )(place, freq, order, initial_state, trace_wide, send_list, flux_jacobian, sources)
    got = exchange(outgoing)
    base = pl.pallas_call(
        base_kernel,
        out_shape=wide_shape,
        in_specs=[vmem] * 4,
        out_specs=vmem,
        scratch_shapes=chunks,
        compiler_params=params,
        cost_estimate=diag_cost,
        name="own_terms",
    )(initial_state, diagonal_blocks, forcing, entries)
    partial, message, *outgoing = pl.pallas_call(
        functools.partial(step_kernel, parts),
        out_shape=[wide_shape, message_shape] + out_shapes,
        in_specs=[smem] + [vmem] * (slots + 9),
        out_specs=[vmem] * (2 + len(out_shapes)),
        compiler_params=params,
        name="first_step",
    )(place, spread, *got, initial_state, pool, base, hot, flux, lift_wide, trace_wide, send_list)
    messages = [
        lax.ppermute(message, "inst", [((i + rank) % ranks, i) for i in range(ranks)])
        for rank in range(1, ranks)
    ]
    got = exchange(outgoing)
    state, base, factors, mend = pl.pallas_call(
        functools.partial(last_base_kernel, ranks),
        out_shape=[like(initial_state), wide_shape, factor_shape, mend_shape],
        in_specs=[vmem] * (ranks + 9),
        out_specs=[vmem] * 4,
        scratch_shapes=chunks,
        compiler_params=params,
        cost_estimate=diag_cost,
        name="last_own_terms",
    )(partial, initial_state, *messages, diagonal_blocks, forcing, trace_wide, hot, flux, spread,
      lift_wide, entries)
    return pl.pallas_call(
        functools.partial(last_kernel, parts),
        out_shape=[like(initial_state), wide_shape],
        in_specs=[smem] + [vmem] * (slots + 6),
        out_specs=[pl.BlockSpec(memory_space=pl.ANY)] * 2,
        scratch_shapes=[
            pltpu.VMEM(initial_state.shape, BF16),
            pltpu.VMEM(initial_state.shape, F32),
            pltpu.SemaphoreType.DMA((2, insts)),
        ],
        compiler_params=params,
        name="last_step",
    )(place, *got, state, base, hot, factors, mend, lift_wide)


def solution(mesh):
    return jax.shard_map(
        on_device,
        mesh=mesh,
        in_specs=(
            P("inst", "dom", None),
            P("inst", "dom", None),
            P("dom", None, None),
            P("dom", None),
            P("dom", None, None),
            P("dom", None),
            P(),
        ),
        out_specs=(P("inst", "dom", None), P("inst", "dom", None)),
        check_vma=False,
    )
```

```python
import functools
import math

import jax
import jax.numpy as jnp
import numpy as np
from jax import lax
from jax.experimental import pallas as pl
from jax.experimental.pallas import tpu as pltpu
from jax.sharding import PartitionSpec as P

FIELDS = 5
ORDER = 3
NODES = 64
FPTS = 16
NI = 8
REACH = 2
ITERS = 2


pseudo_step = 0.5
dissipation = 0.25


def gauss_legendre(count):
    points = []
    weights = []
    for i in range(count):
        where = math.cos(math.pi * (i + 0.75) / (count + 0.5))
        for sweep in range(100):
            before = 1.0
            value = where
            for j in range(2, count + 1):
                after = ((2 * j - 1) * where * value - (j - 1) * before) / j
                before = value
                value = after
            slope = count * (where * value - before) / (where * where - 1.0)
            where = where - value / slope
        before = 1.0
        value = where
        for j in range(2, count + 1):
            after = ((2 * j - 1) * where * value - (j - 1) * before) / j
            before = value
            value = after
        slope = count * (where * value - before) / (where * where - 1.0)
        points.append(where)
        weights.append(2.0 / ((1.0 - where * where) * slope * slope))
    return (np.array(points[::-1]), np.array(weights[::-1]))


def lagrange_at(points, where):
    values = np.ones(points.shape[0])
    for i in range(points.shape[0]):
        for j in range(points.shape[0]):
            if j != i:
                values[i] = values[i] * (where - points[j]) / (points[i] - points[j])
    return values


def tables(order, count):
    points, weights = gauss_legendre(order + 1)
    at_minus = lagrange_at(points, -1.0)
    at_plus = lagrange_at(points, 1.0)
    per_side = order + 1
    node_count = per_side**3
    face_points = per_side**2
    trace_table = np.zeros((node_count, 6 * face_points))
    lift_table = np.zeros((node_count, 6 * face_points))
    for k in range(per_side):
        for j in range(per_side):
            for i in range(per_side):
                node = i + per_side * j + per_side * per_side * k
                entries = [
                    (0, at_minus[i], j + per_side * k, weights[i]),
                    (1, at_plus[i], j + per_side * k, weights[i]),
                    (2, at_minus[j], i + per_side * k, weights[j]),
                    (3, at_plus[j], i + per_side * k, weights[j]),
                    (4, at_minus[k], i + per_side * j, weights[k]),
                    (5, at_plus[k], i + per_side * j, weights[k]),
                ]
                for face_index, factor, point, weight in entries:
                    trace_table[node, face_index * face_points + point] = factor
                    lift_table[node, face_index * face_points + point] = factor / weight
    spectral = np.zeros((count, count))
    second = np.zeros((count, count))
    for t in range(count):
        for s in range(count):
            if t != s:
                spectral[t, s] = 0.5 * (-1.0) ** (t - s + 1) / math.tan(math.pi * (t - s) / count)
                second[t, s] = -0.5 * (-1.0) ** (t - s) / math.sin(math.pi * (t - s) / count) ** 2
            else:
                second[t, s] = -(count * count + 2.0) / 12.0
    return (trace_table, lift_table, spectral, second)


LANE = 128
WIDE = FIELDS * NODES
FACES = 6
VMEM_LIMIT = 16 * 1024 * 1024
BF16 = jnp.bfloat16
F32 = jnp.float32
OFFSETS = list(range(-REACH, 0)) + list(range(1, REACH + 1))
SWAP_ORDER = (3, 1, 2, 0)


def wide_tables():
    trace_np, lift_np, spectral_np, second_np = tables(ORDER, NI)
    trace_wide = np.zeros((WIDE, FACES * LANE))
    lift_wide = np.zeros((FACES * LANE, WIDE))
    for c in range(FIELDS):
        rows = slice(c * NODES, (c + 1) * NODES)
        for f in range(FACES):
            cols = slice(f * LANE + c * FPTS, f * LANE + (c + 1) * FPTS)
            face = slice(f * FPTS, (f + 1) * FPTS)
            trace_wide[rows, cols] = trace_np[:, face]
            lift_wide[cols, rows] = lift_np[:, face].T
    return trace_wide, lift_wide, spectral_np[:, 0], second_np[:, 0]


def iotas(shape):
    return [lax.broadcasted_iota(jnp.int32, shape, axis) for axis in range(2)]


def one_hot(mask):
    return jnp.where(mask, 1.0, 0.0).astype(BF16)


def spread_table():
    row, col = iotas((LANE, FIELDS * LANE))
    inside = col % LANE < FIELDS * FPTS
    return one_hot(inside & (row == col // LANE * FPTS + col % FPTS))


def order_table():
    row, col = iotas((FIELDS * FIELDS * FPTS, FIELDS * LANE))
    place = col % LANE
    source = place // FPTS * FIELDS * FPTS + col // LANE * FPTS + col % FPTS
    return one_hot((place < FIELDS * FPTS) & (row == source))


def trace_pool(state, trace_wide, insts, elems):
    wide = jnp.dot(state, trace_wide, preferred_element_type=F32).astype(BF16)
    by_inst = []
    for t in range(insts):
        rows = wide[t * elems : (t + 1) * elems]
        by_inst.append(
            jnp.concatenate([rows[:, f * LANE : (f + 1) * LANE] for f in range(FACES)], 0)
        )
    return jnp.concatenate(by_inst, 1)


def swap_routes(ranks, parts):
    near = [[(p, p + 1) for p in range(first, parts - 1, 2)] for first in range(2)]
    far = [
        [(p + i, p + i + 2) for p in range(first, parts - 3, 4) for i in range(2)]
        for first in (0, 2)
    ]
    routes = []
    for pairs in near + far:
        met = {p for pair in pairs for p in pair}
        alone = [p for p in range(parts) if p not in met]
        swaps = [(r * parts + p, r * parts + q) for r in range(ranks) for p, q in pairs]
        swaps += [(r * parts + p, (r ^ 1) * parts + p) for r in range(0, ranks, 2) for p in alone]
        routes.append(swaps + [(q, p) for p, q in swaps])
    return routes


def by_swap(place, by_offset):
    two_down, one_down, one_up, two_up = by_offset
    even = place % 2 == 0
    low = place // 2 % 2 == 0
    return [
        jnp.where(even, one_up, one_down),
        jnp.where(even, one_down, one_up),
        jnp.where(low, two_up, two_down),
        jnp.where(low, two_down, two_up),
    ]


def by_offset(place, blocks):
    even = place % 2 == 0
    low = place // 2 % 2 == 0
    return [
        jnp.where(low, blocks[3], blocks[2]),
        jnp.where(even, blocks[1], blocks[0]),
        jnp.where(even, blocks[0], blocks[1]),
        jnp.where(low, blocks[2], blocks[3]),
    ]


def fill_outgoing(pool, send, out_refs, place, elems):
    slots, capacity = send.shape
    rows, cols = iotas((FACES * elems, slots * capacity))
    ids = FACES * (rows % elems) + rows // elems
    wanted = jnp.concatenate([send[k : k + 1] for k in range(slots)], 1)
    out = lax.dot_general(
        one_hot(ids == wanted), pool, (((0,), (0,)), ((), ())), preferred_element_type=F32
    )
    blocks = by_swap(place, [out[k * capacity : (k + 1) * capacity] for k in range(slots)])
    for block, ref in zip(blocks, out_refs):
        ref[...] = block.astype(BF16)


def diagonal(states, diag, wide_ref, prod_ref, insts, elems):
    tall = insts * elems
    width = diag.shape[1]
    cuts = [(j, j * LANE, min((j + 1) * LANE, width)) for j in range(pl.cdiv(width, LANE))]
    for t in range(insts):
        rows = states[t].astype(F32)
        for j, low, high in cuts:
            first = j * tall + t * elems
            wide_ref[first : first + elems, 0 : high - low] = rows[:, low:high]
    for e in range(elems):
        rows = jnp.concatenate(
            [wide_ref[pl.ds(j * tall + e, insts, stride=elems), :] for j, low, high in cuts], 1
        )
        product = jnp.dot(rows[:, 0:width].astype(BF16), diag[e], preferred_element_type=F32)
        for j, low, high in cuts:
            chunk = product[:, low:high]
            if high - low < LANE:
                chunk = jnp.concatenate([chunk, jnp.zeros((insts, LANE - high + low), F32)], 1)
            prod_ref[pl.ds(j * tall + e, insts, stride=elems), :] = chunk
    return [
        jnp.concatenate(
            [
                prod_ref[j * tall + t * elems : j * tall + (t + 1) * elems, 0 : high - low]
                for j, low, high in cuts
            ],
            1,
        )
        for t in range(insts)
    ]


def flux_order(rows, order):
    per_face = FIELDS * FIELDS * FPTS
    by_face = jnp.concatenate(
        [rows[:, f * per_face : (f + 1) * per_face] for f in range(FACES)], 0
    )
    return jnp.dot(by_face, order, preferred_element_type=F32).astype(BF16)


def source_table(sources, elems, slots):
    faces = FACES * elems
    columns = lax.broadcasted_iota(jnp.int32, (elems, faces + slots), 1)
    ids = jnp.where(columns < faces, FACES * (columns % elems) + columns // elems, columns)
    hot = [jnp.where(sources[:, f : f + 1] == ids, 1.0, 0.0) for f in range(FACES)]
    return jnp.concatenate(hot, 0).astype(BF16)


def face_flux(picked, flux, spread, insts):
    count = picked.shape[0]
    stacked = jnp.concatenate([picked[:, t * LANE : (t + 1) * LANE] for t in range(insts)], 0)
    wide = jnp.dot(stacked, spread, preferred_element_type=F32)
    normal = []
    for t in range(insts):
        rows = wide[t * count : (t + 1) * count]
        summed = flux[:, 0:LANE] * rows[:, 0:LANE]
        for d in range(1, FIELDS):
            summed += flux[:, d * LANE : (d + 1) * LANE] * rows[:, d * LANE : (d + 1) * LANE]
        normal.append(summed.astype(BF16))
    return normal


def lift_faces(normal, lift, elems):
    rows = [
        jnp.concatenate([n[f * elems : (f + 1) * elems] for f in range(FACES)], 1) for n in normal
    ]
    return jnp.dot(jnp.concatenate(rows, 0), lift, preferred_element_type=F32)


def couple(entry_ref, states, t, shift, insts):
    summed = None
    for s in range(insts):
        d = (t - s + shift * insts) % NI
        term = entry_ref[d : d + 1, :] * states[s].astype(F32)
        summed = term if summed is None else summed + term
    return summed


def rotated(flux):
    place = lax.broadcasted_iota(jnp.int32, (flux.shape[0], LANE), 1) // FPTS
    blocks = []
    for k in range(LANE // FPTS):
        block = jnp.zeros((flux.shape[0], LANE), F32)
        for d in range(FIELDS):
            met = place == (d + k) % (LANE // FPTS)
            block = jnp.where(met, flux[:, d * LANE : (d + 1) * LANE], block)
        blocks.append(block)
    return jnp.concatenate(blocks, 1)


def slot_normal(blocks, factors, insts):
    count = blocks.shape[0]
    stacked = jnp.concatenate([blocks[:, t * LANE : (t + 1) * LANE] for t in range(insts)], 0)
    summed = [None] * insts
    for k in range(LANE // FPTS):
        turned = stacked if k == 0 else pltpu.roll(stacked, k * FPTS, 1)
        for t in range(insts):
            term = factors[:, k * LANE : (k + 1) * LANE] * turned[t * count : (t + 1) * count]
            summed[t] = term if k == 0 else summed[t] + term
    return [rows.astype(BF16) for rows in summed]


def table_kernel(spread_ref, order_ref):
    spread_ref[...] = spread_table()
    order_ref[...] = order_table()


def first_kernel(spectral, second, place_ref, freq_ref, order_ref, state_ref, trace_ref, send_ref, flux_ref, source_ref,
                 flux_out_ref, hot_ref, entry_ref, pool_ref, *out_refs):
    insts, elems, width = state_ref.shape
    state = state_ref[...].reshape(insts * elems, width)
    pool = trace_pool(state, trace_ref[...], insts, elems)
    pool_ref[...] = pool
    fill_outgoing(pool, send_ref[0], out_refs, place_ref[0], elems)
    slots = send_ref.shape[1] * send_ref.shape[2]
    hot_ref[...] = source_table(source_ref[...].T, elems, slots)
    flux_out_ref[...] = flux_order(flux_ref[...], order_ref[...])
    freq = freq_ref[0]
    for d in range(NI):
        entry = freq * float(spectral[d]) - dissipation * float(second[d])
        entry_ref[d : d + 1, :] = jnp.full((1, width), entry, F32)


def base_kernel(state_ref, diag_ref, forcing_ref, entry_ref, prod_out_ref, rest_ref, wide_ref,
                prod_ref):
    insts, elems, width = state_ref.shape
    states = [state_ref[t] for t in range(insts)]
    products = diagonal(states, diag_ref, wide_ref, prod_ref, insts, elems)
    for t in range(insts):
        prod_out_ref[t] = products[t]
        rest_ref[t] = couple(entry_ref, states, t, 0, insts) - forcing_ref[t].astype(F32)


def last_base_kernel(state_ref, pool_ref, diag_ref, forcing_ref, hot_ref, flux_ref, spread_ref,
                     lift_ref, base_ref, factor_ref, wide_ref, prod_ref):
    insts, elems, width = state_ref.shape
    flux = flux_ref[...]
    hot = hot_ref[...]
    faces = hot.shape[0]
    factors = lax.dot_general(hot, flux, (((0,), (0,)), ((), ())), preferred_element_type=F32)
    factor_ref[...] = rotated(factors[faces:])
    empty = jnp.zeros((hot.shape[1] - faces, insts * LANE), BF16)
    pool = jnp.concatenate([pool_ref[...], empty], 0)
    picked = jnp.dot(hot, pool, preferred_element_type=F32).astype(BF16)
    normal = face_flux(picked, flux.astype(F32), spread_ref[...], insts)
    lifted = lift_faces(normal, lift_ref[...], elems)
    states = [state_ref[t].astype(BF16) for t in range(insts)]
    products = diagonal(states, diag_ref, wide_ref, prod_ref, insts, elems)
    for t in range(insts):
        base_ref[t] = (
            products[t] + lifted[t * elems : (t + 1) * elems] - forcing_ref[t].astype(F32)
        )


def message_kernel(ranks, partial_ref, first_ref, base_ref, entry_ref, *refs):
    message_refs, (state_ref, out_ref) = refs[: ranks - 1], refs[ranks - 1 :]
    insts, elems, width = base_ref.shape
    firsts = [[first_ref[t] for t in range(insts)]]
    partials = [[partial_ref[t] for t in range(insts)]]
    spatial = [None]
    for message_ref in message_refs:
        rows = [
            message_ref[i * elems : (i + 1) * elems, 0:width] for i in range(3 * insts)
        ]
        firsts.append(rows[:insts])
        partials.append(rows[insts : 2 * insts])
        spatial.append(rows[2 * insts :])
    states = []
    for k in range(ranks):
        of_rank = []
        for t in range(insts):
            state = partials[k][t].astype(F32)
            for j in range(ranks):
                if j != k:
                    state -= pseudo_step * couple(entry_ref, firsts[j], t, k - j, insts)
            of_rank.append(state.astype(BF16))
        states.append(of_rank)
    for t in range(insts):
        state_ref[t] = states[0][t]
        coupling = couple(entry_ref, states[0], t, 0, insts)
        missing = jnp.zeros((elems, width), F32)
        for k in range(1, ranks):
            coupling += couple(entry_ref, states[k], t, -k, insts)
            missing += couple(entry_ref, spatial[k], t, -k, insts)
        out_ref[t] = base_ref[t] + coupling.astype(BF16).astype(F32) - pseudo_step * missing


def received(parts, place, got_refs):
    got_refs = {swap: got_refs[i] for i, swap in enumerate(SWAP_ORDER)}
    arrived = by_offset(
        place, [got_refs[swap][...].astype(F32) for swap in range(len(OFFSETS))]
    )
    for k, offset in enumerate(OFFSETS):
        exists = (place + offset >= 0) & (place + offset < parts)
        arrived[k] = jnp.where(exists, arrived[k], jnp.zeros_like(arrived[k]))
    return jnp.concatenate(arrived, 0)


def step_kernel(parts, place_ref, spread_ref, *refs):
    got_refs, refs = refs[: len(OFFSETS)], refs[len(OFFSETS) :]
    (state_ref, pool_ref, prod_ref, rest_ref, hot_ref, flux_ref, lift_ref, trace_ref, send_ref,
     partial_ref, message_ref, next_pool_ref, *out_refs) = refs
    insts, elems, width = state_ref.shape
    place = place_ref[0]
    blocks = received(parts, place, got_refs).astype(BF16)
    pool = jnp.concatenate([pool_ref[...], blocks], 0)
    picked = jnp.dot(hot_ref[...], pool, preferred_element_type=F32).astype(BF16)
    normal = face_flux(picked, flux_ref[...].astype(F32), spread_ref[...], insts)
    lifted = lift_faces(normal, lift_ref[...], elems)
    message_ref[...] = jnp.zeros_like(message_ref)
    fresh = []
    for t in range(insts):
        spatial = prod_ref[t] + lifted[t * elems : (t + 1) * elems]
        moved = state_ref[t].astype(F32) - pseudo_step * (spatial + rest_ref[t])
        partial_ref[t] = moved
        fresh.append(moved.astype(BF16))
        for i, block in enumerate((state_ref[t], fresh[t], spatial.astype(BF16))):
            low = (i * insts + t) * elems
            message_ref[low : low + elems, 0:width] = block
    pool = trace_pool(jnp.concatenate(fresh, 0), trace_ref[...], insts, elems)
    next_pool_ref[...] = pool
    fill_outgoing(pool, send_ref[0], out_refs, place, elems)


def last_kernel(parts, place_ref, *refs):
    got_refs, refs = refs[: len(OFFSETS)], refs[len(OFFSETS) :]
    (state_ref, base_ref, hot_ref, factor_ref, lift_ref, final_hbm, residual_hbm,
     final_ref, residual_ref, sems) = refs
    insts, elems, width = state_ref.shape
    blocks = received(parts, place_ref[0], got_refs)
    normal = slot_normal(blocks, factor_ref[...], insts)
    empty = jnp.zeros((FACES * elems, insts * LANE), BF16)
    rows = jnp.concatenate([empty, jnp.concatenate(normal, 1)], 0)
    spots = jnp.dot(hot_ref[...], rows, preferred_element_type=F32).astype(BF16)
    lifted = lift_faces(
        [spots[:, t * LANE : (t + 1) * LANE] for t in range(insts)], lift_ref[...], elems
    )
    copies = []
    for t in range(insts):
        residual = base_ref[t] + lifted[t * elems : (t + 1) * elems]
        residual_ref[t] = residual
        final_ref[t] = (state_ref[t].astype(F32) - pseudo_step * residual).astype(BF16)
        copies += [
            pltpu.make_async_copy(residual_ref.at[t], residual_hbm.at[t], sems.at[0, t]),
            pltpu.make_async_copy(final_ref.at[t], final_hbm.at[t], sems.at[1, t]),
        ]
        copies[-2].start()
        copies[-1].start()
    for copy in copies:
        copy.wait()


def on_device(
    initial_state, forcing, diagonal_blocks, flux_jacobian, send_list, source_index, frequency
):
    insts, elems, width = initial_state.shape
    parts = lax.axis_size("dom")
    ranks = lax.axis_size("inst")
    slots, capacity = send_list.shape[1:]
    faces = FACES * elems
    trace_np, lift_np, spectral, second = wide_tables()
    trace_wide = jnp.asarray(trace_np, BF16)
    lift_wide = jnp.asarray(lift_np, BF16)
    place = lax.axis_index("dom").reshape(1)
    sources = source_index.T
    routes = swap_routes(ranks, parts)

    smem = pl.BlockSpec(memory_space=pltpu.SMEM)
    vmem = pl.BlockSpec(memory_space=pltpu.VMEM)
    params = pltpu.CompilerParams(vmem_limit_bytes=VMEM_LIMIT)

    def like(array):
        return jax.ShapeDtypeStruct(array.shape, array.dtype)

    wide_shape = jax.ShapeDtypeStruct(initial_state.shape, F32)
    pool_shape = jax.ShapeDtypeStruct((faces, insts * LANE), BF16)
    out_shapes = [jax.ShapeDtypeStruct((capacity, insts * LANE), BF16)] * slots
    flux_shape = jax.ShapeDtypeStruct((faces, FIELDS * LANE), BF16)
    hot_shape = jax.ShapeDtypeStruct((faces, faces + slots * capacity), BF16)
    factor_shape = jax.ShapeDtypeStruct((slots * capacity, LANE // FPTS * LANE), F32)

    def exchange(outgoing):
        return [
            lax.ppermute(outgoing[swap], ("inst", "dom"), routes[swap]) for swap in SWAP_ORDER
        ]

    entry_shape = jax.ShapeDtypeStruct((NI, width), F32)
    message_shape = jax.ShapeDtypeStruct((3 * insts * elems, pl.cdiv(width, LANE) * LANE), BF16)
    chunks = [pltpu.VMEM((pl.cdiv(width, LANE) * insts * elems, LANE), F32)] * 2
    diag_cost = pl.CostEstimate(
        flops=2 * insts * diagonal_blocks.size, bytes_accessed=2 * diagonal_blocks.size,
        transcendentals=0,
    )
    spread, order = pl.pallas_call(
        table_kernel,
        out_shape=[
            jax.ShapeDtypeStruct((LANE, FIELDS * LANE), BF16),
            jax.ShapeDtypeStruct((FIELDS * FIELDS * FPTS, FIELDS * LANE), BF16),
        ],
        out_specs=[vmem] * 2,
        compiler_params=params,
        cost_estimate=pl.CostEstimate(flops=10**10, bytes_accessed=10**6, transcendentals=0),
        name="tables",
    )()
    freq, _ = lax.optimization_barrier((frequency, spread))
    flux, hot, entries, pool, *outgoing = pl.pallas_call(
        functools.partial(first_kernel, spectral, second),
        out_shape=[flux_shape, hot_shape, entry_shape, pool_shape] + out_shapes,
        in_specs=[smem] * 2 + [vmem] * 6,
        out_specs=[vmem] * (4 + len(out_shapes)),
        compiler_params=params,
        cost_estimate=pl.CostEstimate(flops=10**10, bytes_accessed=10**6, transcendentals=0),
        name="first_traces",
    )(place, freq, order, initial_state, trace_wide, send_list, flux_jacobian, sources)
    got = exchange(outgoing)
    product, rest = pl.pallas_call(
        base_kernel,
        out_shape=[wide_shape] * 2,
        in_specs=[vmem] * 4,
        out_specs=[vmem] * 2,
        scratch_shapes=chunks,
        compiler_params=params,
        cost_estimate=diag_cost,
        name="own_terms",
    )(initial_state, diagonal_blocks, forcing, entries)
    partial, message, pool, *outgoing = pl.pallas_call(
        functools.partial(step_kernel, parts),
        out_shape=[wide_shape, message_shape, pool_shape] + out_shapes,
        in_specs=[smem] + [vmem] * (slots + 10),
        out_specs=[vmem] * (3 + len(out_shapes)),
        compiler_params=params,
        name="first_step",
    )(place, spread, *got, initial_state, pool, product, rest, hot, flux, lift_wide, trace_wide,
      send_list)
    messages = [
        lax.ppermute(message, "inst", [((i + rank) % ranks, i) for i in range(ranks)])
        for rank in range(1, ranks)
    ]
    got = exchange(outgoing)
    base, factors = pl.pallas_call(
        last_base_kernel,
        out_shape=[wide_shape, factor_shape],
        in_specs=[vmem] * 8,
        out_specs=[vmem] * 2,
        scratch_shapes=chunks,
        compiler_params=params,
        cost_estimate=diag_cost,
        name="last_own_terms",
    )(partial, pool, diagonal_blocks, forcing, hot, flux, spread, lift_wide)
    state, base = pl.pallas_call(
        functools.partial(message_kernel, ranks),
        out_shape=[like(initial_state), wide_shape],
        in_specs=[vmem] * (ranks + 3),
        out_specs=[vmem] * 2,
        compiler_params=params,
        name="message_terms",
    )(partial, initial_state, base, entries, *messages)
    return pl.pallas_call(
        functools.partial(last_kernel, parts),
        out_shape=[like(initial_state), wide_shape],
        in_specs=[smem] + [vmem] * (slots + 5),
        out_specs=[pl.BlockSpec(memory_space=pl.ANY)] * 2,
        scratch_shapes=[
            pltpu.VMEM(initial_state.shape, BF16),
            pltpu.VMEM(initial_state.shape, F32),
            pltpu.SemaphoreType.DMA((2, insts)),
        ],
        compiler_params=params,
        name="last_step",
    )(place, *got, state, base, hot, factors, lift_wide)


def solution(mesh):
    return jax.shard_map(
        on_device,
        mesh=mesh,
        in_specs=(
            P("inst", "dom", None),
            P("inst", "dom", None),
            P("dom", None, None),
            P("dom", None),
            P("dom", None, None),
            P("dom", None),
            P(),
        ),
        out_specs=(P("inst", "dom", None), P("inst", "dom", None)),
        check_vma=False,
    )
```

```python
import functools
import math

import jax
import jax.numpy as jnp
import numpy as np
from jax import lax
from jax.experimental import pallas as pl
from jax.experimental.pallas import tpu as pltpu
from jax.sharding import PartitionSpec as P

FIELDS = 5
ORDER = 3
NODES = 64
FPTS = 16
NI = 8
REACH = 2
ITERS = 2


pseudo_step = 0.5
dissipation = 0.25


def gauss_legendre(count):
    points = []
    weights = []
    for i in range(count):
        where = math.cos(math.pi * (i + 0.75) / (count + 0.5))
        for sweep in range(100):
            before = 1.0
            value = where
            for j in range(2, count + 1):
                after = ((2 * j - 1) * where * value - (j - 1) * before) / j
                before = value
                value = after
            slope = count * (where * value - before) / (where * where - 1.0)
            where = where - value / slope
        before = 1.0
        value = where
        for j in range(2, count + 1):
            after = ((2 * j - 1) * where * value - (j - 1) * before) / j
            before = value
            value = after
        slope = count * (where * value - before) / (where * where - 1.0)
        points.append(where)
        weights.append(2.0 / ((1.0 - where * where) * slope * slope))
    return (np.array(points[::-1]), np.array(weights[::-1]))


def lagrange_at(points, where):
    values = np.ones(points.shape[0])
    for i in range(points.shape[0]):
        for j in range(points.shape[0]):
            if j != i:
                values[i] = values[i] * (where - points[j]) / (points[i] - points[j])
    return values


def tables(order, count):
    points, weights = gauss_legendre(order + 1)
    at_minus = lagrange_at(points, -1.0)
    at_plus = lagrange_at(points, 1.0)
    per_side = order + 1
    node_count = per_side**3
    face_points = per_side**2
    trace_table = np.zeros((node_count, 6 * face_points))
    lift_table = np.zeros((node_count, 6 * face_points))
    for k in range(per_side):
        for j in range(per_side):
            for i in range(per_side):
                node = i + per_side * j + per_side * per_side * k
                entries = [
                    (0, at_minus[i], j + per_side * k, weights[i]),
                    (1, at_plus[i], j + per_side * k, weights[i]),
                    (2, at_minus[j], i + per_side * k, weights[j]),
                    (3, at_plus[j], i + per_side * k, weights[j]),
                    (4, at_minus[k], i + per_side * j, weights[k]),
                    (5, at_plus[k], i + per_side * j, weights[k]),
                ]
                for face_index, factor, point, weight in entries:
                    trace_table[node, face_index * face_points + point] = factor
                    lift_table[node, face_index * face_points + point] = factor / weight
    spectral = np.zeros((count, count))
    second = np.zeros((count, count))
    for t in range(count):
        for s in range(count):
            if t != s:
                spectral[t, s] = 0.5 * (-1.0) ** (t - s + 1) / math.tan(math.pi * (t - s) / count)
                second[t, s] = -0.5 * (-1.0) ** (t - s) / math.sin(math.pi * (t - s) / count) ** 2
            else:
                second[t, s] = -(count * count + 2.0) / 12.0
    return (trace_table, lift_table, spectral, second)


LANE = 128
WIDE = FIELDS * NODES
FACES = 6
VMEM_LIMIT = 16 * 1024 * 1024
BF16 = jnp.bfloat16
F32 = jnp.float32
OFFSETS = list(range(-REACH, 0)) + list(range(1, REACH + 1))
FIRST_ORDER = (3, 1, 2, 0)
LAST_ORDER = (2, 1, 3, 0)


def wide_tables():
    trace_np, lift_np, spectral_np, second_np = tables(ORDER, NI)
    trace_wide = np.zeros((WIDE, FACES * LANE))
    lift_wide = np.zeros((FACES * LANE, WIDE))
    for c in range(FIELDS):
        rows = slice(c * NODES, (c + 1) * NODES)
        for f in range(FACES):
            cols = slice(f * LANE + c * FPTS, f * LANE + (c + 1) * FPTS)
            face = slice(f * FPTS, (f + 1) * FPTS)
            trace_wide[rows, cols] = trace_np[:, face]
            lift_wide[cols, rows] = lift_np[:, face].T
    return trace_wide, lift_wide, spectral_np[:, 0], second_np[:, 0]


def iotas(shape):
    return [lax.broadcasted_iota(jnp.int32, shape, axis) for axis in range(2)]


def one_hot(mask):
    return jnp.where(mask, 1.0, 0.0).astype(BF16)


def spread_table():
    row, col = iotas((LANE, FIELDS * LANE))
    inside = col % LANE < FIELDS * FPTS
    return one_hot(inside & (row == col // LANE * FPTS + col % FPTS))


def order_table():
    row, col = iotas((FIELDS * FIELDS * FPTS, FIELDS * LANE))
    place = col % LANE
    source = place // FPTS * FIELDS * FPTS + col // LANE * FPTS + col % FPTS
    return one_hot((place < FIELDS * FPTS) & (row == source))


def trace_pool(state, trace_wide, insts, elems):
    wide = jnp.dot(state, trace_wide, preferred_element_type=F32).astype(BF16)
    by_inst = []
    for t in range(insts):
        rows = wide[t * elems : (t + 1) * elems]
        by_inst.append(
            jnp.concatenate([rows[:, f * LANE : (f + 1) * LANE] for f in range(FACES)], 0)
        )
    return jnp.concatenate(by_inst, 1)


def swap_routes(ranks, parts):
    near = [[(p, p + 1) for p in range(first, parts - 1, 2)] for first in range(2)]
    far = [
        [(p + i, p + i + 2) for p in range(first, parts - 3, 4) for i in range(2)]
        for first in (0, 2)
    ]
    routes = []
    for pairs in near + far:
        met = {p for pair in pairs for p in pair}
        alone = [p for p in range(parts) if p not in met]
        idle = [(p, p + 1) for p in alone if p + 1 in alone]
        alone = [p for p in alone if p + 1 not in alone and p - 1 not in alone]
        swaps = [(r * parts + p, r * parts + q) for r in range(ranks) for p, q in pairs + idle]
        swaps += [(r * parts + p, (r ^ 1) * parts + p) for r in range(0, ranks, 2) for p in alone]
        routes.append(swaps + [(q, p) for p, q in swaps])
    return routes


def by_swap(place, by_offset):
    two_down, one_down, one_up, two_up = by_offset
    even = place % 2 == 0
    low = place // 2 % 2 == 0
    return [
        jnp.where(even, one_up, one_down),
        jnp.where(even, one_down, one_up),
        jnp.where(low, two_up, two_down),
        jnp.where(low, two_down, two_up),
    ]


def by_offset(place, blocks):
    even = place % 2 == 0
    low = place // 2 % 2 == 0
    return [
        jnp.where(low, blocks[3], blocks[2]),
        jnp.where(even, blocks[1], blocks[0]),
        jnp.where(even, blocks[0], blocks[1]),
        jnp.where(low, blocks[2], blocks[3]),
    ]


def fill_outgoing(pool, send, out_refs, place, elems):
    slots, capacity = send.shape
    rows, cols = iotas((FACES * elems, slots * capacity))
    ids = FACES * (rows % elems) + rows // elems
    wanted = jnp.concatenate([send[k : k + 1] for k in range(slots)], 1)
    out = lax.dot_general(
        one_hot(ids == wanted), pool, (((0,), (0,)), ((), ())), preferred_element_type=F32
    )
    blocks = by_swap(place, [out[k * capacity : (k + 1) * capacity] for k in range(slots)])
    for block, ref in zip(blocks, out_refs):
        ref[...] = block.astype(BF16)


def diagonal(states, diag, wide_ref, prod_ref, insts, elems):
    tall = insts * elems
    width = diag.shape[1]
    cuts = [(j, j * LANE, min((j + 1) * LANE, width)) for j in range(pl.cdiv(width, LANE))]
    for t in range(insts):
        rows = states[t].astype(F32)
        for j, low, high in cuts:
            first = j * tall + t * elems
            wide_ref[first : first + elems, 0 : high - low] = rows[:, low:high]
    for e in range(elems):
        rows = jnp.concatenate(
            [wide_ref[pl.ds(j * tall + e, insts, stride=elems), :] for j, low, high in cuts], 1
        )
        product = jnp.dot(rows[:, 0:width].astype(BF16), diag[e], preferred_element_type=F32)
        for j, low, high in cuts:
            chunk = product[:, low:high]
            if high - low < LANE:
                chunk = jnp.concatenate([chunk, jnp.zeros((insts, LANE - high + low), F32)], 1)
            prod_ref[pl.ds(j * tall + e, insts, stride=elems), :] = chunk
    return [
        jnp.concatenate(
            [
                prod_ref[j * tall + t * elems : j * tall + (t + 1) * elems, 0 : high - low]
                for j, low, high in cuts
            ],
            1,
        )
        for t in range(insts)
    ]


def flux_order(rows, order):
    per_face = FIELDS * FIELDS * FPTS
    by_face = jnp.concatenate(
        [rows[:, f * per_face : (f + 1) * per_face] for f in range(FACES)], 0
    )
    return jnp.dot(by_face, order, preferred_element_type=F32).astype(BF16)


def source_table(sources, elems, slots):
    faces = FACES * elems
    columns = lax.broadcasted_iota(jnp.int32, (elems, faces + slots), 1)
    ids = jnp.where(columns < faces, FACES * (columns % elems) + columns // elems, columns)
    hot = [jnp.where(sources[:, f : f + 1] == ids, 1.0, 0.0) for f in range(FACES)]
    return jnp.concatenate(hot, 0).astype(BF16)


def face_flux(picked, flux, spread, insts):
    count = picked.shape[0]
    stacked = jnp.concatenate([picked[:, t * LANE : (t + 1) * LANE] for t in range(insts)], 0)
    wide = jnp.dot(stacked, spread, preferred_element_type=F32)
    normal = []
    for t in range(insts):
        rows = wide[t * count : (t + 1) * count]
        summed = flux[:, 0:LANE] * rows[:, 0:LANE]
        for d in range(1, FIELDS):
            summed += flux[:, d * LANE : (d + 1) * LANE] * rows[:, d * LANE : (d + 1) * LANE]
        normal.append(summed.astype(BF16))
    return normal


def lift_faces(normal, lift, elems):
    rows = [
        jnp.concatenate([n[f * elems : (f + 1) * elems] for f in range(FACES)], 1) for n in normal
    ]
    return jnp.dot(jnp.concatenate(rows, 0), lift, preferred_element_type=F32)


def couple(entry_ref, states, t, shift, insts):
    summed = None
    for s in range(insts):
        d = (t - s + shift * insts) % NI
        term = entry_ref[d : d + 1, :] * states[s].astype(F32)
        summed = term if summed is None else summed + term
    return summed


def rotated(flux):
    place = lax.broadcasted_iota(jnp.int32, (flux.shape[0], LANE), 1) // FPTS
    blocks = []
    for k in range(LANE // FPTS):
        block = jnp.zeros((flux.shape[0], LANE), F32)
        for d in range(FIELDS):
            met = place == (d + k) % (LANE // FPTS)
            block = jnp.where(met, flux[:, d * LANE : (d + 1) * LANE], block)
        blocks.append(block)
    return jnp.concatenate(blocks, 1)


def slot_normal(blocks, factors, insts):
    count = blocks.shape[0]
    stacked = jnp.concatenate([blocks[:, t * LANE : (t + 1) * LANE] for t in range(insts)], 0)
    summed = [None] * insts
    for k in range(LANE // FPTS):
        turned = stacked if k == 0 else pltpu.roll(stacked, k * FPTS, 1)
        for t in range(insts):
            term = factors[:, k * LANE : (k + 1) * LANE] * turned[t * count : (t + 1) * count]
            summed[t] = term if k == 0 else summed[t] + term
    return [rows.astype(BF16) for rows in summed]


def table_kernel(spread_ref, order_ref):
    spread_ref[...] = spread_table()
    order_ref[...] = order_table()


def first_kernel(spectral, second, place_ref, freq_ref, order_ref, state_ref, trace_ref, send_ref, flux_ref, source_ref,
                 flux_out_ref, hot_ref, entry_ref, pool_ref, *out_refs):
    insts, elems, width = state_ref.shape
    state = state_ref[...].reshape(insts * elems, width)
    pool = trace_pool(state, trace_ref[...], insts, elems)
    pool_ref[...] = pool
    fill_outgoing(pool, send_ref[0], out_refs, place_ref[0], elems)
    slots = send_ref.shape[1] * send_ref.shape[2]
    hot_ref[...] = source_table(source_ref[...].T, elems, slots)
    flux_out_ref[...] = flux_order(flux_ref[...], order_ref[...])
    freq = freq_ref[0]
    for d in range(NI):
        entry = freq * float(spectral[d]) - dissipation * float(second[d])
        entry_ref[d : d + 1, :] = jnp.full((1, width), entry, F32)


def base_kernel(state_ref, diag_ref, forcing_ref, entry_ref, prod_out_ref, rest_ref, wide_ref,
                prod_ref):
    insts, elems, width = state_ref.shape
    states = [state_ref[t] for t in range(insts)]
    products = diagonal(states, diag_ref, wide_ref, prod_ref, insts, elems)
    for t in range(insts):
        prod_out_ref[t] = products[t]
        rest_ref[t] = couple(entry_ref, states, t, 0, insts) - forcing_ref[t].astype(F32)


def last_base_kernel(state_ref, pool_ref, diag_ref, forcing_ref, hot_ref, flux_ref, spread_ref,
                     lift_ref, base_ref, factor_ref, wide_ref, prod_ref):
    insts, elems, width = state_ref.shape
    flux = flux_ref[...]
    hot = hot_ref[...]
    faces = hot.shape[0]
    factors = lax.dot_general(hot, flux, (((0,), (0,)), ((), ())), preferred_element_type=F32)
    factor_ref[...] = rotated(factors[faces:])
    empty = jnp.zeros((hot.shape[1] - faces, insts * LANE), BF16)
    pool = jnp.concatenate([pool_ref[...], empty], 0)
    picked = jnp.dot(hot, pool, preferred_element_type=F32).astype(BF16)
    normal = face_flux(picked, flux.astype(F32), spread_ref[...], insts)
    lifted = lift_faces(normal, lift_ref[...], elems)
    states = [state_ref[t].astype(BF16) for t in range(insts)]
    products = diagonal(states, diag_ref, wide_ref, prod_ref, insts, elems)
    for t in range(insts):
        base_ref[t] = (
            products[t] + lifted[t * elems : (t + 1) * elems] - forcing_ref[t].astype(F32)
        )


def message_kernel(ranks, partial_ref, first_ref, base_ref, entry_ref, *refs):
    message_refs, (state_ref, out_ref) = refs[: ranks - 1], refs[ranks - 1 :]
    insts, elems, width = base_ref.shape
    firsts = [[first_ref[t] for t in range(insts)]]
    partials = [[partial_ref[t] for t in range(insts)]]
    spatial = [None]
    for message_ref in message_refs:
        rows = [
            message_ref[i * elems : (i + 1) * elems, 0:width] for i in range(3 * insts)
        ]
        firsts.append(rows[:insts])
        partials.append(rows[insts : 2 * insts])
        spatial.append(rows[2 * insts :])
    states = []
    for k in range(ranks):
        of_rank = []
        for t in range(insts):
            state = partials[k][t].astype(F32)
            for j in range(ranks):
                if j != k:
                    state -= pseudo_step * couple(entry_ref, firsts[j], t, k - j, insts)
            of_rank.append(state.astype(BF16))
        states.append(of_rank)
    for t in range(insts):
        state_ref[t] = states[0][t]
        coupling = couple(entry_ref, states[0], t, 0, insts)
        missing = jnp.zeros((elems, width), F32)
        for k in range(1, ranks):
            coupling += couple(entry_ref, states[k], t, -k, insts)
            missing += couple(entry_ref, spatial[k], t, -k, insts)
        out_ref[t] = base_ref[t] + coupling.astype(BF16).astype(F32) - pseudo_step * missing


def received(parts, place, got_refs, order):
    got_refs = {swap: got_refs[i] for i, swap in enumerate(order)}
    arrived = by_offset(
        place, [got_refs[swap][...].astype(F32) for swap in range(len(OFFSETS))]
    )
    for k, offset in enumerate(OFFSETS):
        exists = (place + offset >= 0) & (place + offset < parts)
        arrived[k] = jnp.where(exists, arrived[k], jnp.zeros_like(arrived[k]))
    return jnp.concatenate(arrived, 0)


def step_kernel(parts, place_ref, spread_ref, *refs):
    got_refs, refs = refs[: len(OFFSETS)], refs[len(OFFSETS) :]
    (state_ref, pool_ref, prod_ref, rest_ref, hot_ref, flux_ref, lift_ref, trace_ref, send_ref,
     partial_ref, message_ref, next_pool_ref, *out_refs) = refs
    insts, elems, width = state_ref.shape
    place = place_ref[0]
    blocks = received(parts, place, got_refs, FIRST_ORDER).astype(BF16)
    pool = jnp.concatenate([pool_ref[...], blocks], 0)
    picked = jnp.dot(hot_ref[...], pool, preferred_element_type=F32).astype(BF16)
    normal = face_flux(picked, flux_ref[...].astype(F32), spread_ref[...], insts)
    lifted = lift_faces(normal, lift_ref[...], elems)
    message_ref[...] = jnp.zeros_like(message_ref)
    fresh = []
    for t in range(insts):
        spatial = prod_ref[t] + lifted[t * elems : (t + 1) * elems]
        moved = state_ref[t].astype(F32) - pseudo_step * (spatial + rest_ref[t])
        partial_ref[t] = moved
        fresh.append(moved.astype(BF16))
        for i, block in enumerate((state_ref[t], fresh[t], spatial.astype(BF16))):
            low = (i * insts + t) * elems
            message_ref[low : low + elems, 0:width] = block
    pool = trace_pool(jnp.concatenate(fresh, 0), trace_ref[...], insts, elems)
    next_pool_ref[...] = pool
    fill_outgoing(pool, send_ref[0], out_refs, place, elems)


def last_kernel(parts, place_ref, *refs):
    got_refs, refs = refs[: len(OFFSETS)], refs[len(OFFSETS) :]
    (state_ref, base_ref, hot_ref, factor_ref, lift_ref, final_hbm, residual_hbm,
     final_ref, residual_ref, sems) = refs
    insts, elems, width = state_ref.shape
    blocks = received(parts, place_ref[0], got_refs, LAST_ORDER)
    normal = slot_normal(blocks, factor_ref[...], insts)
    empty = jnp.zeros((FACES * elems, insts * LANE), BF16)
    rows = jnp.concatenate([empty, jnp.concatenate(normal, 1)], 0)
    spots = jnp.dot(hot_ref[...], rows, preferred_element_type=F32).astype(BF16)
    lifted = lift_faces(
        [spots[:, t * LANE : (t + 1) * LANE] for t in range(insts)], lift_ref[...], elems
    )
    copies = []
    for t in range(insts):
        residual = base_ref[t] + lifted[t * elems : (t + 1) * elems]
        residual_ref[t] = residual
        final_ref[t] = (state_ref[t].astype(F32) - pseudo_step * residual).astype(BF16)
        copies += [
            pltpu.make_async_copy(residual_ref.at[t], residual_hbm.at[t], sems.at[0, t]),
            pltpu.make_async_copy(final_ref.at[t], final_hbm.at[t], sems.at[1, t]),
        ]
        copies[-2].start()
        copies[-1].start()
    for copy in copies:
        copy.wait()


def on_device(
    initial_state, forcing, diagonal_blocks, flux_jacobian, send_list, source_index, frequency
):
    insts, elems, width = initial_state.shape
    parts = lax.axis_size("dom")
    ranks = lax.axis_size("inst")
    slots, capacity = send_list.shape[1:]
    faces = FACES * elems
    trace_np, lift_np, spectral, second = wide_tables()
    trace_wide = jnp.asarray(trace_np, BF16)
    lift_wide = jnp.asarray(lift_np, BF16)
    place = lax.axis_index("dom").reshape(1)
    sources = source_index.T
    routes = swap_routes(ranks, parts)

    smem = pl.BlockSpec(memory_space=pltpu.SMEM)
    vmem = pl.BlockSpec(memory_space=pltpu.VMEM)
    params = pltpu.CompilerParams(vmem_limit_bytes=VMEM_LIMIT)

    def like(array):
        return jax.ShapeDtypeStruct(array.shape, array.dtype)

    wide_shape = jax.ShapeDtypeStruct(initial_state.shape, F32)
    pool_shape = jax.ShapeDtypeStruct((faces, insts * LANE), BF16)
    out_shapes = [jax.ShapeDtypeStruct((capacity, insts * LANE), BF16)] * slots
    flux_shape = jax.ShapeDtypeStruct((faces, FIELDS * LANE), BF16)
    hot_shape = jax.ShapeDtypeStruct((faces, faces + slots * capacity), BF16)
    factor_shape = jax.ShapeDtypeStruct((slots * capacity, LANE // FPTS * LANE), F32)

    def exchange(outgoing, order):
        return [
            lax.ppermute(outgoing[swap], ("inst", "dom"), routes[swap]) for swap in order
        ]

    entry_shape = jax.ShapeDtypeStruct((NI, width), F32)
    message_shape = jax.ShapeDtypeStruct((3 * insts * elems, pl.cdiv(width, LANE) * LANE), BF16)
    chunks = [pltpu.VMEM((pl.cdiv(width, LANE) * insts * elems, LANE), F32)] * 2
    diag_cost = pl.CostEstimate(
        flops=2 * insts * diagonal_blocks.size, bytes_accessed=2 * diagonal_blocks.size,
        transcendentals=0,
    )
    spread, order = pl.pallas_call(
        table_kernel,
        out_shape=[
            jax.ShapeDtypeStruct((LANE, FIELDS * LANE), BF16),
            jax.ShapeDtypeStruct((FIELDS * FIELDS * FPTS, FIELDS * LANE), BF16),
        ],
        out_specs=[vmem] * 2,
        compiler_params=params,
        cost_estimate=pl.CostEstimate(flops=10**10, bytes_accessed=10**6, transcendentals=0),
        name="tables",
    )()
    freq, _ = lax.optimization_barrier((frequency, spread))
    flux, hot, entries, pool, *outgoing = pl.pallas_call(
        functools.partial(first_kernel, spectral, second),
        out_shape=[flux_shape, hot_shape, entry_shape, pool_shape] + out_shapes,
        in_specs=[smem] * 2 + [vmem] * 6,
        out_specs=[vmem] * (4 + len(out_shapes)),
        compiler_params=params,
        cost_estimate=pl.CostEstimate(flops=10**10, bytes_accessed=10**6, transcendentals=0),
        name="first_traces",
    )(place, freq, order, initial_state, trace_wide, send_list, flux_jacobian, sources)
    got = exchange(outgoing, FIRST_ORDER)
    product, rest = pl.pallas_call(
        base_kernel,
        out_shape=[wide_shape] * 2,
        in_specs=[vmem] * 4,
        out_specs=[vmem] * 2,
        scratch_shapes=chunks,
        compiler_params=params,
        cost_estimate=diag_cost,
        name="own_terms",
    )(initial_state, diagonal_blocks, forcing, entries)
    partial, message, pool, *outgoing = pl.pallas_call(
        functools.partial(step_kernel, parts),
        out_shape=[wide_shape, message_shape, pool_shape] + out_shapes,
        in_specs=[smem] + [vmem] * (slots + 10),
        out_specs=[vmem] * (3 + len(out_shapes)),
        compiler_params=params,
        name="first_step",
    )(place, spread, *got, initial_state, pool, product, rest, hot, flux, lift_wide, trace_wide,
      send_list)
    messages = [
        lax.ppermute(message, "inst", [((i + rank) % ranks, i) for i in range(ranks)])
        for rank in range(1, ranks)
    ]
    got = exchange(outgoing, LAST_ORDER)
    base, factors = pl.pallas_call(
        last_base_kernel,
        out_shape=[wide_shape, factor_shape],
        in_specs=[vmem] * 8,
        out_specs=[vmem] * 2,
        scratch_shapes=chunks,
        compiler_params=params,
        cost_estimate=diag_cost,
        name="last_own_terms",
    )(partial, pool, diagonal_blocks, forcing, hot, flux, spread, lift_wide)
    state, base = pl.pallas_call(
        functools.partial(message_kernel, ranks),
        out_shape=[like(initial_state), wide_shape],
        in_specs=[vmem] * (ranks + 3),
        out_specs=[vmem] * 2,
        compiler_params=params,
        name="message_terms",
    )(partial, initial_state, base, entries, *messages)
    return pl.pallas_call(
        functools.partial(last_kernel, parts),
        out_shape=[like(initial_state), wide_shape],
        in_specs=[smem] + [vmem] * (slots + 5),
        out_specs=[pl.BlockSpec(memory_space=pl.ANY)] * 2,
        scratch_shapes=[
            pltpu.VMEM(initial_state.shape, BF16),
            pltpu.VMEM(initial_state.shape, F32),
            pltpu.SemaphoreType.DMA((2, insts)),
        ],
        compiler_params=params,
        name="last_step",
    )(place, *got, state, base, hot, factors, lift_wide)


def solution(mesh):
    return jax.shard_map(
        on_device,
        mesh=mesh,
        in_specs=(
            P("inst", "dom", None),
            P("inst", "dom", None),
            P("dom", None, None),
            P("dom", None),
            P("dom", None, None),
            P("dom", None),
            P(),
        ),
        out_specs=(P("inst", "dom", None), P("inst", "dom", None)),
        check_vma=False,
    )
```

```python
import functools
import math

import jax
import jax.numpy as jnp
import numpy as np
from jax import lax
from jax.experimental import pallas as pl
from jax.experimental.pallas import tpu as pltpu
from jax.sharding import PartitionSpec as P

FIELDS = 5
ORDER = 3
NODES = 64
FPTS = 16
NI = 8
REACH = 2
ITERS = 2


pseudo_step = 0.5
dissipation = 0.25


def gauss_legendre(count):
    points = []
    weights = []
    for i in range(count):
        where = math.cos(math.pi * (i + 0.75) / (count + 0.5))
        for sweep in range(100):
            before = 1.0
            value = where
            for j in range(2, count + 1):
                after = ((2 * j - 1) * where * value - (j - 1) * before) / j
                before = value
                value = after
            slope = count * (where * value - before) / (where * where - 1.0)
            where = where - value / slope
        before = 1.0
        value = where
        for j in range(2, count + 1):
            after = ((2 * j - 1) * where * value - (j - 1) * before) / j
            before = value
            value = after
        slope = count * (where * value - before) / (where * where - 1.0)
        points.append(where)
        weights.append(2.0 / ((1.0 - where * where) * slope * slope))
    return (np.array(points[::-1]), np.array(weights[::-1]))


def lagrange_at(points, where):
    values = np.ones(points.shape[0])
    for i in range(points.shape[0]):
        for j in range(points.shape[0]):
            if j != i:
                values[i] = values[i] * (where - points[j]) / (points[i] - points[j])
    return values


def tables(order, count):
    points, weights = gauss_legendre(order + 1)
    at_minus = lagrange_at(points, -1.0)
    at_plus = lagrange_at(points, 1.0)
    per_side = order + 1
    node_count = per_side**3
    face_points = per_side**2
    trace_table = np.zeros((node_count, 6 * face_points))
    lift_table = np.zeros((node_count, 6 * face_points))
    for k in range(per_side):
        for j in range(per_side):
            for i in range(per_side):
                node = i + per_side * j + per_side * per_side * k
                entries = [
                    (0, at_minus[i], j + per_side * k, weights[i]),
                    (1, at_plus[i], j + per_side * k, weights[i]),
                    (2, at_minus[j], i + per_side * k, weights[j]),
                    (3, at_plus[j], i + per_side * k, weights[j]),
                    (4, at_minus[k], i + per_side * j, weights[k]),
                    (5, at_plus[k], i + per_side * j, weights[k]),
                ]
                for face_index, factor, point, weight in entries:
                    trace_table[node, face_index * face_points + point] = factor
                    lift_table[node, face_index * face_points + point] = factor / weight
    spectral = np.zeros((count, count))
    second = np.zeros((count, count))
    for t in range(count):
        for s in range(count):
            if t != s:
                spectral[t, s] = 0.5 * (-1.0) ** (t - s + 1) / math.tan(math.pi * (t - s) / count)
                second[t, s] = -0.5 * (-1.0) ** (t - s) / math.sin(math.pi * (t - s) / count) ** 2
            else:
                second[t, s] = -(count * count + 2.0) / 12.0
    return (trace_table, lift_table, spectral, second)


LANE = 128
WIDE = FIELDS * NODES
FACES = 6
VMEM_LIMIT = 16 * 1024 * 1024
BF16 = jnp.bfloat16
F32 = jnp.float32
OFFSETS = list(range(-REACH, 0)) + list(range(1, REACH + 1))
FIRST_ORDER = (3, 1, 2, 0)
LAST_ORDER = (2, 1, 3, 0)


def wide_tables():
    trace_np, lift_np, spectral_np, second_np = tables(ORDER, NI)
    trace_wide = np.zeros((WIDE, FACES * LANE))
    lift_wide = np.zeros((FACES * LANE, WIDE))
    for c in range(FIELDS):
        rows = slice(c * NODES, (c + 1) * NODES)
        for f in range(FACES):
            cols = slice(f * LANE + c * FPTS, f * LANE + (c + 1) * FPTS)
            face = slice(f * FPTS, (f + 1) * FPTS)
            trace_wide[rows, cols] = trace_np[:, face]
            lift_wide[cols, rows] = lift_np[:, face].T
    return trace_wide, lift_wide, spectral_np[:, 0], second_np[:, 0]


def iotas(shape):
    return [lax.broadcasted_iota(jnp.int32, shape, axis) for axis in range(2)]


def one_hot(mask):
    return jnp.where(mask, 1.0, 0.0).astype(BF16)


def spread_table():
    row, col = iotas((LANE, FIELDS * LANE))
    inside = col % LANE < FIELDS * FPTS
    return one_hot(inside & (row == col // LANE * FPTS + col % FPTS))


def order_table():
    row, col = iotas((FIELDS * FIELDS * FPTS, FIELDS * LANE))
    place = col % LANE
    source = place // FPTS * FIELDS * FPTS + col // LANE * FPTS + col % FPTS
    return one_hot((place < FIELDS * FPTS) & (row == source))


def trace_pool(state, trace_wide, insts, elems):
    wide = jnp.dot(state, trace_wide, preferred_element_type=F32).astype(BF16)
    by_inst = []
    for t in range(insts):
        rows = wide[t * elems : (t + 1) * elems]
        by_inst.append(
            jnp.concatenate([rows[:, f * LANE : (f + 1) * LANE] for f in range(FACES)], 0)
        )
    return jnp.concatenate(by_inst, 1)


def swap_routes(ranks, parts):
    near = [[(p, p + 1) for p in range(first, parts - 1, 2)] for first in range(2)]
    far = [
        [(p + i, p + i + 2) for p in range(first, parts - 3, 4) for i in range(2)]
        for first in (0, 2)
    ]
    routes = []
    for pairs in near + far:
        met = {p for pair in pairs for p in pair}
        alone = [p for p in range(parts) if p not in met]
        idle = [(p, p + 1) for p in alone if p + 1 in alone]
        alone = [p for p in alone if p + 1 not in alone and p - 1 not in alone]
        swaps = [(r * parts + p, r * parts + q) for r in range(ranks) for p, q in pairs + idle]
        swaps += [(r * parts + p, (r ^ 1) * parts + p) for r in range(0, ranks, 2) for p in alone]
        routes.append(swaps + [(q, p) for p, q in swaps])
    return routes


def by_swap(place, by_offset):
    two_down, one_down, one_up, two_up = by_offset
    even = place % 2 == 0
    low = place // 2 % 2 == 0
    return [
        jnp.where(even, one_up, one_down),
        jnp.where(even, one_down, one_up),
        jnp.where(low, two_up, two_down),
        jnp.where(low, two_down, two_up),
    ]


def by_offset(place, blocks):
    even = place % 2 == 0
    low = place // 2 % 2 == 0
    return [
        jnp.where(low, blocks[3], blocks[2]),
        jnp.where(even, blocks[1], blocks[0]),
        jnp.where(even, blocks[0], blocks[1]),
        jnp.where(low, blocks[2], blocks[3]),
    ]


def fill_outgoing(pool, send, out_refs, place, elems):
    slots, capacity = send.shape
    rows, cols = iotas((FACES * elems, slots * capacity))
    ids = FACES * (rows % elems) + rows // elems
    wanted = jnp.concatenate([send[k : k + 1] for k in range(slots)], 1)
    out = lax.dot_general(
        one_hot(ids == wanted), pool, (((0,), (0,)), ((), ())), preferred_element_type=F32
    )
    blocks = by_swap(place, [out[k * capacity : (k + 1) * capacity] for k in range(slots)])
    for block, ref in zip(blocks, out_refs):
        ref[...] = block.astype(BF16)


def diagonal(states, diag, wide_ref, prod_ref, insts, elems):
    tall = insts * elems
    width = diag.shape[1]
    cuts = [(j, j * LANE, min((j + 1) * LANE, width)) for j in range(pl.cdiv(width, LANE))]
    for t in range(insts):
        rows = states[t].astype(F32)
        for j, low, high in cuts:
            first = j * tall + t * elems
            wide_ref[first : first + elems, 0 : high - low] = rows[:, low:high]
    for e in range(elems):
        rows = jnp.concatenate(
            [wide_ref[pl.ds(j * tall + e, insts, stride=elems), :] for j, low, high in cuts], 1
        )
        product = jnp.dot(rows[:, 0:width].astype(BF16), diag[e], preferred_element_type=F32)
        for j, low, high in cuts:
            chunk = product[:, low:high]
            if high - low < LANE:
                chunk = jnp.concatenate([chunk, jnp.zeros((insts, LANE - high + low), F32)], 1)
            prod_ref[pl.ds(j * tall + e, insts, stride=elems), :] = chunk
    return [
        jnp.concatenate(
            [
                prod_ref[j * tall + t * elems : j * tall + (t + 1) * elems, 0 : high - low]
                for j, low, high in cuts
            ],
            1,
        )
        for t in range(insts)
    ]


def flux_order(rows, order):
    per_face = FIELDS * FIELDS * FPTS
    by_face = jnp.concatenate(
        [rows[:, f * per_face : (f + 1) * per_face] for f in range(FACES)], 0
    )
    return jnp.dot(by_face, order, preferred_element_type=F32).astype(BF16)


def source_table(sources, elems, slots):
    faces = FACES * elems
    columns = lax.broadcasted_iota(jnp.int32, (elems, faces + slots), 1)
    ids = jnp.where(columns < faces, FACES * (columns % elems) + columns // elems, columns)
    hot = [jnp.where(sources[:, f : f + 1] == ids, 1.0, 0.0) for f in range(FACES)]
    return jnp.concatenate(hot, 0).astype(BF16)


def face_flux(picked, flux, spread, insts):
    count = picked.shape[0]
    stacked = jnp.concatenate([picked[:, t * LANE : (t + 1) * LANE] for t in range(insts)], 0)
    wide = jnp.dot(stacked, spread, preferred_element_type=F32)
    normal = []
    for t in range(insts):
        rows = wide[t * count : (t + 1) * count]
        summed = flux[:, 0:LANE] * rows[:, 0:LANE]
        for d in range(1, FIELDS):
            summed += flux[:, d * LANE : (d + 1) * LANE] * rows[:, d * LANE : (d + 1) * LANE]
        normal.append(summed.astype(BF16))
    return normal


def lift_faces(normal, lift, elems):
    rows = [
        jnp.concatenate([n[f * elems : (f + 1) * elems] for f in range(FACES)], 1) for n in normal
    ]
    return jnp.dot(jnp.concatenate(rows, 0), lift, preferred_element_type=F32)


def couple(entry_ref, states, t, shift, insts):
    summed = None
    for s in range(insts):
        d = (t - s + shift * insts) % NI
        term = entry_ref[d : d + 1, :] * states[s].astype(F32)
        summed = term if summed is None else summed + term
    return summed


def rotated(flux):
    place = lax.broadcasted_iota(jnp.int32, (flux.shape[0], LANE), 1) // FPTS
    blocks = []
    for k in range(LANE // FPTS):
        block = jnp.zeros((flux.shape[0], LANE), F32)
        for d in range(FIELDS):
            met = place == (d + k) % (LANE // FPTS)
            block = jnp.where(met, flux[:, d * LANE : (d + 1) * LANE], block)
        blocks.append(block)
    return jnp.concatenate(blocks, 1)


def slot_normal(blocks, factors, insts):
    count = blocks.shape[0]
    stacked = jnp.concatenate([blocks[:, t * LANE : (t + 1) * LANE] for t in range(insts)], 0)
    summed = [None] * insts
    for k in range(LANE // FPTS):
        turned = stacked if k == 0 else pltpu.roll(stacked, k * FPTS, 1)
        for t in range(insts):
            term = factors[:, k * LANE : (k + 1) * LANE] * turned[t * count : (t + 1) * count]
            summed[t] = term if k == 0 else summed[t] + term
    return [rows.astype(BF16) for rows in summed]


def table_kernel(spread_ref, order_ref):
    spread_ref[...] = spread_table()
    order_ref[...] = order_table()


def first_kernel(spectral, second, place_ref, freq_ref, spread_ref, state_ref, trace_ref, send_ref,
                 entry_ref, pool_ref, *out_refs):
    insts, elems, width = state_ref.shape
    state = state_ref[...].reshape(insts * elems, width)
    pool = trace_pool(state, trace_ref[...], insts, elems)
    pool_ref[...] = pool
    fill_outgoing(pool, send_ref[0], out_refs, place_ref[0], elems)
    freq = freq_ref[0]
    for d in range(NI):
        entry = freq * float(spectral[d]) - dissipation * float(second[d])
        entry_ref[d : d + 1, :] = jnp.full((1, width), entry, F32)


def base_kernel(slots, state_ref, diag_ref, forcing_ref, entry_ref, flux_ref, source_ref, order_ref,
                prod_out_ref, rest_ref, flux_out_ref, hot_ref, wide_ref, prod_ref):
    insts, elems, width = state_ref.shape
    hot_ref[...] = source_table(source_ref[...].T, elems, slots)
    flux_out_ref[...] = flux_order(flux_ref[...], order_ref[...])
    states = [state_ref[t] for t in range(insts)]
    products = diagonal(states, diag_ref, wide_ref, prod_ref, insts, elems)
    for t in range(insts):
        prod_out_ref[t] = products[t]
        rest_ref[t] = couple(entry_ref, states, t, 0, insts) - forcing_ref[t].astype(F32)


def last_base_kernel(state_ref, pool_ref, diag_ref, forcing_ref, hot_ref, flux_ref, spread_ref,
                     lift_ref, base_ref, factor_ref, wide_ref, prod_ref):
    insts, elems, width = state_ref.shape
    flux = flux_ref[...]
    hot = hot_ref[...]
    faces = hot.shape[0]
    factors = lax.dot_general(hot, flux, (((0,), (0,)), ((), ())), preferred_element_type=F32)
    factor_ref[...] = rotated(factors[faces:])
    empty = jnp.zeros((hot.shape[1] - faces, insts * LANE), BF16)
    pool = jnp.concatenate([pool_ref[...], empty], 0)
    picked = jnp.dot(hot, pool, preferred_element_type=F32).astype(BF16)
    normal = face_flux(picked, flux.astype(F32), spread_ref[...], insts)
    lifted = lift_faces(normal, lift_ref[...], elems)
    states = [state_ref[t].astype(BF16) for t in range(insts)]
    products = diagonal(states, diag_ref, wide_ref, prod_ref, insts, elems)
    for t in range(insts):
        base_ref[t] = (
            products[t] + lifted[t * elems : (t + 1) * elems] - forcing_ref[t].astype(F32)
        )


def message_kernel(ranks, partial_ref, first_ref, base_ref, entry_ref, *refs):
    message_refs, (state_ref, out_ref) = refs[: ranks - 1], refs[ranks - 1 :]
    insts, elems, width = base_ref.shape
    firsts = [[first_ref[t] for t in range(insts)]]
    partials = [[partial_ref[t] for t in range(insts)]]
    for message_ref in message_refs:
        rows = [
            message_ref[i * elems : (i + 1) * elems, 0:width] for i in range(2 * insts)
        ]
        firsts.append(rows[:insts])
        partials.append(rows[insts:])
    states = []
    for k in range(ranks):
        of_rank = []
        for t in range(insts):
            state = partials[k][t].astype(F32)
            for j in range(ranks):
                if j != k:
                    state -= pseudo_step * couple(entry_ref, firsts[j], t, k - j, insts)
            of_rank.append(state.astype(BF16) if k == 0 else state)
        states.append(of_rank)
    for t in range(insts):
        state_ref[t] = states[0][t]
        coupling = base_ref[t]
        for k in range(ranks):
            coupling += couple(entry_ref, states[k], t, -k, insts)
        out_ref[t] = coupling


def received(parts, place, got_refs, order):
    got_refs = {swap: got_refs[i] for i, swap in enumerate(order)}
    arrived = by_offset(
        place, [got_refs[swap][...].astype(F32) for swap in range(len(OFFSETS))]
    )
    for k, offset in enumerate(OFFSETS):
        exists = (place + offset >= 0) & (place + offset < parts)
        arrived[k] = jnp.where(exists, arrived[k], jnp.zeros_like(arrived[k]))
    return jnp.concatenate(arrived, 0)


def step_kernel(parts, place_ref, spread_ref, *refs):
    got_refs, refs = refs[: len(OFFSETS)], refs[len(OFFSETS) :]
    (state_ref, pool_ref, prod_ref, rest_ref, hot_ref, flux_ref, lift_ref, trace_ref, send_ref,
     partial_ref, message_ref, next_pool_ref, *out_refs) = refs
    insts, elems, width = state_ref.shape
    place = place_ref[0]
    blocks = received(parts, place, got_refs, FIRST_ORDER).astype(BF16)
    pool = jnp.concatenate([pool_ref[...], blocks], 0)
    picked = jnp.dot(hot_ref[...], pool, preferred_element_type=F32).astype(BF16)
    normal = face_flux(picked, flux_ref[...].astype(F32), spread_ref[...], insts)
    lifted = lift_faces(normal, lift_ref[...], elems)
    message_ref[...] = jnp.zeros_like(message_ref)
    fresh = []
    for t in range(insts):
        spatial = prod_ref[t] + lifted[t * elems : (t + 1) * elems]
        moved = state_ref[t].astype(F32) - pseudo_step * (spatial + rest_ref[t])
        partial_ref[t] = moved
        fresh.append(moved.astype(BF16))
        lean = (moved - pseudo_step * spatial).astype(BF16)
        for i, block in enumerate((state_ref[t], lean)):
            low = (i * insts + t) * elems
            message_ref[low : low + elems, 0:width] = block
    pool = trace_pool(jnp.concatenate(fresh, 0), trace_ref[...], insts, elems)
    next_pool_ref[...] = pool
    fill_outgoing(pool, send_ref[0], out_refs, place, elems)


def last_kernel(parts, place_ref, *refs):
    got_refs, refs = refs[: len(OFFSETS)], refs[len(OFFSETS) :]
    (state_ref, base_ref, hot_ref, factor_ref, lift_ref, final_hbm, residual_hbm,
     final_ref, residual_ref, sems) = refs
    insts, elems, width = state_ref.shape
    blocks = received(parts, place_ref[0], got_refs, LAST_ORDER)
    normal = slot_normal(blocks, factor_ref[...], insts)
    empty = jnp.zeros((FACES * elems, insts * LANE), BF16)
    rows = jnp.concatenate([empty, jnp.concatenate(normal, 1)], 0)
    spots = jnp.dot(hot_ref[...], rows, preferred_element_type=F32).astype(BF16)
    lifted = lift_faces(
        [spots[:, t * LANE : (t + 1) * LANE] for t in range(insts)], lift_ref[...], elems
    )
    copies = []
    for t in range(insts):
        residual = base_ref[t] + lifted[t * elems : (t + 1) * elems]
        residual_ref[t] = residual
        final_ref[t] = (state_ref[t].astype(F32) - pseudo_step * residual).astype(BF16)
        copies += [
            pltpu.make_async_copy(residual_ref.at[t], residual_hbm.at[t], sems.at[0, t]),
            pltpu.make_async_copy(final_ref.at[t], final_hbm.at[t], sems.at[1, t]),
        ]
        copies[-2].start()
        copies[-1].start()
    for copy in copies:
        copy.wait()


def on_device(
    initial_state, forcing, diagonal_blocks, flux_jacobian, send_list, source_index, frequency
):
    insts, elems, width = initial_state.shape
    parts = lax.axis_size("dom")
    ranks = lax.axis_size("inst")
    slots, capacity = send_list.shape[1:]
    faces = FACES * elems
    trace_np, lift_np, spectral, second = wide_tables()
    trace_wide = jnp.asarray(trace_np, BF16)
    lift_wide = jnp.asarray(lift_np, BF16)
    place = lax.axis_index("dom").reshape(1)
    sources = source_index.T
    routes = swap_routes(ranks, parts)

    smem = pl.BlockSpec(memory_space=pltpu.SMEM)
    vmem = pl.BlockSpec(memory_space=pltpu.VMEM)
    params = pltpu.CompilerParams(vmem_limit_bytes=VMEM_LIMIT)

    def like(array):
        return jax.ShapeDtypeStruct(array.shape, array.dtype)

    wide_shape = jax.ShapeDtypeStruct(initial_state.shape, F32)
    pool_shape = jax.ShapeDtypeStruct((faces, insts * LANE), BF16)
    out_shapes = [jax.ShapeDtypeStruct((capacity, insts * LANE), BF16)] * slots
    flux_shape = jax.ShapeDtypeStruct((faces, FIELDS * LANE), BF16)
    hot_shape = jax.ShapeDtypeStruct((faces, faces + slots * capacity), BF16)
    factor_shape = jax.ShapeDtypeStruct((slots * capacity, LANE // FPTS * LANE), F32)

    def exchange(outgoing, order):
        return [
            lax.ppermute(outgoing[swap], ("inst", "dom"), routes[swap]) for swap in order
        ]

    entry_shape = jax.ShapeDtypeStruct((NI, width), F32)
    message_shape = jax.ShapeDtypeStruct((2 * insts * elems, pl.cdiv(width, LANE) * LANE), BF16)
    chunks = [pltpu.VMEM((pl.cdiv(width, LANE) * insts * elems, LANE), F32)] * 2
    diag_cost = pl.CostEstimate(
        flops=2 * insts * diagonal_blocks.size, bytes_accessed=2 * diagonal_blocks.size,
        transcendentals=0,
    )
    spread, order = pl.pallas_call(
        table_kernel,
        out_shape=[
            jax.ShapeDtypeStruct((LANE, FIELDS * LANE), BF16),
            jax.ShapeDtypeStruct((FIELDS * FIELDS * FPTS, FIELDS * LANE), BF16),
        ],
        out_specs=[vmem] * 2,
        compiler_params=params,
        cost_estimate=pl.CostEstimate(flops=10**10, bytes_accessed=10**6, transcendentals=0),
        name="tables",
    )()
    freq, _ = lax.optimization_barrier((frequency, spread))
    entries, pool, *outgoing = pl.pallas_call(
        functools.partial(first_kernel, spectral, second),
        out_shape=[entry_shape, pool_shape] + out_shapes,
        in_specs=[smem] * 2 + [vmem] * 4,
        out_specs=[vmem] * (2 + len(out_shapes)),
        compiler_params=params,
        cost_estimate=pl.CostEstimate(flops=10**10, bytes_accessed=10**6, transcendentals=0),
        name="first_traces",
    )(place, freq, spread, initial_state, trace_wide, send_list)
    got = exchange(outgoing, FIRST_ORDER)
    product, rest, flux, hot = pl.pallas_call(
        functools.partial(base_kernel, slots * capacity),
        out_shape=[wide_shape] * 2 + [flux_shape, hot_shape],
        in_specs=[vmem] * 7,
        out_specs=[vmem] * 4,
        scratch_shapes=chunks,
        compiler_params=params,
        cost_estimate=diag_cost,
        name="own_terms",
    )(initial_state, diagonal_blocks, forcing, entries, flux_jacobian, sources, order)
    partial, message, pool, *outgoing = pl.pallas_call(
        functools.partial(step_kernel, parts),
        out_shape=[wide_shape, message_shape, pool_shape] + out_shapes,
        in_specs=[smem] + [vmem] * (slots + 10),
        out_specs=[vmem] * (3 + len(out_shapes)),
        compiler_params=params,
        name="first_step",
    )(place, spread, *got, initial_state, pool, product, rest, hot, flux, lift_wide, trace_wide,
      send_list)
    messages = [
        lax.ppermute(message, "inst", [((i + rank) % ranks, i) for i in range(ranks)])
        for rank in range(1, ranks)
    ]
    got = exchange(outgoing, LAST_ORDER)
    base, factors = pl.pallas_call(
        last_base_kernel,
        out_shape=[wide_shape, factor_shape],
        in_specs=[vmem] * 8,
        out_specs=[vmem] * 2,
        scratch_shapes=chunks,
        compiler_params=params,
        cost_estimate=diag_cost,
        name="last_own_terms",
    )(partial, pool, diagonal_blocks, forcing, hot, flux, spread, lift_wide)
    state, base = pl.pallas_call(
        functools.partial(message_kernel, ranks),
        out_shape=[like(initial_state), wide_shape],
        in_specs=[vmem] * (ranks + 3),
        out_specs=[vmem] * 2,
        compiler_params=params,
        name="message_terms",
    )(partial, initial_state, base, entries, *messages)
    return pl.pallas_call(
        functools.partial(last_kernel, parts),
        out_shape=[like(initial_state), wide_shape],
        in_specs=[smem] + [vmem] * (slots + 5),
        out_specs=[pl.BlockSpec(memory_space=pl.ANY)] * 2,
        scratch_shapes=[
            pltpu.VMEM(initial_state.shape, BF16),
            pltpu.VMEM(initial_state.shape, F32),
            pltpu.SemaphoreType.DMA((2, insts)),
        ],
        compiler_params=params,
        name="last_step",
    )(place, *got, state, base, hot, factors, lift_wide)


def solution(mesh):
    return jax.shard_map(
        on_device,
        mesh=mesh,
        in_specs=(
            P("inst", "dom", None),
            P("inst", "dom", None),
            P("dom", None, None),
            P("dom", None),
            P("dom", None, None),
            P("dom", None),
            P(),
        ),
        out_specs=(P("inst", "dom", None), P("inst", "dom", None)),
        check_vma=False,
    )
```

```python
import functools
import math

import jax
import jax.numpy as jnp
import numpy as np
from jax import lax
from jax.experimental import pallas as pl
from jax.experimental.pallas import tpu as pltpu
from jax.sharding import PartitionSpec as P

FIELDS = 5
ORDER = 3
NODES = 64
FPTS = 16
NI = 8
REACH = 2
ITERS = 2


pseudo_step = 0.5
dissipation = 0.25


def gauss_legendre(count):
    points = []
    weights = []
    for i in range(count):
        where = math.cos(math.pi * (i + 0.75) / (count + 0.5))
        for sweep in range(100):
            before = 1.0
            value = where
            for j in range(2, count + 1):
                after = ((2 * j - 1) * where * value - (j - 1) * before) / j
                before = value
                value = after
            slope = count * (where * value - before) / (where * where - 1.0)
            where = where - value / slope
        before = 1.0
        value = where
        for j in range(2, count + 1):
            after = ((2 * j - 1) * where * value - (j - 1) * before) / j
            before = value
            value = after
        slope = count * (where * value - before) / (where * where - 1.0)
        points.append(where)
        weights.append(2.0 / ((1.0 - where * where) * slope * slope))
    return (np.array(points[::-1]), np.array(weights[::-1]))


def lagrange_at(points, where):
    values = np.ones(points.shape[0])
    for i in range(points.shape[0]):
        for j in range(points.shape[0]):
            if j != i:
                values[i] = values[i] * (where - points[j]) / (points[i] - points[j])
    return values


def tables(order, count):
    points, weights = gauss_legendre(order + 1)
    at_minus = lagrange_at(points, -1.0)
    at_plus = lagrange_at(points, 1.0)
    per_side = order + 1
    node_count = per_side**3
    face_points = per_side**2
    trace_table = np.zeros((node_count, 6 * face_points))
    lift_table = np.zeros((node_count, 6 * face_points))
    for k in range(per_side):
        for j in range(per_side):
            for i in range(per_side):
                node = i + per_side * j + per_side * per_side * k
                entries = [
                    (0, at_minus[i], j + per_side * k, weights[i]),
                    (1, at_plus[i], j + per_side * k, weights[i]),
                    (2, at_minus[j], i + per_side * k, weights[j]),
                    (3, at_plus[j], i + per_side * k, weights[j]),
                    (4, at_minus[k], i + per_side * j, weights[k]),
                    (5, at_plus[k], i + per_side * j, weights[k]),
                ]
                for face_index, factor, point, weight in entries:
                    trace_table[node, face_index * face_points + point] = factor
                    lift_table[node, face_index * face_points + point] = factor / weight
    spectral = np.zeros((count, count))
    second = np.zeros((count, count))
    for t in range(count):
        for s in range(count):
            if t != s:
                spectral[t, s] = 0.5 * (-1.0) ** (t - s + 1) / math.tan(math.pi * (t - s) / count)
                second[t, s] = -0.5 * (-1.0) ** (t - s) / math.sin(math.pi * (t - s) / count) ** 2
            else:
                second[t, s] = -(count * count + 2.0) / 12.0
    return (trace_table, lift_table, spectral, second)


LANE = 128
WIDE = FIELDS * NODES
FACES = 6
VMEM_LIMIT = 16 * 1024 * 1024
BF16 = jnp.bfloat16
F32 = jnp.float32
OFFSETS = list(range(-REACH, 0)) + list(range(1, REACH + 1))
FIRST_ORDER = (3, 1, 2, 0)
LAST_ORDER = (2, 1, 3, 0)


def wide_tables():
    trace_np, lift_np, spectral_np, second_np = tables(ORDER, NI)
    trace_wide = np.zeros((WIDE, FACES * LANE))
    lift_wide = np.zeros((FACES * LANE, WIDE))
    for c in range(FIELDS):
        rows = slice(c * NODES, (c + 1) * NODES)
        for f in range(FACES):
            cols = slice(f * LANE + c * FPTS, f * LANE + (c + 1) * FPTS)
            face = slice(f * FPTS, (f + 1) * FPTS)
            trace_wide[rows, cols] = trace_np[:, face]
            lift_wide[cols, rows] = lift_np[:, face].T
    return trace_wide, lift_wide, spectral_np[:, 0], second_np[:, 0]


def iotas(shape):
    return [lax.broadcasted_iota(jnp.int32, shape, axis) for axis in range(2)]


def one_hot(mask):
    return jnp.where(mask, 1.0, 0.0).astype(BF16)


def order_table():
    turns = LANE // FPTS
    row, col = iotas((FIELDS * FIELDS * FPTS, turns * LANE))
    c = col % LANE // FPTS
    d = (c + turns - col // LANE) % turns
    source = (c * FIELDS + d) * FPTS + col % FPTS
    return one_hot((c < FIELDS) & (d < FIELDS) & (row == source))


def trace_pool(state, trace_wide, insts, elems):
    wide = jnp.dot(state, trace_wide, preferred_element_type=F32).astype(BF16)
    by_inst = []
    for t in range(insts):
        rows = wide[t * elems : (t + 1) * elems]
        by_inst.append(
            jnp.concatenate([rows[:, f * LANE : (f + 1) * LANE] for f in range(FACES)], 0)
        )
    return jnp.concatenate(by_inst, 1)


def swap_routes(ranks, parts):
    near = [[(p, p + 1) for p in range(first, parts - 1, 2)] for first in range(2)]
    far = [
        [(p + i, p + i + 2) for p in range(first, parts - 3, 4) for i in range(2)]
        for first in (0, 2)
    ]
    routes = []
    for pairs in near + far:
        met = {p for pair in pairs for p in pair}
        alone = [p for p in range(parts) if p not in met]
        idle = [(p, p + 1) for p in alone if p + 1 in alone]
        alone = [p for p in alone if p + 1 not in alone and p - 1 not in alone]
        swaps = [(r * parts + p, r * parts + q) for r in range(ranks) for p, q in pairs + idle]
        swaps += [(r * parts + p, (r ^ 1) * parts + p) for r in range(0, ranks, 2) for p in alone]
        routes.append(swaps + [(q, p) for p, q in swaps])
    return routes


def by_swap(place, by_offset):
    two_down, one_down, one_up, two_up = by_offset
    even = place % 2 == 0
    low = place // 2 % 2 == 0
    return [
        jnp.where(even, one_up, one_down),
        jnp.where(even, one_down, one_up),
        jnp.where(low, two_up, two_down),
        jnp.where(low, two_down, two_up),
    ]


def by_offset(place, blocks):
    even = place % 2 == 0
    low = place // 2 % 2 == 0
    return [
        jnp.where(low, blocks[3], blocks[2]),
        jnp.where(even, blocks[1], blocks[0]),
        jnp.where(even, blocks[0], blocks[1]),
        jnp.where(low, blocks[2], blocks[3]),
    ]


def fill_outgoing(pool, send, out_refs, place, elems):
    slots, capacity = send.shape
    rows, cols = iotas((FACES * elems, slots * capacity))
    ids = FACES * (rows % elems) + rows // elems
    wanted = jnp.concatenate([send[k : k + 1] for k in range(slots)], 1)
    out = lax.dot_general(
        one_hot(ids == wanted), pool, (((0,), (0,)), ((), ())), preferred_element_type=F32
    )
    blocks = by_swap(place, [out[k * capacity : (k + 1) * capacity] for k in range(slots)])
    for block, ref in zip(blocks, out_refs):
        ref[...] = block.astype(BF16)


def diagonal(states, diag, wide_ref, prod_ref, insts, elems):
    tall = insts * elems
    width = diag.shape[1]
    cuts = [(j, j * LANE, min((j + 1) * LANE, width)) for j in range(pl.cdiv(width, LANE))]
    for t in range(insts):
        rows = states[t].astype(F32)
        for j, low, high in cuts:
            first = j * tall + t * elems
            wide_ref[first : first + elems, 0 : high - low] = rows[:, low:high]
    for e in range(elems):
        rows = jnp.concatenate(
            [wide_ref[pl.ds(j * tall + e, insts, stride=elems), :] for j, low, high in cuts], 1
        )
        product = jnp.dot(rows[:, 0:width].astype(BF16), diag[e], preferred_element_type=F32)
        for j, low, high in cuts:
            chunk = product[:, low:high]
            if high - low < LANE:
                chunk = jnp.concatenate([chunk, jnp.zeros((insts, LANE - high + low), F32)], 1)
            prod_ref[pl.ds(j * tall + e, insts, stride=elems), :] = chunk
    return [
        jnp.concatenate(
            [
                prod_ref[j * tall + t * elems : j * tall + (t + 1) * elems, 0 : high - low]
                for j, low, high in cuts
            ],
            1,
        )
        for t in range(insts)
    ]


def flux_order(rows, order):
    per_face = FIELDS * FIELDS * FPTS
    by_face = jnp.concatenate(
        [rows[:, f * per_face : (f + 1) * per_face] for f in range(FACES)], 0
    )
    return jnp.dot(by_face, order, preferred_element_type=F32).astype(BF16)


def source_table(sources, elems, slots):
    faces = FACES * elems
    columns = lax.broadcasted_iota(jnp.int32, (elems, faces + slots), 1)
    ids = jnp.where(columns < faces, FACES * (columns % elems) + columns // elems, columns)
    hot = [jnp.where(sources[:, f : f + 1] == ids, 1.0, 0.0) for f in range(FACES)]
    return jnp.concatenate(hot, 0).astype(BF16)


def normal_flux(blocks, factors, insts):
    count = blocks.shape[0]
    stacked = jnp.concatenate([blocks[:, t * LANE : (t + 1) * LANE] for t in range(insts)], 0)
    summed = [None] * insts
    for k in range(LANE // FPTS):
        turned = stacked if k == 0 else pltpu.roll(stacked, k * FPTS, 1)
        for t in range(insts):
            term = factors[:, k * LANE : (k + 1) * LANE] * turned[t * count : (t + 1) * count]
            summed[t] = term if k == 0 else summed[t] + term
    return [rows.astype(BF16) for rows in summed]


def lift_faces(normal, lift, elems):
    rows = [
        jnp.concatenate([n[f * elems : (f + 1) * elems] for f in range(FACES)], 1) for n in normal
    ]
    return jnp.dot(jnp.concatenate(rows, 0), lift, preferred_element_type=F32)


def couple(entry_ref, states, t, shift, insts):
    summed = None
    for s in range(insts):
        d = (t - s + shift * insts) % NI
        term = entry_ref[d : d + 1, :] * states[s].astype(F32)
        summed = term if summed is None else summed + term
    return summed


def table_kernel(order_ref):
    order_ref[...] = order_table()


def first_kernel(spectral, second, place_ref, freq_ref, order_ref, state_ref, trace_ref, send_ref,
                 entry_ref, pool_ref, *out_refs):
    insts, elems, width = state_ref.shape
    state = state_ref[...].reshape(insts * elems, width)
    pool = trace_pool(state, trace_ref[...], insts, elems)
    pool_ref[...] = pool
    fill_outgoing(pool, send_ref[0], out_refs, place_ref[0], elems)
    freq = freq_ref[0]
    for d in range(NI):
        entry = freq * float(spectral[d]) - dissipation * float(second[d])
        entry_ref[d : d + 1, :] = jnp.full((1, width), entry, F32)


def base_kernel(slots, state_ref, diag_ref, forcing_ref, entry_ref, flux_ref, source_ref, order_ref,
                prod_out_ref, rest_ref, flux_out_ref, hot_ref, wide_ref, prod_ref):
    insts, elems, width = state_ref.shape
    hot_ref[...] = source_table(source_ref[...].T, elems, slots)
    flux_out_ref[...] = flux_order(flux_ref[...], order_ref[...])
    states = [state_ref[t] for t in range(insts)]
    products = diagonal(states, diag_ref, wide_ref, prod_ref, insts, elems)
    for t in range(insts):
        prod_out_ref[t] = products[t]
        rest_ref[t] = couple(entry_ref, states, t, 0, insts) - forcing_ref[t].astype(F32)


def last_base_kernel(state_ref, pool_ref, diag_ref, forcing_ref, hot_ref, flux_ref, lift_ref,
                     base_ref, factor_ref, wide_ref, prod_ref):
    insts, elems, width = state_ref.shape
    flux = flux_ref[...]
    hot = hot_ref[...]
    faces = hot.shape[0]
    factors = lax.dot_general(hot, flux, (((0,), (0,)), ((), ())), preferred_element_type=F32)
    factor_ref[...] = factors[faces:]
    empty = jnp.zeros((hot.shape[1] - faces, insts * LANE), BF16)
    pool = jnp.concatenate([pool_ref[...], empty], 0)
    picked = jnp.dot(hot, pool, preferred_element_type=F32)
    normal = normal_flux(picked, flux.astype(F32), insts)
    lifted = lift_faces(normal, lift_ref[...], elems)
    states = [state_ref[t].astype(BF16) for t in range(insts)]
    products = diagonal(states, diag_ref, wide_ref, prod_ref, insts, elems)
    for t in range(insts):
        base_ref[t] = (
            products[t] + lifted[t * elems : (t + 1) * elems] - forcing_ref[t].astype(F32)
        )


def message_kernel(ranks, partial_ref, first_ref, base_ref, entry_ref, *refs):
    message_refs, (state_ref, out_ref) = refs[: ranks - 1], refs[ranks - 1 :]
    insts, elems, width = base_ref.shape
    firsts = [[first_ref[t] for t in range(insts)]]
    partials = [[partial_ref[t] for t in range(insts)]]
    for message_ref in message_refs:
        rows = [
            message_ref[i * elems : (i + 1) * elems, 0:width] for i in range(2 * insts)
        ]
        firsts.append(rows[:insts])
        partials.append(rows[insts:])
    states = []
    for k in range(ranks):
        of_rank = []
        for t in range(insts):
            state = partials[k][t].astype(F32)
            for j in range(ranks):
                if j != k:
                    state -= pseudo_step * couple(entry_ref, firsts[j], t, k - j, insts)
            of_rank.append(state.astype(BF16) if k == 0 else state)
        states.append(of_rank)
    for t in range(insts):
        state_ref[t] = states[0][t]
        coupling = base_ref[t]
        for k in range(ranks):
            coupling += couple(entry_ref, states[k], t, -k, insts)
        out_ref[t] = coupling


def received(parts, place, got_refs, order):
    got_refs = {swap: got_refs[i] for i, swap in enumerate(order)}
    arrived = by_offset(
        place, [got_refs[swap][...].astype(F32) for swap in range(len(OFFSETS))]
    )
    for k, offset in enumerate(OFFSETS):
        exists = (place + offset >= 0) & (place + offset < parts)
        arrived[k] = jnp.where(exists, arrived[k], jnp.zeros_like(arrived[k]))
    return jnp.concatenate(arrived, 0)


def step_kernel(parts, place_ref, *refs):
    got_refs, refs = refs[: len(OFFSETS)], refs[len(OFFSETS) :]
    (state_ref, pool_ref, prod_ref, rest_ref, hot_ref, flux_ref, lift_ref, trace_ref, send_ref,
     partial_ref, message_ref, next_pool_ref, *out_refs) = refs
    insts, elems, width = state_ref.shape
    place = place_ref[0]
    blocks = received(parts, place, got_refs, FIRST_ORDER).astype(BF16)
    pool = jnp.concatenate([pool_ref[...], blocks], 0)
    picked = jnp.dot(hot_ref[...], pool, preferred_element_type=F32)
    normal = normal_flux(picked, flux_ref[...].astype(F32), insts)
    lifted = lift_faces(normal, lift_ref[...], elems)
    message_ref[...] = jnp.zeros_like(message_ref)
    fresh = []
    for t in range(insts):
        spatial = prod_ref[t] + lifted[t * elems : (t + 1) * elems]
        moved = state_ref[t].astype(F32) - pseudo_step * (spatial + rest_ref[t])
        partial_ref[t] = moved
        fresh.append(moved.astype(BF16))
        lean = (moved - pseudo_step * spatial).astype(BF16)
        for i, block in enumerate((state_ref[t], lean)):
            low = (i * insts + t) * elems
            message_ref[low : low + elems, 0:width] = block
    pool = trace_pool(jnp.concatenate(fresh, 0), trace_ref[...], insts, elems)
    next_pool_ref[...] = pool
    fill_outgoing(pool, send_ref[0], out_refs, place, elems)


def last_kernel(parts, place_ref, *refs):
    got_refs, refs = refs[: len(OFFSETS)], refs[len(OFFSETS) :]
    (state_ref, base_ref, hot_ref, factor_ref, lift_ref, final_hbm, residual_hbm,
     final_ref, residual_ref, sems) = refs
    insts, elems, width = state_ref.shape
    blocks = received(parts, place_ref[0], got_refs, LAST_ORDER)
    normal = normal_flux(blocks, factor_ref[...], insts)
    empty = jnp.zeros((FACES * elems, insts * LANE), BF16)
    rows = jnp.concatenate([empty, jnp.concatenate(normal, 1)], 0)
    spots = jnp.dot(hot_ref[...], rows, preferred_element_type=F32).astype(BF16)
    lifted = lift_faces(
        [spots[:, t * LANE : (t + 1) * LANE] for t in range(insts)], lift_ref[...], elems
    )
    copies = []
    for t in range(insts):
        residual = base_ref[t] + lifted[t * elems : (t + 1) * elems]
        residual_ref[t] = residual
        final_ref[t] = (state_ref[t].astype(F32) - pseudo_step * residual).astype(BF16)
        copies += [
            pltpu.make_async_copy(residual_ref.at[t], residual_hbm.at[t], sems.at[0, t]),
            pltpu.make_async_copy(final_ref.at[t], final_hbm.at[t], sems.at[1, t]),
        ]
        copies[-2].start()
        copies[-1].start()
    for copy in copies:
        copy.wait()


def on_device(
    initial_state, forcing, diagonal_blocks, flux_jacobian, send_list, source_index, frequency
):
    insts, elems, width = initial_state.shape
    parts = lax.axis_size("dom")
    ranks = lax.axis_size("inst")
    slots, capacity = send_list.shape[1:]
    faces = FACES * elems
    trace_np, lift_np, spectral, second = wide_tables()
    trace_wide = jnp.asarray(trace_np, BF16)
    lift_wide = jnp.asarray(lift_np, BF16)
    place = lax.axis_index("dom").reshape(1)
    sources = source_index.T
    routes = swap_routes(ranks, parts)

    smem = pl.BlockSpec(memory_space=pltpu.SMEM)
    vmem = pl.BlockSpec(memory_space=pltpu.VMEM)
    params = pltpu.CompilerParams(vmem_limit_bytes=VMEM_LIMIT)

    def like(array):
        return jax.ShapeDtypeStruct(array.shape, array.dtype)

    wide_shape = jax.ShapeDtypeStruct(initial_state.shape, F32)
    pool_shape = jax.ShapeDtypeStruct((faces, insts * LANE), BF16)
    out_shapes = [jax.ShapeDtypeStruct((capacity, insts * LANE), BF16)] * slots
    flux_shape = jax.ShapeDtypeStruct((faces, LANE // FPTS * LANE), BF16)
    hot_shape = jax.ShapeDtypeStruct((faces, faces + slots * capacity), BF16)
    factor_shape = jax.ShapeDtypeStruct((slots * capacity, LANE // FPTS * LANE), F32)

    def exchange(outgoing, order):
        return [
            lax.ppermute(outgoing[swap], ("inst", "dom"), routes[swap]) for swap in order
        ]

    entry_shape = jax.ShapeDtypeStruct((NI, width), F32)
    message_shape = jax.ShapeDtypeStruct((2 * insts * elems, pl.cdiv(width, LANE) * LANE), BF16)
    chunks = [pltpu.VMEM((pl.cdiv(width, LANE) * insts * elems, LANE), F32)] * 2
    diag_cost = pl.CostEstimate(
        flops=2 * insts * diagonal_blocks.size, bytes_accessed=2 * diagonal_blocks.size,
        transcendentals=0,
    )
    order = pl.pallas_call(
        table_kernel,
        out_shape=jax.ShapeDtypeStruct((FIELDS * FIELDS * FPTS, LANE // FPTS * LANE), BF16),
        out_specs=vmem,
        compiler_params=params,
        cost_estimate=pl.CostEstimate(flops=10**10, bytes_accessed=10**6, transcendentals=0),
        name="tables",
    )()
    freq, _ = lax.optimization_barrier((frequency, order))
    entries, pool, *outgoing = pl.pallas_call(
        functools.partial(first_kernel, spectral, second),
        out_shape=[entry_shape, pool_shape] + out_shapes,
        in_specs=[smem] * 2 + [vmem] * 4,
        out_specs=[vmem] * (2 + len(out_shapes)),
        compiler_params=params,
        cost_estimate=pl.CostEstimate(flops=10**10, bytes_accessed=10**6, transcendentals=0),
        name="first_traces",
    )(place, freq, order, initial_state, trace_wide, send_list)
    got = exchange(outgoing, FIRST_ORDER)
    product, rest, flux, hot = pl.pallas_call(
        functools.partial(base_kernel, slots * capacity),
        out_shape=[wide_shape] * 2 + [flux_shape, hot_shape],
        in_specs=[vmem] * 7,
        out_specs=[vmem] * 4,
        scratch_shapes=chunks,
        compiler_params=params,
        cost_estimate=diag_cost,
        name="own_terms",
    )(initial_state, diagonal_blocks, forcing, entries, flux_jacobian, sources, order)
    partial, message, pool, *outgoing = pl.pallas_call(
        functools.partial(step_kernel, parts),
        out_shape=[wide_shape, message_shape, pool_shape] + out_shapes,
        in_specs=[smem] + [vmem] * (slots + 9),
        out_specs=[vmem] * (3 + len(out_shapes)),
        compiler_params=params,
        name="first_step",
    )(place, *got, initial_state, pool, product, rest, hot, flux, lift_wide, trace_wide,
      send_list)
    messages = [
        lax.ppermute(message, "inst", [((i + rank) % ranks, i) for i in range(ranks)])
        for rank in range(1, ranks)
    ]
    got = exchange(outgoing, LAST_ORDER)
    base, factors = pl.pallas_call(
        last_base_kernel,
        out_shape=[wide_shape, factor_shape],
        in_specs=[vmem] * 7,
        out_specs=[vmem] * 2,
        scratch_shapes=chunks,
        compiler_params=params,
        cost_estimate=diag_cost,
        name="last_own_terms",
    )(partial, pool, diagonal_blocks, forcing, hot, flux, lift_wide)
    state, base = pl.pallas_call(
        functools.partial(message_kernel, ranks),
        out_shape=[like(initial_state), wide_shape],
        in_specs=[vmem] * (ranks + 3),
        out_specs=[vmem] * 2,
        compiler_params=params,
        name="message_terms",
    )(partial, initial_state, base, entries, *messages)
    return pl.pallas_call(
        functools.partial(last_kernel, parts),
        out_shape=[like(initial_state), wide_shape],
        in_specs=[smem] + [vmem] * (slots + 5),
        out_specs=[pl.BlockSpec(memory_space=pl.ANY)] * 2,
        scratch_shapes=[
            pltpu.VMEM(initial_state.shape, BF16),
            pltpu.VMEM(initial_state.shape, F32),
            pltpu.SemaphoreType.DMA((2, insts)),
        ],
        compiler_params=params,
        name="last_step",
    )(place, *got, state, base, hot, factors, lift_wide)


def solution(mesh):
    return jax.shard_map(
        on_device,
        mesh=mesh,
        in_specs=(
            P("inst", "dom", None),
            P("inst", "dom", None),
            P("dom", None, None),
            P("dom", None),
            P("dom", None, None),
            P("dom", None),
            P(),
        ),
        out_specs=(P("inst", "dom", None), P("inst", "dom", None)),
        check_vma=False,
    )
```

```python
import functools
import math

import jax
import jax.numpy as jnp
import numpy as np
from jax import lax
from jax.experimental import pallas as pl
from jax.experimental.pallas import tpu as pltpu
from jax.sharding import PartitionSpec as P

FIELDS = 5
ORDER = 3
NODES = 64
FPTS = 16
NI = 8
REACH = 2
ITERS = 2


pseudo_step = 0.5
dissipation = 0.25


def gauss_legendre(count):
    points = []
    weights = []
    for i in range(count):
        where = math.cos(math.pi * (i + 0.75) / (count + 0.5))
        for sweep in range(100):
            before = 1.0
            value = where
            for j in range(2, count + 1):
                after = ((2 * j - 1) * where * value - (j - 1) * before) / j
                before = value
                value = after
            slope = count * (where * value - before) / (where * where - 1.0)
            where = where - value / slope
        before = 1.0
        value = where
        for j in range(2, count + 1):
            after = ((2 * j - 1) * where * value - (j - 1) * before) / j
            before = value
            value = after
        slope = count * (where * value - before) / (where * where - 1.0)
        points.append(where)
        weights.append(2.0 / ((1.0 - where * where) * slope * slope))
    return (np.array(points[::-1]), np.array(weights[::-1]))


def lagrange_at(points, where):
    values = np.ones(points.shape[0])
    for i in range(points.shape[0]):
        for j in range(points.shape[0]):
            if j != i:
                values[i] = values[i] * (where - points[j]) / (points[i] - points[j])
    return values


def tables(order, count):
    points, weights = gauss_legendre(order + 1)
    at_minus = lagrange_at(points, -1.0)
    at_plus = lagrange_at(points, 1.0)
    per_side = order + 1
    node_count = per_side**3
    face_points = per_side**2
    trace_table = np.zeros((node_count, 6 * face_points))
    lift_table = np.zeros((node_count, 6 * face_points))
    for k in range(per_side):
        for j in range(per_side):
            for i in range(per_side):
                node = i + per_side * j + per_side * per_side * k
                entries = [
                    (0, at_minus[i], j + per_side * k, weights[i]),
                    (1, at_plus[i], j + per_side * k, weights[i]),
                    (2, at_minus[j], i + per_side * k, weights[j]),
                    (3, at_plus[j], i + per_side * k, weights[j]),
                    (4, at_minus[k], i + per_side * j, weights[k]),
                    (5, at_plus[k], i + per_side * j, weights[k]),
                ]
                for face_index, factor, point, weight in entries:
                    trace_table[node, face_index * face_points + point] = factor
                    lift_table[node, face_index * face_points + point] = factor / weight
    spectral = np.zeros((count, count))
    second = np.zeros((count, count))
    for t in range(count):
        for s in range(count):
            if t != s:
                spectral[t, s] = 0.5 * (-1.0) ** (t - s + 1) / math.tan(math.pi * (t - s) / count)
                second[t, s] = -0.5 * (-1.0) ** (t - s) / math.sin(math.pi * (t - s) / count) ** 2
            else:
                second[t, s] = -(count * count + 2.0) / 12.0
    return (trace_table, lift_table, spectral, second)


LANE = 128
WIDE = FIELDS * NODES
FACES = 6
TRACE_TABLES = 3
VMEM_LIMIT = 16 * 1024 * 1024
BF16 = jnp.bfloat16
F32 = jnp.float32
OFFSETS = list(range(-REACH, 0)) + list(range(1, REACH + 1))
FIRST_ORDER = (3, 1, 2, 0)
LAST_ORDER = (2, 1, 3, 0)


def wide_tables():
    trace_np, lift_np, spectral_np, second_np = tables(ORDER, NI)
    trace_wide = np.zeros((WIDE, FACES * LANE))
    lift_wide = np.zeros((FACES * LANE, WIDE))
    for c in range(FIELDS):
        rows = slice(c * NODES, (c + 1) * NODES)
        for f in range(FACES):
            cols = slice(f * LANE + c * FPTS, f * LANE + (c + 1) * FPTS)
            face = slice(f * FPTS, (f + 1) * FPTS)
            trace_wide[rows, cols] = trace_np[:, face]
            lift_wide[cols, rows] = lift_np[:, face].T
    return trace_wide, lift_wide, spectral_np[:, 0], second_np[:, 0]


def iotas(shape):
    return [lax.broadcasted_iota(jnp.int32, shape, axis) for axis in range(2)]


def one_hot(mask):
    return jnp.where(mask, 1.0, 0.0).astype(BF16)


def spread_table():
    row, col = iotas((LANE, FIELDS * LANE))
    inside = col % LANE < FIELDS * FPTS
    return one_hot(inside & (row == col // LANE * FPTS + col % FPTS))


def order_table():
    row, col = iotas((FIELDS * FIELDS * FPTS, FIELDS * LANE))
    place = col % LANE
    source = place // FPTS * FIELDS * FPTS + col // LANE * FPTS + col % FPTS
    return one_hot((place < FIELDS * FPTS) & (row == source))


def trace_pool(state, trace_tables, insts, elems):
    faces = []
    for table in trace_tables:
        wide = jnp.dot(state, table, preferred_element_type=F32).astype(BF16)
        faces += [wide[:, at : at + LANE] for at in range(0, table.shape[1], LANE)]
    by_inst = []
    for t in range(insts):
        by_inst.append(jnp.concatenate([rows[t * elems : (t + 1) * elems] for rows in faces], 0))
    return jnp.concatenate(by_inst, 1)


def swap_routes(ranks, parts):
    near = [[(p, p + 1) for p in range(first, parts - 1, 2)] for first in range(2)]
    far = [
        [(p + i, p + i + 2) for p in range(first, parts - 3, 4) for i in range(2)]
        for first in (0, 2)
    ]
    routes = []
    for pairs in near + far:
        met = {p for pair in pairs for p in pair}
        alone = [p for p in range(parts) if p not in met]
        idle = [(p, p + 1) for p in alone if p + 1 in alone]
        alone = [p for p in alone if p + 1 not in alone and p - 1 not in alone]
        swaps = [(r * parts + p, r * parts + q) for r in range(ranks) for p, q in pairs + idle]
        swaps += [(r * parts + p, (r ^ 1) * parts + p) for r in range(0, ranks, 2) for p in alone]
        routes.append(swaps + [(q, p) for p, q in swaps])
    return routes


def by_swap(place, by_offset):
    two_down, one_down, one_up, two_up = by_offset
    even = place % 2 == 0
    low = place // 2 % 2 == 0
    return [
        jnp.where(even, one_up, one_down),
        jnp.where(even, one_down, one_up),
        jnp.where(low, two_up, two_down),
        jnp.where(low, two_down, two_up),
    ]


def by_offset(place, blocks):
    even = place % 2 == 0
    low = place // 2 % 2 == 0
    return [
        jnp.where(low, blocks[3], blocks[2]),
        jnp.where(even, blocks[1], blocks[0]),
        jnp.where(even, blocks[0], blocks[1]),
        jnp.where(low, blocks[2], blocks[3]),
    ]


def fill_outgoing(pool, send, out_refs, place, elems):
    slots, capacity = send.shape
    rows, cols = iotas((FACES * elems, slots * capacity))
    ids = FACES * (rows % elems) + rows // elems
    wanted = jnp.concatenate([send[k : k + 1] for k in range(slots)], 1)
    out = lax.dot_general(
        one_hot(ids == wanted), pool, (((0,), (0,)), ((), ())), preferred_element_type=F32
    )
    blocks = by_swap(place, [out[k * capacity : (k + 1) * capacity] for k in range(slots)])
    for block, ref in zip(blocks, out_refs):
        ref[...] = block.astype(BF16)


def diagonal(states, diag, wide_ref, prod_ref, insts, elems):
    tall = insts * elems
    width = diag.shape[1]
    cuts = [(j, j * LANE, min((j + 1) * LANE, width)) for j in range(pl.cdiv(width, LANE))]
    for t in range(insts):
        rows = states[t].astype(F32)
        for j, low, high in cuts:
            first = j * tall + t * elems
            wide_ref[first : first + elems, 0 : high - low] = rows[:, low:high]
    for e in range(elems):
        rows = jnp.concatenate(
            [wide_ref[pl.ds(j * tall + e, insts, stride=elems), :] for j, low, high in cuts], 1
        )
        product = jnp.dot(rows[:, 0:width].astype(BF16), diag[e], preferred_element_type=F32)
        for j, low, high in cuts:
            chunk = product[:, low:high]
            if high - low < LANE:
                chunk = jnp.concatenate([chunk, jnp.zeros((insts, LANE - high + low), F32)], 1)
            prod_ref[pl.ds(j * tall + e, insts, stride=elems), :] = chunk
    return [
        jnp.concatenate(
            [
                prod_ref[j * tall + t * elems : j * tall + (t + 1) * elems, 0 : high - low]
                for j, low, high in cuts
            ],
            1,
        )
        for t in range(insts)
    ]


def flux_order(rows, order):
    per_face = FIELDS * FIELDS * FPTS
    by_face = jnp.concatenate(
        [rows[:, f * per_face : (f + 1) * per_face] for f in range(FACES)], 0
    )
    return jnp.dot(by_face, order, preferred_element_type=F32).astype(BF16)


def source_table(sources, elems, slots):
    faces = FACES * elems
    columns = lax.broadcasted_iota(jnp.int32, (elems, faces + slots), 1)
    ids = jnp.where(columns < faces, FACES * (columns % elems) + columns // elems, columns)
    hot = [jnp.where(sources[:, f : f + 1] == ids, 1.0, 0.0) for f in range(FACES)]
    return jnp.concatenate(hot, 0).astype(BF16)


def face_flux(picked, flux, spread, insts):
    count = picked.shape[0]
    stacked = jnp.concatenate([picked[:, t * LANE : (t + 1) * LANE] for t in range(insts)], 0)
    wide = jnp.dot(stacked, spread, preferred_element_type=F32)
    normal = []
    for t in range(insts):
        rows = wide[t * count : (t + 1) * count]
        summed = flux[:, 0:LANE] * rows[:, 0:LANE]
        for d in range(1, FIELDS):
            summed += flux[:, d * LANE : (d + 1) * LANE] * rows[:, d * LANE : (d + 1) * LANE]
        normal.append(summed.astype(BF16))
    return normal


def lift_faces(normal, lift, elems):
    rows = [
        jnp.concatenate([n[f * elems : (f + 1) * elems] for f in range(FACES)], 1) for n in normal
    ]
    return jnp.dot(jnp.concatenate(rows, 0), lift, preferred_element_type=F32)


def couple(entry_ref, states, t, shift, insts):
    summed = None
    for s in range(insts):
        d = (t - s + shift * insts) % NI
        term = entry_ref[d : d + 1, :] * states[s].astype(F32)
        summed = term if summed is None else summed + term
    return summed


def rotated(flux):
    place = lax.broadcasted_iota(jnp.int32, (flux.shape[0], LANE), 1) // FPTS
    blocks = []
    for k in range(LANE // FPTS):
        block = jnp.zeros((flux.shape[0], LANE), F32)
        for d in range(FIELDS):
            met = place == (d + k) % (LANE // FPTS)
            block = jnp.where(met, flux[:, d * LANE : (d + 1) * LANE], block)
        blocks.append(block)
    return jnp.concatenate(blocks, 1)


def slot_normal(blocks, factors, insts):
    count = blocks.shape[0]
    stacked = jnp.concatenate([blocks[:, t * LANE : (t + 1) * LANE] for t in range(insts)], 0)
    summed = [None] * insts
    for k in range(LANE // FPTS):
        turned = stacked if k == 0 else pltpu.roll(stacked, k * FPTS, 1)
        for t in range(insts):
            term = factors[:, k * LANE : (k + 1) * LANE] * turned[t * count : (t + 1) * count]
            summed[t] = term if k == 0 else summed[t] + term
    return [rows.astype(BF16) for rows in summed]


def table_kernel(spread_ref, order_ref):
    spread_ref[...] = spread_table()
    order_ref[...] = order_table()


def first_kernel(spectral, second, place_ref, freq_ref, spread_ref, state_ref, send_ref, *refs):
    insts, elems, width = state_ref.shape
    trace_refs, (entry_ref, pool_ref, *out_refs) = refs[:TRACE_TABLES], refs[TRACE_TABLES:]
    state = state_ref[...].reshape(insts * elems, width)
    pool = trace_pool(state, [ref[...] for ref in trace_refs], insts, elems)
    pool_ref[...] = pool
    fill_outgoing(pool, send_ref[0], out_refs, place_ref[0], elems)
    freq = freq_ref[0]
    for d in range(NI):
        entry = freq * float(spectral[d]) - dissipation * float(second[d])
        entry_ref[d : d + 1, :] = jnp.full((1, width), entry, F32)


def base_kernel(slots, state_ref, diag_ref, forcing_ref, entry_ref, flux_ref, source_ref, order_ref,
                prod_out_ref, rest_ref, flux_out_ref, hot_ref, wide_ref, prod_ref):
    insts, elems, width = state_ref.shape
    hot_ref[...] = source_table(source_ref[...].T, elems, slots)
    flux_out_ref[...] = flux_order(flux_ref[...], order_ref[...])
    states = [state_ref[t] for t in range(insts)]
    products = diagonal(states, diag_ref, wide_ref, prod_ref, insts, elems)
    for t in range(insts):
        prod_out_ref[t] = products[t]
        rest_ref[t] = couple(entry_ref, states, t, 0, insts) - forcing_ref[t].astype(F32)


def last_base_kernel(state_ref, pool_ref, diag_ref, forcing_ref, hot_ref, flux_ref, spread_ref,
                     lift_ref, base_ref, factor_ref, wide_ref, prod_ref):
    insts, elems, width = state_ref.shape
    flux = flux_ref[...]
    hot = hot_ref[...]
    faces = hot.shape[0]
    factors = lax.dot_general(hot, flux, (((0,), (0,)), ((), ())), preferred_element_type=F32)
    factor_ref[...] = rotated(factors[faces:])
    empty = jnp.zeros((hot.shape[1] - faces, insts * LANE), BF16)
    pool = jnp.concatenate([pool_ref[...], empty], 0)
    picked = jnp.dot(hot, pool, preferred_element_type=F32).astype(BF16)
    normal = face_flux(picked, flux.astype(F32), spread_ref[...], insts)
    lifted = lift_faces(normal, lift_ref[...], elems)
    states = [state_ref[t].astype(BF16) for t in range(insts)]
    products = diagonal(states, diag_ref, wide_ref, prod_ref, insts, elems)
    for t in range(insts):
        base_ref[t] = (
            products[t] + lifted[t * elems : (t + 1) * elems] - forcing_ref[t].astype(F32)
        )


def message_kernel(ranks, partial_ref, first_ref, base_ref, entry_ref, *refs):
    message_refs, (state_ref, out_ref) = refs[: ranks - 1], refs[ranks - 1 :]
    insts, elems, width = base_ref.shape
    firsts = [[first_ref[t] for t in range(insts)]]
    partials = [[partial_ref[t] for t in range(insts)]]
    for message_ref in message_refs:
        rows = [
            message_ref[i * elems : (i + 1) * elems, 0:width] for i in range(2 * insts)
        ]
        firsts.append(rows[:insts])
        partials.append(rows[insts:])
    states = []
    for k in range(ranks):
        of_rank = []
        for t in range(insts):
            state = partials[k][t].astype(F32)
            for j in range(ranks):
                if j != k:
                    state -= pseudo_step * couple(entry_ref, firsts[j], t, k - j, insts)
            of_rank.append(state.astype(BF16) if k == 0 else state)
        states.append(of_rank)
    for t in range(insts):
        state_ref[t] = states[0][t]
        coupling = base_ref[t]
        for k in range(ranks):
            coupling += couple(entry_ref, states[k], t, -k, insts)
        out_ref[t] = coupling


def received(parts, place, got_refs, order):
    got_refs = {swap: got_refs[i] for i, swap in enumerate(order)}
    arrived = by_offset(
        place, [got_refs[swap][...].astype(F32) for swap in range(len(OFFSETS))]
    )
    for k, offset in enumerate(OFFSETS):
        exists = (place + offset >= 0) & (place + offset < parts)
        arrived[k] = jnp.where(exists, arrived[k], jnp.zeros_like(arrived[k]))
    return jnp.concatenate(arrived, 0)


def step_kernel(parts, place_ref, spread_ref, *refs):
    got_refs, refs = refs[: len(OFFSETS)], refs[len(OFFSETS) :]
    trace_refs, refs = refs[:TRACE_TABLES], refs[TRACE_TABLES:]
    (state_ref, pool_ref, prod_ref, rest_ref, hot_ref, flux_ref, lift_ref, send_ref,
     partial_ref, message_ref, next_pool_ref, *out_refs) = refs
    insts, elems, width = state_ref.shape
    place = place_ref[0]
    blocks = received(parts, place, got_refs, FIRST_ORDER).astype(BF16)
    pool = jnp.concatenate([pool_ref[...], blocks], 0)
    picked = jnp.dot(hot_ref[...], pool, preferred_element_type=F32).astype(BF16)
    normal = face_flux(picked, flux_ref[...].astype(F32), spread_ref[...], insts)
    lifted = lift_faces(normal, lift_ref[...], elems)
    message_ref[...] = jnp.zeros_like(message_ref)
    fresh = []
    for t in range(insts):
        spatial = prod_ref[t] + lifted[t * elems : (t + 1) * elems]
        moved = state_ref[t].astype(F32) - pseudo_step * (spatial + rest_ref[t])
        partial_ref[t] = moved
        fresh.append(moved.astype(BF16))
        lean = (moved - pseudo_step * spatial).astype(BF16)
        for i, block in enumerate((state_ref[t], lean)):
            low = (i * insts + t) * elems
            message_ref[low : low + elems, 0:width] = block
    tables_of_traces = [ref[...] for ref in trace_refs]
    pool = trace_pool(jnp.concatenate(fresh, 0), tables_of_traces, insts, elems)
    next_pool_ref[...] = pool
    fill_outgoing(pool, send_ref[0], out_refs, place, elems)


def last_kernel(parts, place_ref, *refs):
    got_refs, refs = refs[: len(OFFSETS)], refs[len(OFFSETS) :]
    (state_ref, base_ref, hot_ref, factor_ref, lift_ref, final_hbm, residual_hbm,
     final_ref, residual_ref, sems) = refs
    insts, elems, width = state_ref.shape
    blocks = received(parts, place_ref[0], got_refs, LAST_ORDER)
    normal = slot_normal(blocks, factor_ref[...], insts)
    empty = jnp.zeros((FACES * elems, insts * LANE), BF16)
    rows = jnp.concatenate([empty, jnp.concatenate(normal, 1)], 0)
    spots = jnp.dot(hot_ref[...], rows, preferred_element_type=F32).astype(BF16)
    lifted = lift_faces(
        [spots[:, t * LANE : (t + 1) * LANE] for t in range(insts)], lift_ref[...], elems
    )
    for t in range(insts):
        residual = base_ref[t] + lifted[t * elems : (t + 1) * elems]
        residual_ref[t] = residual
        final_ref[t] = (state_ref[t].astype(F32) - pseudo_step * residual).astype(BF16)
    copies = [
        pltpu.make_async_copy(residual_ref, residual_hbm, sems.at[0]),
        pltpu.make_async_copy(final_ref, final_hbm, sems.at[1]),
    ]
    for copy in copies:
        copy.start()
    for copy in copies:
        copy.wait()


def on_device(
    initial_state, forcing, diagonal_blocks, flux_jacobian, send_list, source_index, frequency
):
    insts, elems, width = initial_state.shape
    parts = lax.axis_size("dom")
    ranks = lax.axis_size("inst")
    slots, capacity = send_list.shape[1:]
    faces = FACES * elems
    trace_np, lift_np, spectral, second = wide_tables()
    trace_wide = [jnp.asarray(part, BF16) for part in np.split(trace_np, TRACE_TABLES, 1)]
    lift_wide = jnp.asarray(lift_np, BF16)
    place = lax.axis_index("dom").reshape(1)
    sources = source_index.T
    routes = swap_routes(ranks, parts)

    smem = pl.BlockSpec(memory_space=pltpu.SMEM)
    vmem = pl.BlockSpec(memory_space=pltpu.VMEM)
    params = pltpu.CompilerParams(vmem_limit_bytes=VMEM_LIMIT)

    def like(array):
        return jax.ShapeDtypeStruct(array.shape, array.dtype)

    wide_shape = jax.ShapeDtypeStruct(initial_state.shape, F32)
    pool_shape = jax.ShapeDtypeStruct((faces, insts * LANE), BF16)
    out_shapes = [jax.ShapeDtypeStruct((capacity, insts * LANE), BF16)] * slots
    flux_shape = jax.ShapeDtypeStruct((faces, FIELDS * LANE), BF16)
    hot_shape = jax.ShapeDtypeStruct((faces, faces + slots * capacity), BF16)
    factor_shape = jax.ShapeDtypeStruct((slots * capacity, LANE // FPTS * LANE), F32)

    def exchange(outgoing, order):
        return [
            lax.ppermute(outgoing[swap], ("inst", "dom"), routes[swap]) for swap in order
        ]

    entry_shape = jax.ShapeDtypeStruct((NI, width), F32)
    message_shape = jax.ShapeDtypeStruct((2 * insts * elems, pl.cdiv(width, LANE) * LANE), BF16)
    chunks = [pltpu.VMEM((pl.cdiv(width, LANE) * insts * elems, LANE), F32)] * 2
    diag_cost = pl.CostEstimate(
        flops=2 * insts * diagonal_blocks.size, bytes_accessed=2 * diagonal_blocks.size,
        transcendentals=0,
    )
    spread, order = pl.pallas_call(
        table_kernel,
        out_shape=[
            jax.ShapeDtypeStruct((LANE, FIELDS * LANE), BF16),
            jax.ShapeDtypeStruct((FIELDS * FIELDS * FPTS, FIELDS * LANE), BF16),
        ],
        out_specs=[vmem] * 2,
        compiler_params=params,
        cost_estimate=pl.CostEstimate(flops=10**10, bytes_accessed=10**6, transcendentals=0),
        name="tables",
    )()
    freq, _ = lax.optimization_barrier((frequency, spread))
    entries, pool, *outgoing = pl.pallas_call(
        functools.partial(first_kernel, spectral, second),
        out_shape=[entry_shape, pool_shape] + out_shapes,
        in_specs=[smem] * 2 + [vmem] * (3 + TRACE_TABLES),
        out_specs=[vmem] * (2 + len(out_shapes)),
        compiler_params=params,
        cost_estimate=pl.CostEstimate(flops=10**10, bytes_accessed=10**6, transcendentals=0),
        name="first_traces",
    )(place, freq, spread, initial_state, send_list, *trace_wide)
    got = exchange(outgoing, FIRST_ORDER)
    product, rest, flux, hot = pl.pallas_call(
        functools.partial(base_kernel, slots * capacity),
        out_shape=[wide_shape] * 2 + [flux_shape, hot_shape],
        in_specs=[vmem] * 7,
        out_specs=[vmem] * 4,
        scratch_shapes=chunks,
        compiler_params=params,
        cost_estimate=diag_cost,
        name="own_terms",
    )(initial_state, diagonal_blocks, forcing, entries, flux_jacobian, sources, order)
    partial, message, pool, *outgoing = pl.pallas_call(
        functools.partial(step_kernel, parts),
        out_shape=[wide_shape, message_shape, pool_shape] + out_shapes,
        in_specs=[smem] + [vmem] * (slots + 9 + TRACE_TABLES),
        out_specs=[vmem] * (3 + len(out_shapes)),
        compiler_params=params,
        name="first_step",
    )(place, spread, *got, *trace_wide, initial_state, pool, product, rest, hot, flux, lift_wide,
      send_list)
    messages = [
        lax.ppermute(message, "inst", [((i + rank) % ranks, i) for i in range(ranks)])
        for rank in range(1, ranks)
    ]
    got = exchange(outgoing, LAST_ORDER)
    base, factors = pl.pallas_call(
        last_base_kernel,
        out_shape=[wide_shape, factor_shape],
        in_specs=[vmem] * 8,
        out_specs=[vmem] * 2,
        scratch_shapes=chunks,
        compiler_params=params,
        cost_estimate=diag_cost,
        name="last_own_terms",
    )(partial, pool, diagonal_blocks, forcing, hot, flux, spread, lift_wide)
    state, base = pl.pallas_call(
        functools.partial(message_kernel, ranks),
        out_shape=[like(initial_state), wide_shape],
        in_specs=[vmem] * (ranks + 3),
        out_specs=[vmem] * 2,
        compiler_params=params,
        name="message_terms",
    )(partial, initial_state, base, entries, *messages)
    return pl.pallas_call(
        functools.partial(last_kernel, parts),
        out_shape=[like(initial_state), wide_shape],
        in_specs=[smem] + [vmem] * (slots + 5),
        out_specs=[pl.BlockSpec(memory_space=pl.ANY)] * 2,
        scratch_shapes=[
            pltpu.VMEM(initial_state.shape, BF16),
            pltpu.VMEM(initial_state.shape, F32),
            pltpu.SemaphoreType.DMA((2,)),
        ],
        compiler_params=params,
        name="last_step",
    )(place, *got, state, base, hot, factors, lift_wide)


def solution(mesh):
    return jax.shard_map(
        on_device,
        mesh=mesh,
        in_specs=(
            P("inst", "dom", None),
            P("inst", "dom", None),
            P("dom", None, None),
            P("dom", None),
            P("dom", None, None),
            P("dom", None),
            P(),
        ),
        out_specs=(P("inst", "dom", None), P("inst", "dom", None)),
        check_vma=False,
    )
```

```python
import functools
import math

import jax
import jax.numpy as jnp
import numpy as np
from jax import lax
from jax.experimental import pallas as pl
from jax.experimental.pallas import tpu as pltpu
from jax.sharding import PartitionSpec as P

FIELDS = 5
ORDER = 3
NODES = 64
FPTS = 16
NI = 8
REACH = 2
ITERS = 2


pseudo_step = 0.5
dissipation = 0.25


def gauss_legendre(count):
    points = []
    weights = []
    for i in range(count):
        where = math.cos(math.pi * (i + 0.75) / (count + 0.5))
        for sweep in range(100):
            before = 1.0
            value = where
            for j in range(2, count + 1):
                after = ((2 * j - 1) * where * value - (j - 1) * before) / j
                before = value
                value = after
            slope = count * (where * value - before) / (where * where - 1.0)
            where = where - value / slope
        before = 1.0
        value = where
        for j in range(2, count + 1):
            after = ((2 * j - 1) * where * value - (j - 1) * before) / j
            before = value
            value = after
        slope = count * (where * value - before) / (where * where - 1.0)
        points.append(where)
        weights.append(2.0 / ((1.0 - where * where) * slope * slope))
    return (np.array(points[::-1]), np.array(weights[::-1]))


def lagrange_at(points, where):
    values = np.ones(points.shape[0])
    for i in range(points.shape[0]):
        for j in range(points.shape[0]):
            if j != i:
                values[i] = values[i] * (where - points[j]) / (points[i] - points[j])
    return values


def tables(order, count):
    points, weights = gauss_legendre(order + 1)
    at_minus = lagrange_at(points, -1.0)
    at_plus = lagrange_at(points, 1.0)
    per_side = order + 1
    node_count = per_side**3
    face_points = per_side**2
    trace_table = np.zeros((node_count, 6 * face_points))
    lift_table = np.zeros((node_count, 6 * face_points))
    for k in range(per_side):
        for j in range(per_side):
            for i in range(per_side):
                node = i + per_side * j + per_side * per_side * k
                entries = [
                    (0, at_minus[i], j + per_side * k, weights[i]),
                    (1, at_plus[i], j + per_side * k, weights[i]),
                    (2, at_minus[j], i + per_side * k, weights[j]),
                    (3, at_plus[j], i + per_side * k, weights[j]),
                    (4, at_minus[k], i + per_side * j, weights[k]),
                    (5, at_plus[k], i + per_side * j, weights[k]),
                ]
                for face_index, factor, point, weight in entries:
                    trace_table[node, face_index * face_points + point] = factor
                    lift_table[node, face_index * face_points + point] = factor / weight
    spectral = np.zeros((count, count))
    second = np.zeros((count, count))
    for t in range(count):
        for s in range(count):
            if t != s:
                spectral[t, s] = 0.5 * (-1.0) ** (t - s + 1) / math.tan(math.pi * (t - s) / count)
                second[t, s] = -0.5 * (-1.0) ** (t - s) / math.sin(math.pi * (t - s) / count) ** 2
            else:
                second[t, s] = -(count * count + 2.0) / 12.0
    return (trace_table, lift_table, spectral, second)


LANE = 128
WIDE = FIELDS * NODES
FACES = 6
VMEM_LIMIT = 16 * 1024 * 1024
BF16 = jnp.bfloat16
F32 = jnp.float32
OFFSETS = list(range(-REACH, 0)) + list(range(1, REACH + 1))
FIRST_ORDER = (3, 1, 2, 0)
LAST_ORDER = (2, 1, 3, 0)


def wide_tables():
    trace_np, lift_np, spectral_np, second_np = tables(ORDER, NI)
    trace_wide = np.zeros((WIDE, FACES * LANE))
    lift_wide = np.zeros((FACES * LANE, WIDE))
    for c in range(FIELDS):
        rows = slice(c * NODES, (c + 1) * NODES)
        for f in range(FACES):
            cols = slice(f * LANE + c * FPTS, f * LANE + (c + 1) * FPTS)
            face = slice(f * FPTS, (f + 1) * FPTS)
            trace_wide[rows, cols] = trace_np[:, face]
            lift_wide[cols, rows] = lift_np[:, face].T
    return trace_wide, lift_wide, spectral_np[:, 0], second_np[:, 0]


def iotas(shape):
    return [lax.broadcasted_iota(jnp.int32, shape, axis) for axis in range(2)]


def one_hot(mask):
    return jnp.where(mask, 1.0, 0.0).astype(BF16)


def spread_table():
    row, col = iotas((LANE, FIELDS * LANE))
    inside = col % LANE < FIELDS * FPTS
    return one_hot(inside & (row == col // LANE * FPTS + col % FPTS))


def order_table():
    row, col = iotas((FIELDS * FIELDS * FPTS, FIELDS * LANE))
    place = col % LANE
    source = place // FPTS * FIELDS * FPTS + col // LANE * FPTS + col % FPTS
    return one_hot((place < FIELDS * FPTS) & (row == source))


def trace_pool(state, trace_wide, insts, elems):
    wide = jnp.dot(state, trace_wide, preferred_element_type=F32).astype(BF16)
    by_inst = []
    for t in range(insts):
        rows = wide[t * elems : (t + 1) * elems]
        by_inst.append(
            jnp.concatenate([rows[:, f * LANE : (f + 1) * LANE] for f in range(FACES)], 0)
        )
    return jnp.concatenate(by_inst, 1)


def swap_routes(ranks, parts):
    near = [[(p, p + 1) for p in range(first, parts - 1, 2)] for first in range(2)]
    far = [
        [(p + i, p + i + 2) for p in range(first, parts - 3, 4) for i in range(2)]
        for first in (0, 2)
    ]
    routes = []
    for pairs in near + far:
        met = {p for pair in pairs for p in pair}
        alone = [p for p in range(parts) if p not in met]
        idle = [(p, p + 1) for p in alone if p + 1 in alone]
        alone = [p for p in alone if p + 1 not in alone and p - 1 not in alone]
        swaps = [(r * parts + p, r * parts + q) for r in range(ranks) for p, q in pairs + idle]
        swaps += [(r * parts + p, (r ^ 1) * parts + p) for r in range(0, ranks, 2) for p in alone]
        routes.append(swaps + [(q, p) for p, q in swaps])
    return routes


def by_swap(place, by_offset):
    two_down, one_down, one_up, two_up = by_offset
    even = place % 2 == 0
    low = place // 2 % 2 == 0
    return [
        jnp.where(even, one_up, one_down),
        jnp.where(even, one_down, one_up),
        jnp.where(low, two_up, two_down),
        jnp.where(low, two_down, two_up),
    ]


def by_offset(place, blocks):
    even = place % 2 == 0
    low = place // 2 % 2 == 0
    return [
        jnp.where(low, blocks[3], blocks[2]),
        jnp.where(even, blocks[1], blocks[0]),
        jnp.where(even, blocks[0], blocks[1]),
        jnp.where(low, blocks[2], blocks[3]),
    ]


def fill_outgoing(pool, send, out_refs, place, elems):
    slots, capacity = send.shape
    rows, cols = iotas((FACES * elems, slots * capacity))
    ids = FACES * (rows % elems) + rows // elems
    wanted = jnp.concatenate([send[k : k + 1] for k in range(slots)], 1)
    out = lax.dot_general(
        one_hot(ids == wanted), pool, (((0,), (0,)), ((), ())), preferred_element_type=F32
    )
    blocks = by_swap(place, [out[k * capacity : (k + 1) * capacity] for k in range(slots)])
    for block, ref in zip(blocks, out_refs):
        ref[...] = block.astype(BF16)


def diagonal(states, diag, wide_ref, prod_ref, insts, elems):
    tall = insts * elems
    width = diag.shape[1]
    cuts = [(j, j * LANE, min((j + 1) * LANE, width)) for j in range(pl.cdiv(width, LANE))]
    for t in range(insts):
        rows = states[t].astype(F32)
        for j, low, high in cuts:
            first = j * tall + t * elems
            wide_ref[first : first + elems, 0 : high - low] = rows[:, low:high]
    for e in range(elems):
        rows = jnp.concatenate(
            [wide_ref[pl.ds(j * tall + e, insts, stride=elems), :] for j, low, high in cuts], 1
        )
        product = jnp.dot(rows[:, 0:width].astype(BF16), diag[e], preferred_element_type=F32)
        for j, low, high in cuts:
            chunk = product[:, low:high]
            if high - low < LANE:
                chunk = jnp.concatenate([chunk, jnp.zeros((insts, LANE - high + low), F32)], 1)
            prod_ref[pl.ds(j * tall + e, insts, stride=elems), :] = chunk
    return [
        jnp.concatenate(
            [
                prod_ref[j * tall + t * elems : j * tall + (t + 1) * elems, 0 : high - low]
                for j, low, high in cuts
            ],
            1,
        )
        for t in range(insts)
    ]


def flux_order(rows, order):
    per_face = FIELDS * FIELDS * FPTS
    by_face = jnp.concatenate(
        [rows[:, f * per_face : (f + 1) * per_face] for f in range(FACES)], 0
    )
    return jnp.dot(by_face, order, preferred_element_type=F32).astype(BF16)


def source_table(sources, elems, slots):
    faces = FACES * elems
    columns = lax.broadcasted_iota(jnp.int32, (elems, faces + slots), 1)
    ids = jnp.where(columns < faces, FACES * (columns % elems) + columns // elems, columns)
    hot = [jnp.where(sources[:, f : f + 1] == ids, 1.0, 0.0) for f in range(FACES)]
    return jnp.concatenate(hot, 0).astype(BF16)


def face_flux(picked, flux, spread, insts):
    count = picked.shape[0]
    stacked = jnp.concatenate([picked[:, t * LANE : (t + 1) * LANE] for t in range(insts)], 0)
    wide = jnp.dot(stacked, spread, preferred_element_type=F32)
    normal = []
    for t in range(insts):
        rows = wide[t * count : (t + 1) * count]
        summed = flux[:, 0:LANE] * rows[:, 0:LANE]
        for d in range(1, FIELDS):
            summed += flux[:, d * LANE : (d + 1) * LANE] * rows[:, d * LANE : (d + 1) * LANE]
        normal.append(summed.astype(BF16))
    return normal


def lift_faces(normal, lift, elems):
    rows = [
        jnp.concatenate([n[f * elems : (f + 1) * elems] for f in range(FACES)], 1) for n in normal
    ]
    return jnp.dot(jnp.concatenate(rows, 0), lift, preferred_element_type=F32)


def couple(entry_ref, states, t, shift, insts):
    summed = None
    for s in range(insts):
        d = (t - s + shift * insts) % NI
        term = entry_ref[d : d + 1, :] * states[s].astype(F32)
        summed = term if summed is None else summed + term
    return summed


def rotated(flux):
    place = lax.broadcasted_iota(jnp.int32, (flux.shape[0], LANE), 1) // FPTS
    blocks = []
    for k in range(LANE // FPTS):
        block = jnp.zeros((flux.shape[0], LANE), F32)
        for d in range(FIELDS):
            met = place == (d + k) % (LANE // FPTS)
            block = jnp.where(met, flux[:, d * LANE : (d + 1) * LANE], block)
        blocks.append(block)
    return jnp.concatenate(blocks, 1)


def slot_normal(blocks, factors, insts):
    count = blocks.shape[0]
    stacked = jnp.concatenate([blocks[:, t * LANE : (t + 1) * LANE] for t in range(insts)], 0)
    summed = [None] * insts
    for k in range(LANE // FPTS):
        turned = stacked if k == 0 else pltpu.roll(stacked, k * FPTS, 1)
        for t in range(insts):
            term = factors[:, k * LANE : (k + 1) * LANE] * turned[t * count : (t + 1) * count]
            summed[t] = term if k == 0 else summed[t] + term
    return [rows.astype(BF16) for rows in summed]


def table_kernel(spread_ref, order_ref):
    spread_ref[...] = spread_table()
    order_ref[...] = order_table()


def first_kernel(spectral, second, place_ref, freq_ref, spread_ref, state_ref, trace_ref, send_ref,
                 entry_ref, pool_ref, *out_refs):
    insts, elems, width = state_ref.shape
    state = state_ref[...].reshape(insts * elems, width)
    pool = trace_pool(state, trace_ref[...], insts, elems)
    pool_ref[...] = pool
    fill_outgoing(pool, send_ref[0], out_refs, place_ref[0], elems)
    freq = freq_ref[0]
    for d in range(NI):
        entry = freq * float(spectral[d]) - dissipation * float(second[d])
        entry_ref[d : d + 1, :] = jnp.full((1, width), entry, F32)


def local_lift(pool, hot, flux, spread, lift, insts, elems):
    empty = jnp.zeros((hot.shape[1] - pool.shape[0], pool.shape[1]), BF16)
    pool = jnp.concatenate([pool, empty], 0)
    picked = jnp.dot(hot, pool, preferred_element_type=F32).astype(BF16)
    normal = face_flux(picked, flux.astype(F32), spread, insts)
    return lift_faces(normal, lift, elems)


def slot_lift(blocks, factors, hot, lift, insts, elems):
    normal = slot_normal(blocks, factors, insts)
    empty = jnp.zeros((FACES * elems, insts * LANE), BF16)
    rows = jnp.concatenate([empty, jnp.concatenate(normal, 1)], 0)
    spots = jnp.dot(hot, rows, preferred_element_type=F32).astype(BF16)
    return lift_faces([spots[:, t * LANE : (t + 1) * LANE] for t in range(insts)], lift, elems)


def base_kernel(slots, state_ref, diag_ref, forcing_ref, entry_ref, pool_ref, flux_ref, source_ref,
                order_ref, spread_ref, lift_ref, spatial_ref, rest_ref, flux_out_ref, hot_ref,
                factor_ref, wide_ref, prod_ref):
    insts, elems, width = state_ref.shape
    hot = source_table(source_ref[...].T, elems, slots)
    flux = flux_order(flux_ref[...], order_ref[...])
    hot_ref[...] = hot
    flux_out_ref[...] = flux
    factors = lax.dot_general(hot, flux, (((0,), (0,)), ((), ())), preferred_element_type=F32)
    factor_ref[...] = rotated(factors[FACES * elems :])
    lifted = local_lift(pool_ref[...], hot, flux, spread_ref[...], lift_ref[...], insts, elems)
    states = [state_ref[t] for t in range(insts)]
    products = diagonal(states, diag_ref, wide_ref, prod_ref, insts, elems)
    for t in range(insts):
        spatial_ref[t] = products[t] + lifted[t * elems : (t + 1) * elems]
        rest_ref[t] = couple(entry_ref, states, t, 0, insts) - forcing_ref[t].astype(F32)


def last_base_kernel(state_ref, pool_ref, diag_ref, forcing_ref, hot_ref, flux_ref, spread_ref,
                     lift_ref, base_ref, wide_ref, prod_ref):
    insts, elems, width = state_ref.shape
    lifted = local_lift(
        pool_ref[...], hot_ref[...], flux_ref[...], spread_ref[...], lift_ref[...], insts, elems
    )
    states = [state_ref[t].astype(BF16) for t in range(insts)]
    products = diagonal(states, diag_ref, wide_ref, prod_ref, insts, elems)
    for t in range(insts):
        base_ref[t] = (
            products[t] + lifted[t * elems : (t + 1) * elems] - forcing_ref[t].astype(F32)
        )


def message_kernel(ranks, partial_ref, first_ref, base_ref, entry_ref, *refs):
    message_refs, (state_ref, out_ref) = refs[: ranks - 1], refs[ranks - 1 :]
    insts, elems, width = base_ref.shape
    firsts = [[first_ref[t] for t in range(insts)]]
    partials = [[partial_ref[t] for t in range(insts)]]
    for message_ref in message_refs:
        rows = [
            message_ref[i * elems : (i + 1) * elems, 0:width] for i in range(2 * insts)
        ]
        firsts.append(rows[:insts])
        partials.append(rows[insts:])
    states = []
    for k in range(ranks):
        of_rank = []
        for t in range(insts):
            state = partials[k][t].astype(F32)
            for j in range(ranks):
                if j != k:
                    state -= pseudo_step * couple(entry_ref, firsts[j], t, k - j, insts)
            of_rank.append(state.astype(BF16) if k == 0 else state)
        states.append(of_rank)
    for t in range(insts):
        state_ref[t] = states[0][t]
        coupling = base_ref[t]
        for k in range(ranks):
            coupling += couple(entry_ref, states[k], t, -k, insts)
        out_ref[t] = coupling


def received(parts, place, got_refs, order):
    got_refs = {swap: got_refs[i] for i, swap in enumerate(order)}
    arrived = by_offset(
        place, [got_refs[swap][...].astype(F32) for swap in range(len(OFFSETS))]
    )
    for k, offset in enumerate(OFFSETS):
        exists = (place + offset >= 0) & (place + offset < parts)
        arrived[k] = jnp.where(exists, arrived[k], jnp.zeros_like(arrived[k]))
    return jnp.concatenate(arrived, 0)


def step_kernel(parts, place_ref, *refs):
    got_refs, refs = refs[: len(OFFSETS)], refs[len(OFFSETS) :]
    (state_ref, local_ref, rest_ref, hot_ref, factor_ref, lift_ref, trace_ref, send_ref,
     partial_ref, message_ref, next_pool_ref, *out_refs) = refs
    insts, elems, width = state_ref.shape
    place = place_ref[0]
    blocks = received(parts, place, got_refs, FIRST_ORDER)
    lifted = slot_lift(blocks, factor_ref[...], hot_ref[...], lift_ref[...], insts, elems)
    message_ref[...] = jnp.zeros_like(message_ref)
    fresh = []
    for t in range(insts):
        spatial = local_ref[t] + lifted[t * elems : (t + 1) * elems]
        moved = state_ref[t].astype(F32) - pseudo_step * (spatial + rest_ref[t])
        partial_ref[t] = moved
        fresh.append(moved.astype(BF16))
        lean = (moved - pseudo_step * spatial).astype(BF16)
        for i, block in enumerate((state_ref[t], lean)):
            low = (i * insts + t) * elems
            message_ref[low : low + elems, 0:width] = block
    pool = trace_pool(jnp.concatenate(fresh, 0), trace_ref[...], insts, elems)
    next_pool_ref[...] = pool
    fill_outgoing(pool, send_ref[0], out_refs, place, elems)


def last_kernel(parts, place_ref, *refs):
    got_refs, refs = refs[: len(OFFSETS)], refs[len(OFFSETS) :]
    (state_ref, base_ref, hot_ref, factor_ref, lift_ref, final_hbm, residual_hbm,
     final_ref, residual_ref, sems) = refs
    insts, elems, width = state_ref.shape
    blocks = received(parts, place_ref[0], got_refs, LAST_ORDER)
    lifted = slot_lift(blocks, factor_ref[...], hot_ref[...], lift_ref[...], insts, elems)
    copies = []
    for t in range(insts):
        residual = base_ref[t] + lifted[t * elems : (t + 1) * elems]
        residual_ref[t] = residual
        final_ref[t] = (state_ref[t].astype(F32) - pseudo_step * residual).astype(BF16)
        copies += [
            pltpu.make_async_copy(residual_ref.at[t], residual_hbm.at[t], sems.at[0, t]),
            pltpu.make_async_copy(final_ref.at[t], final_hbm.at[t], sems.at[1, t]),
        ]
        copies[-2].start()
        copies[-1].start()
    for copy in copies:
        copy.wait()


def on_device(
    initial_state, forcing, diagonal_blocks, flux_jacobian, send_list, source_index, frequency
):
    insts, elems, width = initial_state.shape
    parts = lax.axis_size("dom")
    ranks = lax.axis_size("inst")
    slots, capacity = send_list.shape[1:]
    faces = FACES * elems
    trace_np, lift_np, spectral, second = wide_tables()
    trace_wide = jnp.asarray(trace_np, BF16)
    lift_wide = jnp.asarray(lift_np, BF16)
    place = lax.axis_index("dom").reshape(1)
    sources = source_index.T
    routes = swap_routes(ranks, parts)

    smem = pl.BlockSpec(memory_space=pltpu.SMEM)
    vmem = pl.BlockSpec(memory_space=pltpu.VMEM)
    params = pltpu.CompilerParams(vmem_limit_bytes=VMEM_LIMIT)

    def like(array):
        return jax.ShapeDtypeStruct(array.shape, array.dtype)

    wide_shape = jax.ShapeDtypeStruct(initial_state.shape, F32)
    pool_shape = jax.ShapeDtypeStruct((faces, insts * LANE), BF16)
    out_shapes = [jax.ShapeDtypeStruct((capacity, insts * LANE), BF16)] * slots
    flux_shape = jax.ShapeDtypeStruct((faces, FIELDS * LANE), BF16)
    hot_shape = jax.ShapeDtypeStruct((faces, faces + slots * capacity), BF16)
    factor_shape = jax.ShapeDtypeStruct((slots * capacity, LANE // FPTS * LANE), F32)

    def exchange(outgoing, order):
        return [
            lax.ppermute(outgoing[swap], ("inst", "dom"), routes[swap]) for swap in order
        ]

    entry_shape = jax.ShapeDtypeStruct((NI, width), F32)
    message_shape = jax.ShapeDtypeStruct((2 * insts * elems, pl.cdiv(width, LANE) * LANE), BF16)
    chunks = [pltpu.VMEM((pl.cdiv(width, LANE) * insts * elems, LANE), F32)] * 2
    diag_cost = pl.CostEstimate(
        flops=2 * insts * diagonal_blocks.size, bytes_accessed=2 * diagonal_blocks.size,
        transcendentals=0,
    )
    spread, order = pl.pallas_call(
        table_kernel,
        out_shape=[
            jax.ShapeDtypeStruct((LANE, FIELDS * LANE), BF16),
            jax.ShapeDtypeStruct((FIELDS * FIELDS * FPTS, FIELDS * LANE), BF16),
        ],
        out_specs=[vmem] * 2,
        compiler_params=params,
        cost_estimate=pl.CostEstimate(flops=10**10, bytes_accessed=10**6, transcendentals=0),
        name="tables",
    )()
    freq, _ = lax.optimization_barrier((frequency, spread))
    entries, pool, *outgoing = pl.pallas_call(
        functools.partial(first_kernel, spectral, second),
        out_shape=[entry_shape, pool_shape] + out_shapes,
        in_specs=[smem] * 2 + [vmem] * 4,
        out_specs=[vmem] * (2 + len(out_shapes)),
        compiler_params=params,
        cost_estimate=pl.CostEstimate(flops=10**10, bytes_accessed=10**6, transcendentals=0),
        name="first_traces",
    )(place, freq, spread, initial_state, trace_wide, send_list)
    got = exchange(outgoing, FIRST_ORDER)
    local, rest, flux, hot, factors = pl.pallas_call(
        functools.partial(base_kernel, slots * capacity),
        out_shape=[wide_shape] * 2 + [flux_shape, hot_shape, factor_shape],
        in_specs=[vmem] * 10,
        out_specs=[vmem] * 5,
        scratch_shapes=chunks,
        compiler_params=params,
        cost_estimate=diag_cost,
        name="own_terms",
    )(initial_state, diagonal_blocks, forcing, entries, pool, flux_jacobian, sources, order, spread,
      lift_wide)
    partial, message, pool, *outgoing = pl.pallas_call(
        functools.partial(step_kernel, parts),
        out_shape=[wide_shape, message_shape, pool_shape] + out_shapes,
        in_specs=[smem] + [vmem] * (slots + 8),
        out_specs=[vmem] * (3 + len(out_shapes)),
        compiler_params=params,
        name="first_step",
    )(place, *got, initial_state, local, rest, hot, factors, lift_wide, trace_wide, send_list)
    messages = [
        lax.ppermute(message, "inst", [((i + rank) % ranks, i) for i in range(ranks)])
        for rank in range(1, ranks)
    ]
    got = exchange(outgoing, LAST_ORDER)
    base = pl.pallas_call(
        last_base_kernel,
        out_shape=wide_shape,
        in_specs=[vmem] * 8,
        out_specs=vmem,
        scratch_shapes=chunks,
        compiler_params=params,
        cost_estimate=diag_cost,
        name="last_own_terms",
    )(partial, pool, diagonal_blocks, forcing, hot, flux, spread, lift_wide)
    state, base = pl.pallas_call(
        functools.partial(message_kernel, ranks),
        out_shape=[like(initial_state), wide_shape],
        in_specs=[vmem] * (ranks + 3),
        out_specs=[vmem] * 2,
        compiler_params=params,
        name="message_terms",
    )(partial, initial_state, base, entries, *messages)
    return pl.pallas_call(
        functools.partial(last_kernel, parts),
        out_shape=[like(initial_state), wide_shape],
        in_specs=[smem] + [vmem] * (slots + 5),
        out_specs=[pl.BlockSpec(memory_space=pl.ANY)] * 2,
        scratch_shapes=[
            pltpu.VMEM(initial_state.shape, BF16),
            pltpu.VMEM(initial_state.shape, F32),
            pltpu.SemaphoreType.DMA((2, insts)),
        ],
        compiler_params=params,
        name="last_step",
    )(place, *got, state, base, hot, factors, lift_wide)


def solution(mesh):
    return jax.shard_map(
        on_device,
        mesh=mesh,
        in_specs=(
            P("inst", "dom", None),
            P("inst", "dom", None),
            P("dom", None, None),
            P("dom", None),
            P("dom", None, None),
            P("dom", None),
            P(),
        ),
        out_specs=(P("inst", "dom", None), P("inst", "dom", None)),
        check_vma=False,
    )
```

```python
import functools
import math

import jax
import jax.numpy as jnp
import numpy as np
from jax import lax
from jax.experimental import pallas as pl
from jax.experimental.pallas import tpu as pltpu
from jax.sharding import PartitionSpec as P

FIELDS = 5
ORDER = 3
NODES = 64
FPTS = 16
NI = 8
REACH = 2
ITERS = 2


pseudo_step = 0.5
dissipation = 0.25


def gauss_legendre(count):
    points = []
    weights = []
    for i in range(count):
        where = math.cos(math.pi * (i + 0.75) / (count + 0.5))
        for sweep in range(100):
            before = 1.0
            value = where
            for j in range(2, count + 1):
                after = ((2 * j - 1) * where * value - (j - 1) * before) / j
                before = value
                value = after
            slope = count * (where * value - before) / (where * where - 1.0)
            where = where - value / slope
        before = 1.0
        value = where
        for j in range(2, count + 1):
            after = ((2 * j - 1) * where * value - (j - 1) * before) / j
            before = value
            value = after
        slope = count * (where * value - before) / (where * where - 1.0)
        points.append(where)
        weights.append(2.0 / ((1.0 - where * where) * slope * slope))
    return (np.array(points[::-1]), np.array(weights[::-1]))


def lagrange_at(points, where):
    values = np.ones(points.shape[0])
    for i in range(points.shape[0]):
        for j in range(points.shape[0]):
            if j != i:
                values[i] = values[i] * (where - points[j]) / (points[i] - points[j])
    return values


def tables(order, count):
    points, weights = gauss_legendre(order + 1)
    at_minus = lagrange_at(points, -1.0)
    at_plus = lagrange_at(points, 1.0)
    per_side = order + 1
    node_count = per_side**3
    face_points = per_side**2
    trace_table = np.zeros((node_count, 6 * face_points))
    lift_table = np.zeros((node_count, 6 * face_points))
    for k in range(per_side):
        for j in range(per_side):
            for i in range(per_side):
                node = i + per_side * j + per_side * per_side * k
                entries = [
                    (0, at_minus[i], j + per_side * k, weights[i]),
                    (1, at_plus[i], j + per_side * k, weights[i]),
                    (2, at_minus[j], i + per_side * k, weights[j]),
                    (3, at_plus[j], i + per_side * k, weights[j]),
                    (4, at_minus[k], i + per_side * j, weights[k]),
                    (5, at_plus[k], i + per_side * j, weights[k]),
                ]
                for face_index, factor, point, weight in entries:
                    trace_table[node, face_index * face_points + point] = factor
                    lift_table[node, face_index * face_points + point] = factor / weight
    spectral = np.zeros((count, count))
    second = np.zeros((count, count))
    for t in range(count):
        for s in range(count):
            if t != s:
                spectral[t, s] = 0.5 * (-1.0) ** (t - s + 1) / math.tan(math.pi * (t - s) / count)
                second[t, s] = -0.5 * (-1.0) ** (t - s) / math.sin(math.pi * (t - s) / count) ** 2
            else:
                second[t, s] = -(count * count + 2.0) / 12.0
    return (trace_table, lift_table, spectral, second)


LANE = 128
WIDE = FIELDS * NODES
FACES = 6
TRACE_TABLES = 3
VMEM_LIMIT = 16 * 1024 * 1024
BF16 = jnp.bfloat16
F32 = jnp.float32
OFFSETS = list(range(-REACH, 0)) + list(range(1, REACH + 1))
FIRST_ORDER = (3, 1, 2, 0)
LAST_ORDER = (2, 1, 3, 0)


def wide_tables():
    trace_np, lift_np, spectral_np, second_np = tables(ORDER, NI)
    trace_wide = np.zeros((WIDE, FACES * LANE))
    lift_wide = np.zeros((FACES * LANE, WIDE))
    for c in range(FIELDS):
        rows = slice(c * NODES, (c + 1) * NODES)
        for f in range(FACES):
            cols = slice(f * LANE + c * FPTS, f * LANE + (c + 1) * FPTS)
            face = slice(f * FPTS, (f + 1) * FPTS)
            trace_wide[rows, cols] = trace_np[:, face]
            lift_wide[cols, rows] = lift_np[:, face].T
    return trace_wide, lift_wide, spectral_np[:, 0], second_np[:, 0]


def iotas(shape):
    return [lax.broadcasted_iota(jnp.int32, shape, axis) for axis in range(2)]


def one_hot(mask):
    return jnp.where(mask, 1.0, 0.0).astype(BF16)


def spread_table():
    row, col = iotas((LANE, FIELDS * LANE))
    inside = col % LANE < FIELDS * FPTS
    return one_hot(inside & (row == col // LANE * FPTS + col % FPTS))


def order_table():
    row, col = iotas((FIELDS * FIELDS * FPTS, FIELDS * LANE))
    place = col % LANE
    source = place // FPTS * FIELDS * FPTS + col // LANE * FPTS + col % FPTS
    return one_hot((place < FIELDS * FPTS) & (row == source))


def trace_pool(state, trace_tables, insts, elems):
    faces = []
    for table in trace_tables:
        wide = jnp.dot(state, table, preferred_element_type=F32).astype(BF16)
        faces += [wide[:, at : at + LANE] for at in range(0, table.shape[1], LANE)]
    by_inst = []
    for t in range(insts):
        by_inst.append(jnp.concatenate([rows[t * elems : (t + 1) * elems] for rows in faces], 0))
    return jnp.concatenate(by_inst, 1)


def swap_routes(ranks, parts):
    near = [[(p, p + 1) for p in range(first, parts - 1, 2)] for first in range(2)]
    far = [
        [(p + i, p + i + 2) for p in range(first, parts - 3, 4) for i in range(2)]
        for first in (0, 2)
    ]
    routes = []
    for pairs in near + far:
        met = {p for pair in pairs for p in pair}
        alone = [p for p in range(parts) if p not in met]
        idle = []
        for p in list(alone):
            if p in alone and p + 1 in alone:
                idle.append((p, p + 1))
                alone = [q for q in alone if q not in idle[-1]]
        swaps = [(r * parts + p, r * parts + q) for r in range(ranks) for p, q in pairs + idle]
        swaps += [(r * parts + p, (r ^ 1) * parts + p) for r in range(0, ranks, 2) for p in alone]
        routes.append(swaps + [(q, p) for p, q in swaps])
    return routes


def by_swap(place, by_offset):
    two_down, one_down, one_up, two_up = by_offset
    even = place % 2 == 0
    low = place // 2 % 2 == 0
    return [
        jnp.where(even, one_up, one_down),
        jnp.where(even, one_down, one_up),
        jnp.where(low, two_up, two_down),
        jnp.where(low, two_down, two_up),
    ]


def by_offset(place, blocks):
    even = place % 2 == 0
    low = place // 2 % 2 == 0
    return [
        jnp.where(low, blocks[3], blocks[2]),
        jnp.where(even, blocks[1], blocks[0]),
        jnp.where(even, blocks[0], blocks[1]),
        jnp.where(low, blocks[2], blocks[3]),
    ]


def fill_outgoing(pool, send, out_refs, place, elems):
    slots, capacity = send.shape
    rows, cols = iotas((FACES * elems, slots * capacity))
    ids = FACES * (rows % elems) + rows // elems
    wanted = jnp.concatenate([send[k : k + 1] for k in range(slots)], 1)
    out = lax.dot_general(
        one_hot(ids == wanted), pool, (((0,), (0,)), ((), ())), preferred_element_type=F32
    )
    blocks = by_swap(place, [out[k * capacity : (k + 1) * capacity] for k in range(slots)])
    for block, ref in zip(blocks, out_refs):
        ref[...] = block.astype(BF16)


def diagonal(states, diag, wide_ref, prod_ref, insts, elems):
    tall = insts * elems
    width = diag.shape[1]
    cuts = [(j, j * LANE, min((j + 1) * LANE, width)) for j in range(pl.cdiv(width, LANE))]
    for t in range(insts):
        rows = states[t].astype(F32)
        for j, low, high in cuts:
            first = j * tall + t * elems
            wide_ref[first : first + elems, 0 : high - low] = rows[:, low:high]
    for e in range(elems):
        rows = jnp.concatenate(
            [wide_ref[pl.ds(j * tall + e, insts, stride=elems), :] for j, low, high in cuts], 1
        )
        product = jnp.dot(rows[:, 0:width].astype(BF16), diag[e], preferred_element_type=F32)
        for j, low, high in cuts:
            chunk = product[:, low:high]
            if high - low < LANE:
                chunk = jnp.concatenate([chunk, jnp.zeros((insts, LANE - high + low), F32)], 1)
            prod_ref[pl.ds(j * tall + e, insts, stride=elems), :] = chunk
    return [
        jnp.concatenate(
            [
                prod_ref[j * tall + t * elems : j * tall + (t + 1) * elems, 0 : high - low]
                for j, low, high in cuts
            ],
            1,
        )
        for t in range(insts)
    ]


def flux_order(rows, order):
    per_face = FIELDS * FIELDS * FPTS
    by_face = jnp.concatenate(
        [rows[:, f * per_face : (f + 1) * per_face] for f in range(FACES)], 0
    )
    return jnp.dot(by_face, order, preferred_element_type=F32).astype(BF16)


def source_table(sources, elems, slots):
    faces = FACES * elems
    columns = lax.broadcasted_iota(jnp.int32, (elems, faces + slots), 1)
    ids = jnp.where(columns < faces, FACES * (columns % elems) + columns // elems, columns)
    hot = [jnp.where(sources[:, f : f + 1] == ids, 1.0, 0.0) for f in range(FACES)]
    return jnp.concatenate(hot, 0).astype(BF16)


def face_flux(picked, flux, spread, insts):
    count = picked.shape[0]
    stacked = jnp.concatenate([picked[:, t * LANE : (t + 1) * LANE] for t in range(insts)], 0)
    wide = jnp.dot(stacked, spread, preferred_element_type=F32)
    normal = []
    for t in range(insts):
        rows = wide[t * count : (t + 1) * count]
        summed = flux[:, 0:LANE] * rows[:, 0:LANE]
        for d in range(1, FIELDS):
            summed += flux[:, d * LANE : (d + 1) * LANE] * rows[:, d * LANE : (d + 1) * LANE]
        normal.append(summed.astype(BF16))
    return normal


def lift_faces(normal, lift, elems):
    rows = [
        jnp.concatenate([n[f * elems : (f + 1) * elems] for f in range(FACES)], 1) for n in normal
    ]
    return jnp.dot(jnp.concatenate(rows, 0), lift, preferred_element_type=F32)


def couple(entry_ref, states, t, shift, insts):
    summed = None
    for s in range(insts):
        d = (t - s + shift * insts) % NI
        term = entry_ref[d : d + 1, :] * states[s].astype(F32)
        summed = term if summed is None else summed + term
    return summed


def rotated(flux):
    place = lax.broadcasted_iota(jnp.int32, (flux.shape[0], LANE), 1) // FPTS
    blocks = []
    for k in range(LANE // FPTS):
        block = jnp.zeros((flux.shape[0], LANE), F32)
        for d in range(FIELDS):
            met = place == (d + k) % (LANE // FPTS)
            block = jnp.where(met, flux[:, d * LANE : (d + 1) * LANE], block)
        blocks.append(block)
    return jnp.concatenate(blocks, 1)


def slot_normal(blocks, factors, insts):
    count = blocks.shape[0]
    stacked = jnp.concatenate([blocks[:, t * LANE : (t + 1) * LANE] for t in range(insts)], 0)
    summed = [None] * insts
    for k in range(LANE // FPTS):
        turned = stacked if k == 0 else pltpu.roll(stacked, k * FPTS, 1)
        for t in range(insts):
            term = factors[:, k * LANE : (k + 1) * LANE] * turned[t * count : (t + 1) * count]
            summed[t] = term if k == 0 else summed[t] + term
    return [rows.astype(BF16) for rows in summed]


def table_kernel(spread_ref, order_ref):
    spread_ref[...] = spread_table()
    order_ref[...] = order_table()


def first_kernel(spectral, second, place_ref, freq_ref, spread_ref, state_ref, send_ref, *refs):
    insts, elems, width = state_ref.shape
    trace_refs, (entry_ref, pool_ref, *out_refs) = refs[:TRACE_TABLES], refs[TRACE_TABLES:]
    state = state_ref[...].reshape(insts * elems, width)
    pool = trace_pool(state, [ref[...] for ref in trace_refs], insts, elems)
    pool_ref[...] = pool
    fill_outgoing(pool, send_ref[0], out_refs, place_ref[0], elems)
    freq = freq_ref[0]
    for d in range(NI):
        entry = freq * float(spectral[d]) - dissipation * float(second[d])
        entry_ref[d : d + 1, :] = jnp.full((1, width), entry, F32)


def local_lift(pool, hot, flux, spread, lift, insts, elems):
    empty = jnp.zeros((hot.shape[1] - pool.shape[0], pool.shape[1]), BF16)
    pool = jnp.concatenate([pool, empty], 0)
    picked = jnp.dot(hot, pool, preferred_element_type=F32).astype(BF16)
    normal = face_flux(picked, flux.astype(F32), spread, insts)
    return lift_faces(normal, lift, elems)


def slot_lift(blocks, factors, hot, lift, insts, elems):
    normal = slot_normal(blocks, factors, insts)
    empty = jnp.zeros((FACES * elems, insts * LANE), BF16)
    rows = jnp.concatenate([empty, jnp.concatenate(normal, 1)], 0)
    spots = jnp.dot(hot, rows, preferred_element_type=F32).astype(BF16)
    return lift_faces([spots[:, t * LANE : (t + 1) * LANE] for t in range(insts)], lift, elems)


def base_kernel(slots, state_ref, diag_ref, forcing_ref, entry_ref, pool_ref, flux_ref, source_ref,
                order_ref, spread_ref, lift_ref, spatial_ref, rest_ref, flux_out_ref, hot_ref,
                factor_ref, wide_ref, prod_ref):
    insts, elems, width = state_ref.shape
    hot = source_table(source_ref[...].T, elems, slots)
    flux = flux_order(flux_ref[...], order_ref[...])
    hot_ref[...] = hot
    flux_out_ref[...] = flux
    factors = lax.dot_general(hot, flux, (((0,), (0,)), ((), ())), preferred_element_type=F32)
    factor_ref[...] = rotated(factors[FACES * elems :])
    lifted = local_lift(pool_ref[...], hot, flux, spread_ref[...], lift_ref[...], insts, elems)
    states = [state_ref[t] for t in range(insts)]
    products = diagonal(states, diag_ref, wide_ref, prod_ref, insts, elems)
    for t in range(insts):
        spatial_ref[t] = products[t] + lifted[t * elems : (t + 1) * elems]
        rest_ref[t] = couple(entry_ref, states, t, 0, insts) - forcing_ref[t].astype(F32)


def last_base_kernel(state_ref, pool_ref, diag_ref, forcing_ref, hot_ref, flux_ref, spread_ref,
                     lift_ref, base_ref, wide_ref, prod_ref):
    insts, elems, width = state_ref.shape
    lifted = local_lift(
        pool_ref[...], hot_ref[...], flux_ref[...], spread_ref[...], lift_ref[...], insts, elems
    )
    states = [state_ref[t].astype(BF16) for t in range(insts)]
    products = diagonal(states, diag_ref, wide_ref, prod_ref, insts, elems)
    for t in range(insts):
        base_ref[t] = (
            products[t] + lifted[t * elems : (t + 1) * elems] - forcing_ref[t].astype(F32)
        )


def message_kernel(ranks, partial_ref, first_ref, base_ref, entry_ref, *refs):
    message_refs, (state_ref, out_ref) = refs[: ranks - 1], refs[ranks - 1 :]
    insts, elems, width = base_ref.shape
    firsts = [[first_ref[t] for t in range(insts)]]
    partials = [[partial_ref[t] for t in range(insts)]]
    for message_ref in message_refs:
        rows = [
            message_ref[i * elems : (i + 1) * elems, 0:width] for i in range(2 * insts)
        ]
        firsts.append(rows[:insts])
        partials.append(rows[insts:])
    states = []
    for k in range(ranks):
        of_rank = []
        for t in range(insts):
            state = partials[k][t].astype(F32)
            for j in range(ranks):
                if j != k:
                    state -= pseudo_step * couple(entry_ref, firsts[j], t, k - j, insts)
            of_rank.append(state.astype(BF16) if k == 0 else state)
        states.append(of_rank)
    for t in range(insts):
        state_ref[t] = states[0][t]
        coupling = base_ref[t]
        for k in range(ranks):
            coupling += couple(entry_ref, states[k], t, -k, insts)
        out_ref[t] = coupling


def received(parts, place, got_refs, order):
    got_refs = {swap: got_refs[i] for i, swap in enumerate(order)}
    arrived = by_offset(
        place, [got_refs[swap][...].astype(F32) for swap in range(len(OFFSETS))]
    )
    for k, offset in enumerate(OFFSETS):
        exists = (place + offset >= 0) & (place + offset < parts)
        arrived[k] = jnp.where(exists, arrived[k], jnp.zeros_like(arrived[k]))
    return jnp.concatenate(arrived, 0)


def step_kernel(parts, place_ref, *refs):
    got_refs, refs = refs[: len(OFFSETS)], refs[len(OFFSETS) :]
    trace_refs, refs = refs[:TRACE_TABLES], refs[TRACE_TABLES:]
    (state_ref, local_ref, rest_ref, hot_ref, factor_ref, lift_ref, send_ref,
     partial_ref, message_ref, next_pool_ref, *out_refs) = refs
    insts, elems, width = state_ref.shape
    place = place_ref[0]
    blocks = received(parts, place, got_refs, FIRST_ORDER)
    lifted = slot_lift(blocks, factor_ref[...], hot_ref[...], lift_ref[...], insts, elems)
    message_ref[...] = jnp.zeros_like(message_ref)
    fresh = []
    for t in range(insts):
        spatial = local_ref[t] + lifted[t * elems : (t + 1) * elems]
        moved = state_ref[t].astype(F32) - pseudo_step * (spatial + rest_ref[t])
        partial_ref[t] = moved
        fresh.append(moved.astype(BF16))
        lean = (moved - pseudo_step * spatial).astype(BF16)
        for i, block in enumerate((state_ref[t], lean)):
            low = (i * insts + t) * elems
            message_ref[low : low + elems, 0:width] = block
    tables_of_traces = [ref[...] for ref in trace_refs]
    pool = trace_pool(jnp.concatenate(fresh, 0), tables_of_traces, insts, elems)
    next_pool_ref[...] = pool
    fill_outgoing(pool, send_ref[0], out_refs, place, elems)


def last_kernel(parts, place_ref, *refs):
    got_refs, refs = refs[: len(OFFSETS)], refs[len(OFFSETS) :]
    (state_ref, base_ref, hot_ref, factor_ref, lift_ref, final_hbm, residual_hbm,
     final_ref, residual_ref, sems) = refs
    insts, elems, width = state_ref.shape
    blocks = received(parts, place_ref[0], got_refs, LAST_ORDER)
    lifted = slot_lift(blocks, factor_ref[...], hot_ref[...], lift_ref[...], insts, elems)
    for t in range(insts):
        residual = base_ref[t] + lifted[t * elems : (t + 1) * elems]
        residual_ref[t] = residual
        final_ref[t] = (state_ref[t].astype(F32) - pseudo_step * residual).astype(BF16)
    copies = [
        pltpu.make_async_copy(residual_ref, residual_hbm, sems.at[0]),
        pltpu.make_async_copy(final_ref, final_hbm, sems.at[1]),
    ]
    for copy in copies:
        copy.start()
    for copy in copies:
        copy.wait()


def on_device(
    initial_state, forcing, diagonal_blocks, flux_jacobian, send_list, source_index, frequency
):
    insts, elems, width = initial_state.shape
    parts = lax.axis_size("dom")
    ranks = lax.axis_size("inst")
    slots, capacity = send_list.shape[1:]
    faces = FACES * elems
    trace_np, lift_np, spectral, second = wide_tables()
    trace_wide = [jnp.asarray(part, BF16) for part in np.split(trace_np, TRACE_TABLES, 1)]
    lift_wide = jnp.asarray(lift_np, BF16)
    place = lax.axis_index("dom").reshape(1)
    sources = source_index.T
    routes = swap_routes(ranks, parts)

    smem = pl.BlockSpec(memory_space=pltpu.SMEM)
    vmem = pl.BlockSpec(memory_space=pltpu.VMEM)
    params = pltpu.CompilerParams(vmem_limit_bytes=VMEM_LIMIT)

    def like(array):
        return jax.ShapeDtypeStruct(array.shape, array.dtype)

    wide_shape = jax.ShapeDtypeStruct(initial_state.shape, F32)
    pool_shape = jax.ShapeDtypeStruct((faces, insts * LANE), BF16)
    out_shapes = [jax.ShapeDtypeStruct((capacity, insts * LANE), BF16)] * slots
    flux_shape = jax.ShapeDtypeStruct((faces, FIELDS * LANE), BF16)
    hot_shape = jax.ShapeDtypeStruct((faces, faces + slots * capacity), BF16)
    factor_shape = jax.ShapeDtypeStruct((slots * capacity, LANE // FPTS * LANE), F32)

    def exchange(outgoing, order):
        return [
            lax.ppermute(outgoing[swap], ("inst", "dom"), routes[swap]) for swap in order
        ]

    entry_shape = jax.ShapeDtypeStruct((NI, width), F32)
    message_shape = jax.ShapeDtypeStruct((2 * insts * elems, pl.cdiv(width, LANE) * LANE), BF16)
    chunks = [pltpu.VMEM((pl.cdiv(width, LANE) * insts * elems, LANE), F32)] * 2
    diag_cost = pl.CostEstimate(
        flops=2 * insts * diagonal_blocks.size, bytes_accessed=2 * diagonal_blocks.size,
        transcendentals=0,
    )
    spread, order = pl.pallas_call(
        table_kernel,
        out_shape=[
            jax.ShapeDtypeStruct((LANE, FIELDS * LANE), BF16),
            jax.ShapeDtypeStruct((FIELDS * FIELDS * FPTS, FIELDS * LANE), BF16),
        ],
        out_specs=[vmem] * 2,
        compiler_params=params,
        cost_estimate=pl.CostEstimate(flops=10**10, bytes_accessed=10**6, transcendentals=0),
        name="tables",
    )()
    freq, _ = lax.optimization_barrier((frequency, spread))
    entries, pool, *outgoing = pl.pallas_call(
        functools.partial(first_kernel, spectral, second),
        out_shape=[entry_shape, pool_shape] + out_shapes,
        in_specs=[smem] * 2 + [vmem] * (3 + TRACE_TABLES),
        out_specs=[vmem] * (2 + len(out_shapes)),
        compiler_params=params,
        cost_estimate=pl.CostEstimate(flops=10**10, bytes_accessed=10**6, transcendentals=0),
        name="first_traces",
    )(place, freq, spread, initial_state, send_list, *trace_wide)
    got = exchange(outgoing, FIRST_ORDER)
    local, rest, flux, hot, factors = pl.pallas_call(
        functools.partial(base_kernel, slots * capacity),
        out_shape=[wide_shape] * 2 + [flux_shape, hot_shape, factor_shape],
        in_specs=[vmem] * 10,
        out_specs=[vmem] * 5,
        scratch_shapes=chunks,
        compiler_params=params,
        cost_estimate=diag_cost,
        name="own_terms",
    )(initial_state, diagonal_blocks, forcing, entries, pool, flux_jacobian, sources, order, spread,
      lift_wide)
    partial, message, pool, *outgoing = pl.pallas_call(
        functools.partial(step_kernel, parts),
        out_shape=[wide_shape, message_shape, pool_shape] + out_shapes,
        in_specs=[smem] + [vmem] * (slots + 7 + TRACE_TABLES),
        out_specs=[vmem] * (3 + len(out_shapes)),
        compiler_params=params,
        name="first_step",
    )(place, *got, *trace_wide, initial_state, local, rest, hot, factors, lift_wide, send_list)
    messages = [
        lax.ppermute(message, "inst", [((i + rank) % ranks, i) for i in range(ranks)])
        for rank in range(1, ranks)
    ]
    got = exchange(outgoing, LAST_ORDER)
    base = pl.pallas_call(
        last_base_kernel,
        out_shape=wide_shape,
        in_specs=[vmem] * 8,
        out_specs=vmem,
        scratch_shapes=chunks,
        compiler_params=params,
        cost_estimate=diag_cost,
        name="last_own_terms",
    )(partial, pool, diagonal_blocks, forcing, hot, flux, spread, lift_wide)
    state, base = pl.pallas_call(
        functools.partial(message_kernel, ranks),
        out_shape=[like(initial_state), wide_shape],
        in_specs=[vmem] * (ranks + 3),
        out_specs=[vmem] * 2,
        compiler_params=params,
        name="message_terms",
    )(partial, initial_state, base, entries, *messages)
    return pl.pallas_call(
        functools.partial(last_kernel, parts),
        out_shape=[like(initial_state), wide_shape],
        in_specs=[smem] + [vmem] * (slots + 5),
        out_specs=[pl.BlockSpec(memory_space=pl.ANY)] * 2,
        scratch_shapes=[
            pltpu.VMEM(initial_state.shape, BF16),
            pltpu.VMEM(initial_state.shape, F32),
            pltpu.SemaphoreType.DMA((2,)),
        ],
        compiler_params=params,
        name="last_step",
    )(place, *got, state, base, hot, factors, lift_wide)


def solution(mesh):
    return jax.shard_map(
        on_device,
        mesh=mesh,
        in_specs=(
            P("inst", "dom", None),
            P("inst", "dom", None),
            P("dom", None, None),
            P("dom", None),
            P("dom", None, None),
            P("dom", None),
            P(),
        ),
        out_specs=(P("inst", "dom", None), P("inst", "dom", None)),
        check_vma=False,
    )
```

```python
import functools
import math

import jax
import jax.numpy as jnp
import numpy as np
from jax import lax
from jax.experimental import pallas as pl
from jax.experimental.pallas import tpu as pltpu
from jax.sharding import PartitionSpec as P

FIELDS = 5
ORDER = 3
NODES = 64
FPTS = 16
NI = 8
REACH = 2
ITERS = 2


pseudo_step = 0.5
dissipation = 0.25


def gauss_legendre(count):
    points = []
    weights = []
    for i in range(count):
        where = math.cos(math.pi * (i + 0.75) / (count + 0.5))
        for sweep in range(100):
            before = 1.0
            value = where
            for j in range(2, count + 1):
                after = ((2 * j - 1) * where * value - (j - 1) * before) / j
                before = value
                value = after
            slope = count * (where * value - before) / (where * where - 1.0)
            where = where - value / slope
        before = 1.0
        value = where
        for j in range(2, count + 1):
            after = ((2 * j - 1) * where * value - (j - 1) * before) / j
            before = value
            value = after
        slope = count * (where * value - before) / (where * where - 1.0)
        points.append(where)
        weights.append(2.0 / ((1.0 - where * where) * slope * slope))
    return (np.array(points[::-1]), np.array(weights[::-1]))


def lagrange_at(points, where):
    values = np.ones(points.shape[0])
    for i in range(points.shape[0]):
        for j in range(points.shape[0]):
            if j != i:
                values[i] = values[i] * (where - points[j]) / (points[i] - points[j])
    return values


def tables(order, count):
    points, weights = gauss_legendre(order + 1)
    at_minus = lagrange_at(points, -1.0)
    at_plus = lagrange_at(points, 1.0)
    per_side = order + 1
    node_count = per_side**3
    face_points = per_side**2
    trace_table = np.zeros((node_count, 6 * face_points))
    lift_table = np.zeros((node_count, 6 * face_points))
    for k in range(per_side):
        for j in range(per_side):
            for i in range(per_side):
                node = i + per_side * j + per_side * per_side * k
                entries = [
                    (0, at_minus[i], j + per_side * k, weights[i]),
                    (1, at_plus[i], j + per_side * k, weights[i]),
                    (2, at_minus[j], i + per_side * k, weights[j]),
                    (3, at_plus[j], i + per_side * k, weights[j]),
                    (4, at_minus[k], i + per_side * j, weights[k]),
                    (5, at_plus[k], i + per_side * j, weights[k]),
                ]
                for face_index, factor, point, weight in entries:
                    trace_table[node, face_index * face_points + point] = factor
                    lift_table[node, face_index * face_points + point] = factor / weight
    spectral = np.zeros((count, count))
    second = np.zeros((count, count))
    for t in range(count):
        for s in range(count):
            if t != s:
                spectral[t, s] = 0.5 * (-1.0) ** (t - s + 1) / math.tan(math.pi * (t - s) / count)
                second[t, s] = -0.5 * (-1.0) ** (t - s) / math.sin(math.pi * (t - s) / count) ** 2
            else:
                second[t, s] = -(count * count + 2.0) / 12.0
    return (trace_table, lift_table, spectral, second)


LANE = 128
WIDE = FIELDS * NODES
FACES = 6
TRACE_TABLES = 3
VMEM_LIMIT = 16 * 1024 * 1024
BF16 = jnp.bfloat16
F32 = jnp.float32
OFFSETS = list(range(-REACH, 0)) + list(range(1, REACH + 1))
FIRST_ORDER = (3, 1, 2, 0)
LAST_ORDER = (2, 1, 3, 0)


def wide_tables():
    trace_np, lift_np, spectral_np, second_np = tables(ORDER, NI)
    trace_wide = np.zeros((WIDE, FACES * LANE))
    lift_wide = np.zeros((FACES * LANE, WIDE))
    for c in range(FIELDS):
        rows = slice(c * NODES, (c + 1) * NODES)
        for f in range(FACES):
            cols = slice(f * LANE + c * FPTS, f * LANE + (c + 1) * FPTS)
            face = slice(f * FPTS, (f + 1) * FPTS)
            trace_wide[rows, cols] = trace_np[:, face]
            lift_wide[cols, rows] = lift_np[:, face].T
    return trace_wide, lift_wide, spectral_np[:, 0], second_np[:, 0]


def iotas(shape):
    return [lax.broadcasted_iota(jnp.int32, shape, axis) for axis in range(2)]


def one_hot(mask):
    return jnp.where(mask, 1.0, 0.0).astype(BF16)


def spread_table():
    row, col = iotas((LANE, FIELDS * LANE))
    inside = col % LANE < FIELDS * FPTS
    return one_hot(inside & (row == col // LANE * FPTS + col % FPTS))


def order_table():
    row, col = iotas((FIELDS * FIELDS * FPTS, FIELDS * LANE))
    place = col % LANE
    source = place // FPTS * FIELDS * FPTS + col // LANE * FPTS + col % FPTS
    return one_hot((place < FIELDS * FPTS) & (row == source))


def trace_pool(state, trace_tables, insts, elems):
    faces = []
    for table in trace_tables:
        wide = jnp.dot(state, table, preferred_element_type=F32).astype(BF16)
        faces += [wide[:, at : at + LANE] for at in range(0, table.shape[1], LANE)]
    by_inst = []
    for t in range(insts):
        by_inst.append(jnp.concatenate([rows[t * elems : (t + 1) * elems] for rows in faces], 0))
    return jnp.concatenate(by_inst, 1)


def swap_routes(ranks, parts):
    near = [[(p, p + 1) for p in range(first, parts - 1, 2)] for first in range(2)]
    far = [
        [(p + i, p + i + 2) for p in range(first, parts - 3, 4) for i in range(2)]
        for first in (0, 2)
    ]
    routes = []
    for pairs in near + far:
        met = {p for pair in pairs for p in pair}
        alone = [p for p in range(parts) if p not in met]
        idle = []
        for p in list(alone):
            if p in alone and p + 1 in alone:
                idle.append((p, p + 1))
                alone = [q for q in alone if q not in idle[-1]]
        swaps = [(r * parts + p, r * parts + q) for r in range(ranks) for p, q in pairs + idle]
        swaps += [(r * parts + p, (r ^ 1) * parts + p) for r in range(0, ranks, 2) for p in alone]
        routes.append(swaps + [(q, p) for p, q in swaps])
    return routes


def by_swap(place, by_offset):
    two_down, one_down, one_up, two_up = by_offset
    even = place % 2 == 0
    low = place // 2 % 2 == 0
    return [
        jnp.where(even, one_up, one_down),
        jnp.where(even, one_down, one_up),
        jnp.where(low, two_up, two_down),
        jnp.where(low, two_down, two_up),
    ]


def by_offset(place, blocks):
    even = place % 2 == 0
    low = place // 2 % 2 == 0
    return [
        jnp.where(low, blocks[3], blocks[2]),
        jnp.where(even, blocks[1], blocks[0]),
        jnp.where(even, blocks[0], blocks[1]),
        jnp.where(low, blocks[2], blocks[3]),
    ]


def fill_outgoing(pool, send, out_refs, place, elems):
    slots, capacity = send.shape
    rows, cols = iotas((FACES * elems, slots * capacity))
    ids = FACES * (rows % elems) + rows // elems
    wanted = jnp.concatenate([send[k : k + 1] for k in range(slots)], 1)
    out = lax.dot_general(
        one_hot(ids == wanted), pool, (((0,), (0,)), ((), ())), preferred_element_type=F32
    )
    blocks = by_swap(place, [out[k * capacity : (k + 1) * capacity] for k in range(slots)])
    for block, ref in zip(blocks, out_refs):
        ref[...] = block.astype(BF16)


def diagonal_steps(states, diag, wide_ref, prod_ref, insts, elems):
    tall = insts * elems
    width = diag.shape[1]
    cuts = [(j, j * LANE, min((j + 1) * LANE, width)) for j in range(pl.cdiv(width, LANE))]
    for t in range(insts):
        rows = states[t].astype(F32)
        for j, low, high in cuts:
            first = j * tall + t * elems
            wide_ref[first : first + elems, 0 : high - low] = rows[:, low:high]

    def some(begin, end):
        for e in range(begin, end):
            rows = jnp.concatenate(
                [wide_ref[pl.ds(j * tall + e, insts, stride=elems), :] for j, low, high in cuts], 1
            )
            product = jnp.dot(rows[:, 0:width].astype(BF16), diag[e], preferred_element_type=F32)
            for j, low, high in cuts:
                chunk = product[:, low:high]
                if high - low < LANE:
                    empty = jnp.zeros((insts, LANE - high + low), F32)
                    chunk = jnp.concatenate([chunk, empty], 1)
                prod_ref[pl.ds(j * tall + e, insts, stride=elems), :] = chunk

    def collect():
        return [
            jnp.concatenate(
                [
                    prod_ref[j * tall + t * elems : j * tall + (t + 1) * elems, 0 : high - low]
                    for j, low, high in cuts
                ],
                1,
            )
            for t in range(insts)
        ]

    return some, collect


def flux_order(rows, order):
    per_face = FIELDS * FIELDS * FPTS
    by_face = jnp.concatenate(
        [rows[:, f * per_face : (f + 1) * per_face] for f in range(FACES)], 0
    )
    return jnp.dot(by_face, order, preferred_element_type=F32).astype(BF16)


def source_table(sources, elems, slots):
    faces = FACES * elems
    columns = lax.broadcasted_iota(jnp.int32, (elems, faces + slots), 1)
    ids = jnp.where(columns < faces, FACES * (columns % elems) + columns // elems, columns)
    hot = [jnp.where(sources[:, f : f + 1] == ids, 1.0, 0.0) for f in range(FACES)]
    return jnp.concatenate(hot, 0).astype(BF16)


def spread_flux(wide, flux, insts):
    count = flux.shape[0]
    normal = []
    for t in range(insts):
        rows = wide[t * count : (t + 1) * count]
        summed = flux[:, 0:LANE] * rows[:, 0:LANE]
        for d in range(1, FIELDS):
            summed += flux[:, d * LANE : (d + 1) * LANE] * rows[:, d * LANE : (d + 1) * LANE]
        normal.append(summed.astype(BF16))
    return normal


def lift_faces(normal, lift, elems):
    rows = [
        jnp.concatenate([n[f * elems : (f + 1) * elems] for f in range(FACES)], 1) for n in normal
    ]
    return jnp.dot(jnp.concatenate(rows, 0), lift, preferred_element_type=F32)


def couple(entry_ref, states, t, shift, insts):
    summed = None
    for s in range(insts):
        d = (t - s + shift * insts) % NI
        term = entry_ref[d : d + 1, :] * states[s].astype(F32)
        summed = term if summed is None else summed + term
    return summed


def rotated(flux):
    place = lax.broadcasted_iota(jnp.int32, (flux.shape[0], LANE), 1) // FPTS
    blocks = []
    for k in range(LANE // FPTS):
        block = jnp.zeros((flux.shape[0], LANE), F32)
        for d in range(FIELDS):
            met = place == (d + k) % (LANE // FPTS)
            block = jnp.where(met, flux[:, d * LANE : (d + 1) * LANE], block)
        blocks.append(block)
    return jnp.concatenate(blocks, 1)


def slot_normal(blocks, factors, insts):
    count = blocks.shape[0]
    stacked = jnp.concatenate([blocks[:, t * LANE : (t + 1) * LANE] for t in range(insts)], 0)
    summed = [None] * insts
    for k in range(LANE // FPTS):
        turned = stacked if k == 0 else pltpu.roll(stacked, k * FPTS, 1)
        for t in range(insts):
            term = factors[:, k * LANE : (k + 1) * LANE] * turned[t * count : (t + 1) * count]
            summed[t] = term if k == 0 else summed[t] + term
    return [rows.astype(BF16) for rows in summed]


def table_kernel(spread_ref, order_ref):
    spread_ref[...] = spread_table()
    order_ref[...] = order_table()


def first_kernel(spectral, second, place_ref, freq_ref, spread_ref, state_ref, send_ref, *refs):
    insts, elems, width = state_ref.shape
    trace_refs, (entry_ref, pool_ref, *out_refs) = refs[:TRACE_TABLES], refs[TRACE_TABLES:]
    state = state_ref[...].reshape(insts * elems, width)
    pool = trace_pool(state, [ref[...] for ref in trace_refs], insts, elems)
    pool_ref[...] = pool
    fill_outgoing(pool, send_ref[0], out_refs, place_ref[0], elems)
    freq = freq_ref[0]
    for d in range(NI):
        entry = freq * float(spectral[d]) - dissipation * float(second[d])
        entry_ref[d : d + 1, :] = jnp.full((1, width), entry, F32)


def local_terms(states, diag, wide_ref, prod_ref, pool, hot, flux, spread, lift, insts, elems):
    some, collect = diagonal_steps(states, diag, wide_ref, prod_ref, insts, elems)
    quarter = elems // 4
    empty = jnp.zeros((hot.shape[1] - pool.shape[0], pool.shape[1]), BF16)
    pool = jnp.concatenate([pool, empty], 0)
    picked = jnp.dot(hot, pool, preferred_element_type=F32).astype(BF16)
    some(0, quarter)
    stacked = jnp.concatenate([picked[:, t * LANE : (t + 1) * LANE] for t in range(insts)], 0)
    wide = jnp.dot(stacked, spread, preferred_element_type=F32)
    some(quarter, 2 * quarter)
    normal = spread_flux(wide, flux.astype(F32), insts)
    some(2 * quarter, 3 * quarter)
    lifted = lift_faces(normal, lift, elems)
    some(3 * quarter, elems)
    products = collect()
    return [products[t] + lifted[t * elems : (t + 1) * elems] for t in range(insts)]


def slot_lift(blocks, factors, hot, lift, insts, elems):
    normal = slot_normal(blocks, factors, insts)
    empty = jnp.zeros((FACES * elems, insts * LANE), BF16)
    rows = jnp.concatenate([empty, jnp.concatenate(normal, 1)], 0)
    spots = jnp.dot(hot, rows, preferred_element_type=F32).astype(BF16)
    return lift_faces([spots[:, t * LANE : (t + 1) * LANE] for t in range(insts)], lift, elems)


def base_kernel(slots, state_ref, diag_ref, forcing_ref, entry_ref, pool_ref, flux_ref, source_ref,
                order_ref, spread_ref, lift_ref, spatial_ref, rest_ref, flux_out_ref, hot_ref,
                factor_ref, wide_ref, prod_ref):
    insts, elems, width = state_ref.shape
    hot = source_table(source_ref[...].T, elems, slots)
    flux = flux_order(flux_ref[...], order_ref[...])
    hot_ref[...] = hot
    flux_out_ref[...] = flux
    factors = lax.dot_general(hot, flux, (((0,), (0,)), ((), ())), preferred_element_type=F32)
    factor_ref[...] = rotated(factors[FACES * elems :])
    states = [state_ref[t] for t in range(insts)]
    spatial = local_terms(
        states, diag_ref, wide_ref, prod_ref, pool_ref[...], hot, flux, spread_ref[...],
        lift_ref[...], insts, elems,
    )
    for t in range(insts):
        spatial_ref[t] = spatial[t]
        rest_ref[t] = couple(entry_ref, states, t, 0, insts) - forcing_ref[t].astype(F32)


def last_base_kernel(state_ref, pool_ref, diag_ref, forcing_ref, hot_ref, flux_ref, spread_ref,
                     lift_ref, base_ref, wide_ref, prod_ref):
    insts, elems, width = state_ref.shape
    states = [state_ref[t].astype(BF16) for t in range(insts)]
    spatial = local_terms(
        states, diag_ref, wide_ref, prod_ref, pool_ref[...], hot_ref[...], flux_ref[...],
        spread_ref[...], lift_ref[...], insts, elems,
    )
    for t in range(insts):
        base_ref[t] = spatial[t] - forcing_ref[t].astype(F32)


def message_kernel(ranks, partial_ref, first_ref, base_ref, entry_ref, *refs):
    message_refs, (state_ref, out_ref) = refs[: ranks - 1], refs[ranks - 1 :]
    insts, elems, width = base_ref.shape
    firsts = [[first_ref[t] for t in range(insts)]]
    partials = [[partial_ref[t] for t in range(insts)]]
    for message_ref in message_refs:
        rows = [
            message_ref[i * elems : (i + 1) * elems, 0:width] for i in range(2 * insts)
        ]
        firsts.append(rows[:insts])
        partials.append(rows[insts:])
    states = []
    for k in range(ranks):
        of_rank = []
        for t in range(insts):
            state = partials[k][t].astype(F32)
            for j in range(ranks):
                if j != k:
                    state -= pseudo_step * couple(entry_ref, firsts[j], t, k - j, insts)
            of_rank.append(state.astype(BF16) if k == 0 else state)
        states.append(of_rank)
    for t in range(insts):
        state_ref[t] = states[0][t]
        coupling = base_ref[t]
        for k in range(ranks):
            coupling += couple(entry_ref, states[k], t, -k, insts)
        out_ref[t] = coupling


def received(parts, place, got_refs, order):
    got_refs = {swap: got_refs[i] for i, swap in enumerate(order)}
    arrived = by_offset(
        place, [got_refs[swap][...].astype(F32) for swap in range(len(OFFSETS))]
    )
    for k, offset in enumerate(OFFSETS):
        exists = (place + offset >= 0) & (place + offset < parts)
        arrived[k] = jnp.where(exists, arrived[k], jnp.zeros_like(arrived[k]))
    return jnp.concatenate(arrived, 0)


def step_kernel(parts, place_ref, *refs):
    got_refs, refs = refs[: len(OFFSETS)], refs[len(OFFSETS) :]
    trace_refs, refs = refs[:TRACE_TABLES], refs[TRACE_TABLES:]
    (state_ref, local_ref, rest_ref, hot_ref, factor_ref, lift_ref, send_ref,
     partial_ref, message_ref, next_pool_ref, *out_refs) = refs
    insts, elems, width = state_ref.shape
    place = place_ref[0]
    blocks = received(parts, place, got_refs, FIRST_ORDER)
    lifted = slot_lift(blocks, factor_ref[...], hot_ref[...], lift_ref[...], insts, elems)
    message_ref[...] = jnp.zeros_like(message_ref)
    fresh = []
    for t in range(insts):
        spatial = local_ref[t] + lifted[t * elems : (t + 1) * elems]
        moved = state_ref[t].astype(F32) - pseudo_step * (spatial + rest_ref[t])
        partial_ref[t] = moved
        fresh.append(moved.astype(BF16))
        lean = (moved - pseudo_step * spatial).astype(BF16)
        for i, block in enumerate((state_ref[t], lean)):
            low = (i * insts + t) * elems
            message_ref[low : low + elems, 0:width] = block
    tables_of_traces = [ref[...] for ref in trace_refs]
    pool = trace_pool(jnp.concatenate(fresh, 0), tables_of_traces, insts, elems)
    next_pool_ref[...] = pool
    fill_outgoing(pool, send_ref[0], out_refs, place, elems)


def last_kernel(parts, place_ref, *refs):
    got_refs, refs = refs[: len(OFFSETS)], refs[len(OFFSETS) :]
    (state_ref, base_ref, hot_ref, factor_ref, lift_ref, final_hbm, residual_hbm,
     final_ref, residual_ref, sems) = refs
    insts, elems, width = state_ref.shape
    blocks = received(parts, place_ref[0], got_refs, LAST_ORDER)
    lifted = slot_lift(blocks, factor_ref[...], hot_ref[...], lift_ref[...], insts, elems)
    for t in range(insts):
        residual = base_ref[t] + lifted[t * elems : (t + 1) * elems]
        residual_ref[t] = residual
        final_ref[t] = (state_ref[t].astype(F32) - pseudo_step * residual).astype(BF16)
    copies = [
        pltpu.make_async_copy(residual_ref, residual_hbm, sems.at[0]),
        pltpu.make_async_copy(final_ref, final_hbm, sems.at[1]),
    ]
    for copy in copies:
        copy.start()
    for copy in copies:
        copy.wait()


def on_device(
    initial_state, forcing, diagonal_blocks, flux_jacobian, send_list, source_index, frequency
):
    insts, elems, width = initial_state.shape
    parts = lax.axis_size("dom")
    ranks = lax.axis_size("inst")
    slots, capacity = send_list.shape[1:]
    faces = FACES * elems
    trace_np, lift_np, spectral, second = wide_tables()
    trace_wide = [jnp.asarray(part, BF16) for part in np.split(trace_np, TRACE_TABLES, 1)]
    lift_wide = jnp.asarray(lift_np, BF16)
    place = lax.axis_index("dom").reshape(1)
    sources = source_index.T
    routes = swap_routes(ranks, parts)

    smem = pl.BlockSpec(memory_space=pltpu.SMEM)
    vmem = pl.BlockSpec(memory_space=pltpu.VMEM)
    params = pltpu.CompilerParams(vmem_limit_bytes=VMEM_LIMIT)

    def like(array):
        return jax.ShapeDtypeStruct(array.shape, array.dtype)

    wide_shape = jax.ShapeDtypeStruct(initial_state.shape, F32)
    pool_shape = jax.ShapeDtypeStruct((faces, insts * LANE), BF16)
    out_shapes = [jax.ShapeDtypeStruct((capacity, insts * LANE), BF16)] * slots
    flux_shape = jax.ShapeDtypeStruct((faces, FIELDS * LANE), BF16)
    hot_shape = jax.ShapeDtypeStruct((faces, faces + slots * capacity), BF16)
    factor_shape = jax.ShapeDtypeStruct((slots * capacity, LANE // FPTS * LANE), F32)

    def exchange(outgoing, order):
        return [
            lax.ppermute(outgoing[swap], ("inst", "dom"), routes[swap]) for swap in order
        ]

    entry_shape = jax.ShapeDtypeStruct((NI, width), F32)
    message_shape = jax.ShapeDtypeStruct((2 * insts * elems, pl.cdiv(width, LANE) * LANE), BF16)
    chunks = [pltpu.VMEM((pl.cdiv(width, LANE) * insts * elems, LANE), F32)] * 2
    diag_cost = pl.CostEstimate(
        flops=2 * insts * diagonal_blocks.size, bytes_accessed=2 * diagonal_blocks.size,
        transcendentals=0,
    )
    spread, order = pl.pallas_call(
        table_kernel,
        out_shape=[
            jax.ShapeDtypeStruct((LANE, FIELDS * LANE), BF16),
            jax.ShapeDtypeStruct((FIELDS * FIELDS * FPTS, FIELDS * LANE), BF16),
        ],
        out_specs=[vmem] * 2,
        compiler_params=params,
        cost_estimate=pl.CostEstimate(flops=10**10, bytes_accessed=10**6, transcendentals=0),
        name="tables",
    )()
    freq, _ = lax.optimization_barrier((frequency, spread))
    entries, pool, *outgoing = pl.pallas_call(
        functools.partial(first_kernel, spectral, second),
        out_shape=[entry_shape, pool_shape] + out_shapes,
        in_specs=[smem] * 2 + [vmem] * (3 + TRACE_TABLES),
        out_specs=[vmem] * (2 + len(out_shapes)),
        compiler_params=params,
        cost_estimate=pl.CostEstimate(flops=10**10, bytes_accessed=10**6, transcendentals=0),
        name="first_traces",
    )(place, freq, spread, initial_state, send_list, *trace_wide)
    got = exchange(outgoing, FIRST_ORDER)
    local, rest, flux, hot, factors = pl.pallas_call(
        functools.partial(base_kernel, slots * capacity),
        out_shape=[wide_shape] * 2 + [flux_shape, hot_shape, factor_shape],
        in_specs=[vmem] * 10,
        out_specs=[vmem] * 5,
        scratch_shapes=chunks,
        compiler_params=params,
        cost_estimate=diag_cost,
        name="own_terms",
    )(initial_state, diagonal_blocks, forcing, entries, pool, flux_jacobian, sources, order, spread,
      lift_wide)
    partial, message, pool, *outgoing = pl.pallas_call(
        functools.partial(step_kernel, parts),
        out_shape=[wide_shape, message_shape, pool_shape] + out_shapes,
        in_specs=[smem] + [vmem] * (slots + 7 + TRACE_TABLES),
        out_specs=[vmem] * (3 + len(out_shapes)),
        compiler_params=params,
        name="first_step",
    )(place, *got, *trace_wide, initial_state, local, rest, hot, factors, lift_wide, send_list)
    messages = [
        lax.ppermute(message, "inst", [((i + rank) % ranks, i) for i in range(ranks)])
        for rank in range(1, ranks)
    ]
    got = exchange(outgoing, LAST_ORDER)
    base = pl.pallas_call(
        last_base_kernel,
        out_shape=wide_shape,
        in_specs=[vmem] * 8,
        out_specs=vmem,
        scratch_shapes=chunks,
        compiler_params=params,
        cost_estimate=diag_cost,
        name="last_own_terms",
    )(partial, pool, diagonal_blocks, forcing, hot, flux, spread, lift_wide)
    state, base = pl.pallas_call(
        functools.partial(message_kernel, ranks),
        out_shape=[like(initial_state), wide_shape],
        in_specs=[vmem] * (ranks + 3),
        out_specs=[vmem] * 2,
        compiler_params=params,
        name="message_terms",
    )(partial, initial_state, base, entries, *messages)
    return pl.pallas_call(
        functools.partial(last_kernel, parts),
        out_shape=[like(initial_state), wide_shape],
        in_specs=[smem] + [vmem] * (slots + 5),
        out_specs=[pl.BlockSpec(memory_space=pl.ANY)] * 2,
        scratch_shapes=[
            pltpu.VMEM(initial_state.shape, BF16),
            pltpu.VMEM(initial_state.shape, F32),
            pltpu.SemaphoreType.DMA((2,)),
        ],
        compiler_params=params,
        name="last_step",
    )(place, *got, state, base, hot, factors, lift_wide)


def solution(mesh):
    return jax.shard_map(
        on_device,
        mesh=mesh,
        in_specs=(
            P("inst", "dom", None),
            P("inst", "dom", None),
            P("dom", None, None),
            P("dom", None),
            P("dom", None, None),
            P("dom", None),
            P(),
        ),
        out_specs=(P("inst", "dom", None), P("inst", "dom", None)),
        check_vma=False,
    )
```

```python
import functools
import math

import jax
import jax.numpy as jnp
import numpy as np
from jax import lax
from jax.experimental import pallas as pl
from jax.experimental.pallas import tpu as pltpu
from jax.sharding import PartitionSpec as P

FIELDS = 5
ORDER = 3
NODES = 64
FPTS = 16
NI = 8
REACH = 2
ITERS = 2


pseudo_step = 0.5
dissipation = 0.25


def gauss_legendre(count):
    points = []
    weights = []
    for i in range(count):
        where = math.cos(math.pi * (i + 0.75) / (count + 0.5))
        for sweep in range(100):
            before = 1.0
            value = where
            for j in range(2, count + 1):
                after = ((2 * j - 1) * where * value - (j - 1) * before) / j
                before = value
                value = after
            slope = count * (where * value - before) / (where * where - 1.0)
            where = where - value / slope
        before = 1.0
        value = where
        for j in range(2, count + 1):
            after = ((2 * j - 1) * where * value - (j - 1) * before) / j
            before = value
            value = after
        slope = count * (where * value - before) / (where * where - 1.0)
        points.append(where)
        weights.append(2.0 / ((1.0 - where * where) * slope * slope))
    return (np.array(points[::-1]), np.array(weights[::-1]))


def lagrange_at(points, where):
    values = np.ones(points.shape[0])
    for i in range(points.shape[0]):
        for j in range(points.shape[0]):
            if j != i:
                values[i] = values[i] * (where - points[j]) / (points[i] - points[j])
    return values


def tables(order, count):
    points, weights = gauss_legendre(order + 1)
    at_minus = lagrange_at(points, -1.0)
    at_plus = lagrange_at(points, 1.0)
    per_side = order + 1
    node_count = per_side**3
    face_points = per_side**2
    trace_table = np.zeros((node_count, 6 * face_points))
    lift_table = np.zeros((node_count, 6 * face_points))
    for k in range(per_side):
        for j in range(per_side):
            for i in range(per_side):
                node = i + per_side * j + per_side * per_side * k
                entries = [
                    (0, at_minus[i], j + per_side * k, weights[i]),
                    (1, at_plus[i], j + per_side * k, weights[i]),
                    (2, at_minus[j], i + per_side * k, weights[j]),
                    (3, at_plus[j], i + per_side * k, weights[j]),
                    (4, at_minus[k], i + per_side * j, weights[k]),
                    (5, at_plus[k], i + per_side * j, weights[k]),
                ]
                for face_index, factor, point, weight in entries:
                    trace_table[node, face_index * face_points + point] = factor
                    lift_table[node, face_index * face_points + point] = factor / weight
    spectral = np.zeros((count, count))
    second = np.zeros((count, count))
    for t in range(count):
        for s in range(count):
            if t != s:
                spectral[t, s] = 0.5 * (-1.0) ** (t - s + 1) / math.tan(math.pi * (t - s) / count)
                second[t, s] = -0.5 * (-1.0) ** (t - s) / math.sin(math.pi * (t - s) / count) ** 2
            else:
                second[t, s] = -(count * count + 2.0) / 12.0
    return (trace_table, lift_table, spectral, second)


LANE = 128
WIDE = FIELDS * NODES
FACES = 6
TRACE_TABLES = 3
VMEM_LIMIT = 16 * 1024 * 1024
BF16 = jnp.bfloat16
F32 = jnp.float32
OFFSETS = list(range(-REACH, 0)) + list(range(1, REACH + 1))
FIRST_ORDER = (3, 1, 2, 0)
LAST_ORDER = (2, 1, 3, 0)


def wide_tables():
    trace_np, lift_np, spectral_np, second_np = tables(ORDER, NI)
    trace_wide = np.zeros((WIDE, FACES * LANE))
    lift_wide = np.zeros((FACES * LANE, WIDE))
    for c in range(FIELDS):
        rows = slice(c * NODES, (c + 1) * NODES)
        for f in range(FACES):
            cols = slice(f * LANE + c * FPTS, f * LANE + (c + 1) * FPTS)
            face = slice(f * FPTS, (f + 1) * FPTS)
            trace_wide[rows, cols] = trace_np[:, face]
            lift_wide[cols, rows] = lift_np[:, face].T
    return trace_wide, lift_wide, spectral_np[:, 0], second_np[:, 0]


def iotas(shape):
    return [lax.broadcasted_iota(jnp.int32, shape, axis) for axis in range(2)]


def one_hot(mask):
    return jnp.where(mask, 1.0, 0.0).astype(BF16)


def spread_table():
    row, col = iotas((LANE, FIELDS * LANE))
    inside = col % LANE < FIELDS * FPTS
    return one_hot(inside & (row == col // LANE * FPTS + col % FPTS))


def order_table():
    row, col = iotas((FIELDS * FIELDS * FPTS, FIELDS * LANE))
    place = col % LANE
    source = place // FPTS * FIELDS * FPTS + col // LANE * FPTS + col % FPTS
    return one_hot((place < FIELDS * FPTS) & (row == source))


def pooled(faces, insts, elems):
    by_inst = []
    for t in range(insts):
        by_inst.append(jnp.concatenate([rows[t * elems : (t + 1) * elems] for rows in faces], 0))
    return jnp.concatenate(by_inst, 1)


def trace_pool(state, trace_tables, insts, elems):
    faces = []
    for table in trace_tables:
        wide = jnp.dot(state, table, preferred_element_type=F32)
        faces += [wide[:, at : at + LANE] for at in range(0, table.shape[1], LANE)]
    return pooled(faces, insts, elems)


def swap_routes(ranks, parts):
    near = [[(p, p + 1) for p in range(first, parts - 1, 2)] for first in range(2)]
    far = [
        [(p + i, p + i + 2) for p in range(first, parts - 3, 4) for i in range(2)]
        for first in (0, 2)
    ]
    routes = []
    for pairs in near + far:
        met = {p for pair in pairs for p in pair}
        alone = [p for p in range(parts) if p not in met]
        idle = []
        for p in list(alone):
            if p in alone and p + 1 in alone:
                idle.append((p, p + 1))
                alone = [q for q in alone if q not in idle[-1]]
        swaps = [(r * parts + p, r * parts + q) for r in range(ranks) for p, q in pairs + idle]
        swaps += [(r * parts + p, (r ^ 1) * parts + p) for r in range(0, ranks, 2) for p in alone]
        routes.append(swaps + [(q, p) for p, q in swaps])
    return routes


def by_swap(place, by_offset):
    two_down, one_down, one_up, two_up = by_offset
    even = place % 2 == 0
    low = place // 2 % 2 == 0
    return [
        jnp.where(even, one_up, one_down),
        jnp.where(even, one_down, one_up),
        jnp.where(low, two_up, two_down),
        jnp.where(low, two_down, two_up),
    ]


def by_offset(place, blocks):
    even = place % 2 == 0
    low = place // 2 % 2 == 0
    return [
        jnp.where(low, blocks[3], blocks[2]),
        jnp.where(even, blocks[1], blocks[0]),
        jnp.where(even, blocks[0], blocks[1]),
        jnp.where(low, blocks[2], blocks[3]),
    ]


def fill_outgoing(pool, send, out_refs, place, elems):
    slots, capacity = send.shape
    rows, cols = iotas((FACES * elems, slots * capacity))
    ids = FACES * (rows % elems) + rows // elems
    wanted = jnp.concatenate([send[k : k + 1] for k in range(slots)], 1)
    out = lax.dot_general(
        one_hot(ids == wanted), pool, (((0,), (0,)), ((), ())), preferred_element_type=F32
    )
    blocks = by_swap(place, [out[k * capacity : (k + 1) * capacity] for k in range(slots)])
    for block, ref in zip(blocks, out_refs):
        ref[...] = block.astype(BF16)


def diagonal_steps(states, diag, wide_ref, prod_ref, insts, elems):
    tall = insts * elems
    width = diag.shape[1]
    cuts = [(j, j * LANE, min((j + 1) * LANE, width)) for j in range(pl.cdiv(width, LANE))]
    for t in range(insts):
        rows = states[t].astype(F32)
        for j, low, high in cuts:
            first = j * tall + t * elems
            wide_ref[first : first + elems, 0 : high - low] = rows[:, low:high]

    def some(begin, end):
        for e in range(begin, end):
            rows = jnp.concatenate(
                [wide_ref[pl.ds(j * tall + e, insts, stride=elems), :] for j, low, high in cuts], 1
            )
            product = jnp.dot(rows[:, 0:width].astype(BF16), diag[e], preferred_element_type=F32)
            for j, low, high in cuts:
                chunk = product[:, low:high]
                if high - low < LANE:
                    empty = jnp.zeros((insts, LANE - high + low), F32)
                    chunk = jnp.concatenate([chunk, empty], 1)
                prod_ref[pl.ds(j * tall + e, insts, stride=elems), :] = chunk

    def collect():
        return [
            jnp.concatenate(
                [
                    prod_ref[j * tall + t * elems : j * tall + (t + 1) * elems, 0 : high - low]
                    for j, low, high in cuts
                ],
                1,
            )
            for t in range(insts)
        ]

    return some, collect


def flux_order(rows, order):
    per_face = FIELDS * FIELDS * FPTS
    by_face = jnp.concatenate(
        [rows[:, f * per_face : (f + 1) * per_face] for f in range(FACES)], 0
    )
    return jnp.dot(by_face, order, preferred_element_type=F32).astype(BF16)


def source_table(sources, elems, slots):
    faces = FACES * elems
    columns = lax.broadcasted_iota(jnp.int32, (elems, faces + slots), 1)
    ids = jnp.where(columns < faces, FACES * (columns % elems) + columns // elems, columns)
    hot = [jnp.where(sources[:, f : f + 1] == ids, 1.0, 0.0) for f in range(FACES)]
    return jnp.concatenate(hot, 0).astype(BF16)


def spread_flux(wide, flux, insts):
    count = flux.shape[0]
    normal = []
    for t in range(insts):
        rows = wide[t * count : (t + 1) * count]
        summed = flux[:, 0:LANE] * rows[:, 0:LANE]
        for d in range(1, FIELDS):
            summed += flux[:, d * LANE : (d + 1) * LANE] * rows[:, d * LANE : (d + 1) * LANE]
        normal.append(summed.astype(BF16))
    return normal


def face_rows(normal, elems):
    rows = [
        jnp.concatenate([n[f * elems : (f + 1) * elems] for f in range(FACES)], 1) for n in normal
    ]
    return jnp.concatenate(rows, 0)


def lift_faces(normal, lift, elems):
    return jnp.dot(face_rows(normal, elems), lift, preferred_element_type=F32)


def couple(entry_ref, states, t, shift, insts):
    summed = None
    for s in range(insts):
        d = (t - s + shift * insts) % NI
        term = entry_ref[d : d + 1, :] * states[s].astype(F32)
        summed = term if summed is None else summed + term
    return summed


def rotated(flux):
    place = lax.broadcasted_iota(jnp.int32, (flux.shape[0], LANE), 1) // FPTS
    blocks = []
    for k in range(LANE // FPTS):
        block = jnp.zeros((flux.shape[0], LANE), F32)
        for d in range(FIELDS):
            met = place == (d + k) % (LANE // FPTS)
            block = jnp.where(met, flux[:, d * LANE : (d + 1) * LANE], block)
        blocks.append(block)
    return jnp.concatenate(blocks, 1)


def slot_normal(blocks, factors, insts):
    count = blocks.shape[0]
    stacked = jnp.concatenate([blocks[:, t * LANE : (t + 1) * LANE] for t in range(insts)], 0)
    summed = [None] * insts
    for k in range(LANE // FPTS):
        turned = stacked if k == 0 else pltpu.roll(stacked, k * FPTS, 1)
        for t in range(insts):
            term = factors[:, k * LANE : (k + 1) * LANE] * turned[t * count : (t + 1) * count]
            summed[t] = term if k == 0 else summed[t] + term
    return [rows.astype(BF16) for rows in summed]


def table_kernel(spread_ref, order_ref):
    spread_ref[...] = spread_table()
    order_ref[...] = order_table()


def first_kernel(spectral, second, place_ref, freq_ref, spread_ref, state_ref, send_ref, *refs):
    insts, elems, width = state_ref.shape
    trace_refs, (entry_ref, pool_ref, *out_refs) = refs[:TRACE_TABLES], refs[TRACE_TABLES:]
    state = state_ref[...].reshape(insts * elems, width)
    pool = trace_pool(state, [ref[...] for ref in trace_refs], insts, elems).astype(BF16)
    pool_ref[...] = pool
    fill_outgoing(pool, send_ref[0], out_refs, place_ref[0], elems)
    freq = freq_ref[0]
    for d in range(NI):
        entry = freq * float(spectral[d]) - dissipation * float(second[d])
        entry_ref[d : d + 1, :] = jnp.full((1, width), entry, F32)


def local_terms(states, diag, wide_ref, prod_ref, pool, hot, flux, spread, lift, insts, elems):
    some, collect = diagonal_steps(states, diag, wide_ref, prod_ref, insts, elems)
    quarter = elems // 4
    empty = jnp.zeros((hot.shape[1] - pool.shape[0], pool.shape[1]), BF16)
    pool = jnp.concatenate([pool, empty], 0)
    picked = jnp.dot(hot, pool, preferred_element_type=F32).astype(BF16)
    some(0, quarter)
    stacked = jnp.concatenate([picked[:, t * LANE : (t + 1) * LANE] for t in range(insts)], 0)
    wide = jnp.dot(stacked, spread, preferred_element_type=F32)
    some(quarter, 2 * quarter)
    normal = spread_flux(wide, flux.astype(F32), insts)
    some(2 * quarter, 3 * quarter)
    lifted = lift_faces(normal, lift, elems)
    some(3 * quarter, elems)
    products = collect()
    return [products[t] + lifted[t * elems : (t + 1) * elems] for t in range(insts)]


def slot_faces(blocks, factors, hot, insts, elems):
    normal = slot_normal(blocks, factors, insts)
    empty = jnp.zeros((FACES * elems, insts * LANE), BF16)
    rows = jnp.concatenate([empty, jnp.concatenate(normal, 1)], 0)
    spots = jnp.dot(hot, rows, preferred_element_type=F32).astype(BF16)
    return [spots[:, t * LANE : (t + 1) * LANE] for t in range(insts)]


def base_kernel(slots, state_ref, diag_ref, forcing_ref, entry_ref, pool_ref, flux_ref, source_ref,
                order_ref, spread_ref, lift_ref, *refs):
    trace_refs, refs = refs[:TRACE_TABLES], refs[TRACE_TABLES:]
    (spatial_ref, rest_ref, flux_out_ref, hot_ref, factor_ref, early_ref, wide_ref,
     prod_ref) = refs
    insts, elems, width = state_ref.shape
    hot = source_table(source_ref[...].T, elems, slots)
    flux = flux_order(flux_ref[...], order_ref[...])
    hot_ref[...] = hot
    flux_out_ref[...] = flux
    factors = lax.dot_general(hot, flux, (((0,), (0,)), ((), ())), preferred_element_type=F32)
    factor_ref[...] = rotated(factors[FACES * elems :])
    states = [state_ref[t] for t in range(insts)]
    spatial = local_terms(
        states, diag_ref, wide_ref, prod_ref, pool_ref[...], hot, flux, spread_ref[...],
        lift_ref[...], insts, elems,
    )
    early = []
    for t in range(insts):
        spatial_ref[t] = spatial[t]
        rest = couple(entry_ref, states, t, 0, insts) - forcing_ref[t].astype(F32)
        rest_ref[t] = rest
        early.append((states[t].astype(F32) - pseudo_step * (spatial[t] + rest)).astype(BF16))
    tables_of_traces = [ref[...] for ref in trace_refs]
    early_ref[...] = trace_pool(jnp.concatenate(early, 0), tables_of_traces, insts, elems)


def last_base_kernel(state_ref, pool_ref, diag_ref, forcing_ref, hot_ref, flux_ref, spread_ref,
                     lift_ref, base_ref, wide_ref, prod_ref):
    insts, elems, width = state_ref.shape
    states = [state_ref[t].astype(BF16) for t in range(insts)]
    spatial = local_terms(
        states, diag_ref, wide_ref, prod_ref, pool_ref[...], hot_ref[...], flux_ref[...],
        spread_ref[...], lift_ref[...], insts, elems,
    )
    for t in range(insts):
        base_ref[t] = spatial[t] - forcing_ref[t].astype(F32)


def message_kernel(ranks, partial_ref, first_ref, base_ref, entry_ref, *refs):
    message_refs, (state_ref, out_ref) = refs[: ranks - 1], refs[ranks - 1 :]
    insts, elems, width = base_ref.shape
    firsts = [[first_ref[t] for t in range(insts)]]
    partials = [[partial_ref[t] for t in range(insts)]]
    for message_ref in message_refs:
        rows = [
            message_ref[i * elems : (i + 1) * elems, 0:width] for i in range(2 * insts)
        ]
        firsts.append(rows[:insts])
        partials.append(rows[insts:])
    states = []
    for k in range(ranks):
        of_rank = []
        for t in range(insts):
            state = partials[k][t].astype(F32)
            for j in range(ranks):
                if j != k:
                    state -= pseudo_step * couple(entry_ref, firsts[j], t, k - j, insts)
            of_rank.append(state.astype(BF16) if k == 0 else state)
        states.append(of_rank)
    for t in range(insts):
        state_ref[t] = states[0][t]
        coupling = base_ref[t]
        for k in range(ranks):
            coupling += couple(entry_ref, states[k], t, -k, insts)
        out_ref[t] = coupling


def received(parts, place, got_refs, order):
    got_refs = {swap: got_refs[i] for i, swap in enumerate(order)}
    arrived = by_offset(
        place, [got_refs[swap][...].astype(F32) for swap in range(len(OFFSETS))]
    )
    for k, offset in enumerate(OFFSETS):
        exists = (place + offset >= 0) & (place + offset < parts)
        arrived[k] = jnp.where(exists, arrived[k], jnp.zeros_like(arrived[k]))
    return jnp.concatenate(arrived, 0)


def step_kernel(parts, place_ref, *refs):
    got_refs, refs = refs[: len(OFFSETS)], refs[len(OFFSETS) :]
    (state_ref, local_ref, rest_ref, hot_ref, factor_ref, early_ref, lift_ref, through_ref,
     send_ref, partial_ref, message_ref, next_pool_ref, *out_refs) = refs
    insts, elems, width = state_ref.shape
    place = place_ref[0]
    blocks = received(parts, place, got_refs, FIRST_ORDER)
    rows = face_rows(slot_faces(blocks, factor_ref[...], hot_ref[...], insts, elems), elems)
    late = jnp.dot(rows, through_ref[...], preferred_element_type=F32)
    late = [late[:, f * LANE : (f + 1) * LANE] for f in range(FACES)]
    pool = (early_ref[...] - pseudo_step * pooled(late, insts, elems)).astype(BF16)
    next_pool_ref[...] = pool
    fill_outgoing(pool, send_ref[0], out_refs, place, elems)
    lifted = jnp.dot(rows, lift_ref[...], preferred_element_type=F32)
    message_ref[...] = jnp.zeros_like(message_ref)
    for t in range(insts):
        spatial = local_ref[t] + lifted[t * elems : (t + 1) * elems]
        moved = state_ref[t].astype(F32) - pseudo_step * (spatial + rest_ref[t])
        partial_ref[t] = moved
        lean = (moved - pseudo_step * spatial).astype(BF16)
        for i, block in enumerate((state_ref[t], lean)):
            low = (i * insts + t) * elems
            message_ref[low : low + elems, 0:width] = block


def last_kernel(parts, place_ref, *refs):
    got_refs, refs = refs[: len(OFFSETS)], refs[len(OFFSETS) :]
    (state_ref, base_ref, hot_ref, factor_ref, lift_ref, final_hbm, residual_hbm,
     final_ref, residual_ref, sems) = refs
    insts, elems, width = state_ref.shape
    blocks = received(parts, place_ref[0], got_refs, LAST_ORDER)
    normal = slot_faces(blocks, factor_ref[...], hot_ref[...], insts, elems)
    lifted = lift_faces(normal, lift_ref[...], elems)
    for t in range(insts):
        residual = base_ref[t] + lifted[t * elems : (t + 1) * elems]
        residual_ref[t] = residual
        final_ref[t] = (state_ref[t].astype(F32) - pseudo_step * residual).astype(BF16)
    copies = [
        pltpu.make_async_copy(residual_ref, residual_hbm, sems.at[0]),
        pltpu.make_async_copy(final_ref, final_hbm, sems.at[1]),
    ]
    for copy in copies:
        copy.start()
    for copy in copies:
        copy.wait()


def on_device(
    initial_state, forcing, diagonal_blocks, flux_jacobian, send_list, source_index, frequency
):
    insts, elems, width = initial_state.shape
    parts = lax.axis_size("dom")
    ranks = lax.axis_size("inst")
    slots, capacity = send_list.shape[1:]
    faces = FACES * elems
    trace_np, lift_np, spectral, second = wide_tables()
    through = jnp.asarray(lift_np @ trace_np, BF16)
    trace_wide = [jnp.asarray(part, BF16) for part in np.split(trace_np, TRACE_TABLES, 1)]
    lift_wide = jnp.asarray(lift_np, BF16)
    place = lax.axis_index("dom").reshape(1)
    sources = source_index.T
    routes = swap_routes(ranks, parts)

    smem = pl.BlockSpec(memory_space=pltpu.SMEM)
    vmem = pl.BlockSpec(memory_space=pltpu.VMEM)
    params = pltpu.CompilerParams(vmem_limit_bytes=VMEM_LIMIT)

    def like(array):
        return jax.ShapeDtypeStruct(array.shape, array.dtype)

    wide_shape = jax.ShapeDtypeStruct(initial_state.shape, F32)
    pool_shape = jax.ShapeDtypeStruct((faces, insts * LANE), BF16)
    out_shapes = [jax.ShapeDtypeStruct((capacity, insts * LANE), BF16)] * slots
    flux_shape = jax.ShapeDtypeStruct((faces, FIELDS * LANE), BF16)
    hot_shape = jax.ShapeDtypeStruct((faces, faces + slots * capacity), BF16)
    factor_shape = jax.ShapeDtypeStruct((slots * capacity, LANE // FPTS * LANE), F32)

    def exchange(outgoing, order):
        return [
            lax.ppermute(outgoing[swap], ("inst", "dom"), routes[swap]) for swap in order
        ]

    early_shape = jax.ShapeDtypeStruct((faces, insts * LANE), F32)
    entry_shape = jax.ShapeDtypeStruct((NI, width), F32)
    message_shape = jax.ShapeDtypeStruct((2 * insts * elems, pl.cdiv(width, LANE) * LANE), BF16)
    chunks = [pltpu.VMEM((pl.cdiv(width, LANE) * insts * elems, LANE), F32)] * 2
    diag_cost = pl.CostEstimate(
        flops=2 * insts * diagonal_blocks.size, bytes_accessed=2 * diagonal_blocks.size,
        transcendentals=0,
    )
    spread, order = pl.pallas_call(
        table_kernel,
        out_shape=[
            jax.ShapeDtypeStruct((LANE, FIELDS * LANE), BF16),
            jax.ShapeDtypeStruct((FIELDS * FIELDS * FPTS, FIELDS * LANE), BF16),
        ],
        out_specs=[vmem] * 2,
        compiler_params=params,
        cost_estimate=pl.CostEstimate(flops=10**10, bytes_accessed=10**6, transcendentals=0),
        name="tables",
    )()
    freq, _ = lax.optimization_barrier((frequency, spread))
    entries, pool, *outgoing = pl.pallas_call(
        functools.partial(first_kernel, spectral, second),
        out_shape=[entry_shape, pool_shape] + out_shapes,
        in_specs=[smem] * 2 + [vmem] * (3 + TRACE_TABLES),
        out_specs=[vmem] * (2 + len(out_shapes)),
        compiler_params=params,
        cost_estimate=pl.CostEstimate(flops=10**10, bytes_accessed=10**6, transcendentals=0),
        name="first_traces",
    )(place, freq, spread, initial_state, send_list, *trace_wide)
    got = exchange(outgoing, FIRST_ORDER)
    local, rest, flux, hot, factors, early = pl.pallas_call(
        functools.partial(base_kernel, slots * capacity),
        out_shape=[wide_shape] * 2 + [flux_shape, hot_shape, factor_shape, early_shape],
        in_specs=[vmem] * (10 + TRACE_TABLES),
        out_specs=[vmem] * 6,
        scratch_shapes=chunks,
        compiler_params=params,
        cost_estimate=diag_cost,
        name="own_terms",
    )(initial_state, diagonal_blocks, forcing, entries, pool, flux_jacobian, sources, order, spread,
      lift_wide, *trace_wide)
    partial, message, pool, *outgoing = pl.pallas_call(
        functools.partial(step_kernel, parts),
        out_shape=[wide_shape, message_shape, pool_shape] + out_shapes,
        in_specs=[smem] + [vmem] * (slots + 9),
        out_specs=[vmem] * (3 + len(out_shapes)),
        compiler_params=params,
        name="first_step",
    )(place, *got, initial_state, local, rest, hot, factors, early, lift_wide, through, send_list)
    messages = [
        lax.ppermute(message, "inst", [((i + rank) % ranks, i) for i in range(ranks)])
        for rank in range(1, ranks)
    ]
    got = exchange(outgoing, LAST_ORDER)
    base = pl.pallas_call(
        last_base_kernel,
        out_shape=wide_shape,
        in_specs=[vmem] * 8,
        out_specs=vmem,
        scratch_shapes=chunks,
        compiler_params=params,
        cost_estimate=diag_cost,
        name="last_own_terms",
    )(partial, pool, diagonal_blocks, forcing, hot, flux, spread, lift_wide)
    state, base = pl.pallas_call(
        functools.partial(message_kernel, ranks),
        out_shape=[like(initial_state), wide_shape],
        in_specs=[vmem] * (ranks + 3),
        out_specs=[vmem] * 2,
        compiler_params=params,
        name="message_terms",
    )(partial, initial_state, base, entries, *messages)
    return pl.pallas_call(
        functools.partial(last_kernel, parts),
        out_shape=[like(initial_state), wide_shape],
        in_specs=[smem] + [vmem] * (slots + 5),
        out_specs=[pl.BlockSpec(memory_space=pl.ANY)] * 2,
        scratch_shapes=[
            pltpu.VMEM(initial_state.shape, BF16),
            pltpu.VMEM(initial_state.shape, F32),
            pltpu.SemaphoreType.DMA((2,)),
        ],
        compiler_params=params,
        name="last_step",
    )(place, *got, state, base, hot, factors, lift_wide)


def solution(mesh):
    return jax.shard_map(
        on_device,
        mesh=mesh,
        in_specs=(
            P("inst", "dom", None),
            P("inst", "dom", None),
            P("dom", None, None),
            P("dom", None),
            P("dom", None, None),
            P("dom", None),
            P(),
        ),
        out_specs=(P("inst", "dom", None), P("inst", "dom", None)),
        check_vma=False,
    )
```

```python
import functools
import math

import jax
import jax.numpy as jnp
import numpy as np
from jax import lax
from jax.experimental import pallas as pl
from jax.experimental.pallas import tpu as pltpu
from jax.sharding import PartitionSpec as P

FIELDS = 5
ORDER = 3
NODES = 64
FPTS = 16
NI = 8
REACH = 2
ITERS = 2


pseudo_step = 0.5
dissipation = 0.25


def gauss_legendre(count):
    points = []
    weights = []
    for i in range(count):
        where = math.cos(math.pi * (i + 0.75) / (count + 0.5))
        for sweep in range(100):
            before = 1.0
            value = where
            for j in range(2, count + 1):
                after = ((2 * j - 1) * where * value - (j - 1) * before) / j
                before = value
                value = after
            slope = count * (where * value - before) / (where * where - 1.0)
            where = where - value / slope
        before = 1.0
        value = where
        for j in range(2, count + 1):
            after = ((2 * j - 1) * where * value - (j - 1) * before) / j
            before = value
            value = after
        slope = count * (where * value - before) / (where * where - 1.0)
        points.append(where)
        weights.append(2.0 / ((1.0 - where * where) * slope * slope))
    return (np.array(points[::-1]), np.array(weights[::-1]))


def lagrange_at(points, where):
    values = np.ones(points.shape[0])
    for i in range(points.shape[0]):
        for j in range(points.shape[0]):
            if j != i:
                values[i] = values[i] * (where - points[j]) / (points[i] - points[j])
    return values


def tables(order, count):
    points, weights = gauss_legendre(order + 1)
    at_minus = lagrange_at(points, -1.0)
    at_plus = lagrange_at(points, 1.0)
    per_side = order + 1
    node_count = per_side**3
    face_points = per_side**2
    trace_table = np.zeros((node_count, 6 * face_points))
    lift_table = np.zeros((node_count, 6 * face_points))
    for k in range(per_side):
        for j in range(per_side):
            for i in range(per_side):
                node = i + per_side * j + per_side * per_side * k
                entries = [
                    (0, at_minus[i], j + per_side * k, weights[i]),
                    (1, at_plus[i], j + per_side * k, weights[i]),
                    (2, at_minus[j], i + per_side * k, weights[j]),
                    (3, at_plus[j], i + per_side * k, weights[j]),
                    (4, at_minus[k], i + per_side * j, weights[k]),
                    (5, at_plus[k], i + per_side * j, weights[k]),
                ]
                for face_index, factor, point, weight in entries:
                    trace_table[node, face_index * face_points + point] = factor
                    lift_table[node, face_index * face_points + point] = factor / weight
    spectral = np.zeros((count, count))
    second = np.zeros((count, count))
    for t in range(count):
        for s in range(count):
            if t != s:
                spectral[t, s] = 0.5 * (-1.0) ** (t - s + 1) / math.tan(math.pi * (t - s) / count)
                second[t, s] = -0.5 * (-1.0) ** (t - s) / math.sin(math.pi * (t - s) / count) ** 2
            else:
                second[t, s] = -(count * count + 2.0) / 12.0
    return (trace_table, lift_table, spectral, second)


LANE = 128
WIDE = FIELDS * NODES
FACES = 6
TRACE_TABLES = 3
VMEM_LIMIT = 16 * 1024 * 1024
BF16 = jnp.bfloat16
F32 = jnp.float32
OFFSETS = list(range(-REACH, 0)) + list(range(1, REACH + 1))
FIRST_ORDER = (3, 1, 2, 0)
LAST_ORDER = (2, 1, 3, 0)


def wide_tables():
    trace_np, lift_np, spectral_np, second_np = tables(ORDER, NI)
    trace_wide = np.zeros((WIDE, FACES * LANE))
    lift_wide = np.zeros((FACES * LANE, WIDE))
    for c in range(FIELDS):
        rows = slice(c * NODES, (c + 1) * NODES)
        for f in range(FACES):
            cols = slice(f * LANE + c * FPTS, f * LANE + (c + 1) * FPTS)
            face = slice(f * FPTS, (f + 1) * FPTS)
            trace_wide[rows, cols] = trace_np[:, face]
            lift_wide[cols, rows] = lift_np[:, face].T
    return trace_wide, lift_wide, spectral_np[:, 0], second_np[:, 0]


def iotas(shape):
    return [lax.broadcasted_iota(jnp.int32, shape, axis) for axis in range(2)]


def one_hot(mask):
    return jnp.where(mask, 1.0, 0.0).astype(BF16)


def spread_table():
    row, col = iotas((LANE, FIELDS * LANE))
    inside = col % LANE < FIELDS * FPTS
    return one_hot(inside & (row == col // LANE * FPTS + col % FPTS))


def order_table():
    row, col = iotas((FIELDS * FIELDS * FPTS, FIELDS * LANE))
    place = col % LANE
    source = place // FPTS * FIELDS * FPTS + col // LANE * FPTS + col % FPTS
    return one_hot((place < FIELDS * FPTS) & (row == source))


def trace_pool(state, trace_tables, insts, elems):
    faces = []
    for table in trace_tables:
        wide = jnp.dot(state, table, preferred_element_type=F32).astype(BF16)
        faces += [wide[:, at : at + LANE] for at in range(0, table.shape[1], LANE)]
    by_inst = []
    for t in range(insts):
        by_inst.append(jnp.concatenate([rows[t * elems : (t + 1) * elems] for rows in faces], 0))
    return jnp.concatenate(by_inst, 1)


def swap_routes(ranks, parts):
    near = [[(p, p + 1) for p in range(first, parts - 1, 2)] for first in range(2)]
    far = [
        [(p + i, p + i + 2) for p in range(first, parts - 3, 4) for i in range(2)]
        for first in (0, 2)
    ]
    routes = []
    for pairs in near + far:
        met = {p for pair in pairs for p in pair}
        alone = [p for p in range(parts) if p not in met]
        idle = []
        for p in list(alone):
            if p in alone and p + 1 in alone:
                idle.append((p, p + 1))
                alone = [q for q in alone if q not in idle[-1]]
        swaps = [(r * parts + p, r * parts + q) for r in range(ranks) for p, q in pairs + idle]
        swaps += [(r * parts + p, (r ^ 1) * parts + p) for r in range(0, ranks, 2) for p in alone]
        routes.append(swaps + [(q, p) for p, q in swaps])
    return routes


def by_swap(place, by_offset):
    two_down, one_down, one_up, two_up = by_offset
    even = place % 2 == 0
    low = place // 2 % 2 == 0
    return [
        jnp.where(even, one_up, one_down),
        jnp.where(even, one_down, one_up),
        jnp.where(low, two_up, two_down),
        jnp.where(low, two_down, two_up),
    ]


def by_offset(place, blocks):
    even = place % 2 == 0
    low = place // 2 % 2 == 0
    return [
        jnp.where(low, blocks[3], blocks[2]),
        jnp.where(even, blocks[1], blocks[0]),
        jnp.where(even, blocks[0], blocks[1]),
        jnp.where(low, blocks[2], blocks[3]),
    ]


def fill_outgoing(pool, send, out_refs, place, elems):
    slots, capacity = send.shape
    rows, cols = iotas((FACES * elems, slots * capacity))
    ids = FACES * (rows % elems) + rows // elems
    wanted = jnp.concatenate([send[k : k + 1] for k in range(slots)], 1)
    out = lax.dot_general(
        one_hot(ids == wanted), pool, (((0,), (0,)), ((), ())), preferred_element_type=F32
    )
    blocks = by_swap(place, [out[k * capacity : (k + 1) * capacity] for k in range(slots)])
    for block, ref in zip(blocks, out_refs):
        ref[...] = block.astype(BF16)


def diagonal_steps(states, diag, wide_ref, prod_ref, insts, elems):
    tall = insts * elems
    width = diag.shape[1]
    cuts = [(j, j * LANE, min((j + 1) * LANE, width)) for j in range(pl.cdiv(width, LANE))]
    for t in range(insts):
        rows = states[t].astype(F32)
        for j, low, high in cuts:
            first = j * tall + t * elems
            wide_ref[first : first + elems, 0 : high - low] = rows[:, low:high]

    def some(begin, end):
        for e in range(begin, end):
            rows = jnp.concatenate(
                [wide_ref[pl.ds(j * tall + e, insts, stride=elems), :] for j, low, high in cuts], 1
            )
            product = jnp.dot(rows[:, 0:width].astype(BF16), diag[e], preferred_element_type=F32)
            for j, low, high in cuts:
                chunk = product[:, low:high]
                if high - low < LANE:
                    empty = jnp.zeros((insts, LANE - high + low), F32)
                    chunk = jnp.concatenate([chunk, empty], 1)
                prod_ref[pl.ds(j * tall + e, insts, stride=elems), :] = chunk

    def collect():
        return [
            jnp.concatenate(
                [
                    prod_ref[j * tall + t * elems : j * tall + (t + 1) * elems, 0 : high - low]
                    for j, low, high in cuts
                ],
                1,
            )
            for t in range(insts)
        ]

    return some, collect


def flux_order(rows, order):
    per_face = FIELDS * FIELDS * FPTS
    by_face = jnp.concatenate(
        [rows[:, f * per_face : (f + 1) * per_face] for f in range(FACES)], 0
    )
    return jnp.dot(by_face, order, preferred_element_type=F32).astype(BF16)


def source_table(sources, elems, slots):
    faces = FACES * elems
    columns = lax.broadcasted_iota(jnp.int32, (elems, faces + slots), 1)
    ids = jnp.where(columns < faces, FACES * (columns % elems) + columns // elems, columns)
    hot = [jnp.where(sources[:, f : f + 1] == ids, 1.0, 0.0) for f in range(FACES)]
    return jnp.concatenate(hot, 0).astype(BF16)


def spread_flux(wide, flux, insts):
    count = flux.shape[0]
    normal = []
    for t in range(insts):
        rows = wide[t * count : (t + 1) * count]
        summed = flux[:, 0:LANE] * rows[:, 0:LANE]
        for d in range(1, FIELDS):
            summed += flux[:, d * LANE : (d + 1) * LANE] * rows[:, d * LANE : (d + 1) * LANE]
        normal.append(summed.astype(BF16))
    return normal


def lift_faces(normal, lift, elems):
    rows = [
        jnp.concatenate([n[f * elems : (f + 1) * elems] for f in range(FACES)], 1) for n in normal
    ]
    return jnp.dot(jnp.concatenate(rows, 0), lift, preferred_element_type=F32)


def couple(entry_ref, states, t, shift, insts):
    summed = None
    for s in range(insts):
        d = (t - s + shift * insts) % NI
        term = entry_ref[d : d + 1, :] * states[s].astype(F32)
        summed = term if summed is None else summed + term
    return summed


def rotated(flux):
    place = lax.broadcasted_iota(jnp.int32, (flux.shape[0], LANE), 1) // FPTS
    blocks = []
    for k in range(LANE // FPTS):
        block = jnp.zeros((flux.shape[0], LANE), F32)
        for d in range(FIELDS):
            met = place == (d + k) % (LANE // FPTS)
            block = jnp.where(met, flux[:, d * LANE : (d + 1) * LANE], block)
        blocks.append(block)
    return jnp.concatenate(blocks, 1)


def slot_normal(blocks, factors, insts):
    count = blocks.shape[0]
    stacked = jnp.concatenate([blocks[:, t * LANE : (t + 1) * LANE] for t in range(insts)], 0)
    summed = [None] * insts
    for k in range(LANE // FPTS):
        turned = stacked if k == 0 else pltpu.roll(stacked, k * FPTS, 1)
        for t in range(insts):
            term = factors[:, k * LANE : (k + 1) * LANE] * turned[t * count : (t + 1) * count]
            summed[t] = term if k == 0 else summed[t] + term
    return [rows.astype(BF16) for rows in summed]


def table_kernel(spread_ref, order_ref):
    spread_ref[...] = spread_table()
    order_ref[...] = order_table()


def first_kernel(spectral, second, place_ref, freq_ref, spread_ref, state_ref, send_ref, *refs):
    insts, elems, width = state_ref.shape
    trace_refs, (entry_ref, pool_ref, *out_refs) = refs[:TRACE_TABLES], refs[TRACE_TABLES:]
    state = state_ref[...].reshape(insts * elems, width)
    pool = trace_pool(state, [ref[...] for ref in trace_refs], insts, elems)
    pool_ref[...] = pool
    fill_outgoing(pool, send_ref[0], out_refs, place_ref[0], elems)
    freq = freq_ref[0]
    for d in range(NI):
        entry = freq * float(spectral[d]) - dissipation * float(second[d])
        entry_ref[d : d + 1, :] = jnp.full((1, width), entry, F32)


def local_terms(states, diag, wide_ref, prod_ref, pool, hot, flux, spread, lift, insts, elems):
    some, collect = diagonal_steps(states, diag, wide_ref, prod_ref, insts, elems)
    quarter = elems // 4
    empty = jnp.zeros((hot.shape[1] - pool.shape[0], pool.shape[1]), BF16)
    pool = jnp.concatenate([pool, empty], 0)
    picked = jnp.dot(hot, pool, preferred_element_type=F32).astype(BF16)
    some(0, quarter)
    stacked = jnp.concatenate([picked[:, t * LANE : (t + 1) * LANE] for t in range(insts)], 0)
    wide = jnp.dot(stacked, spread, preferred_element_type=F32)
    some(quarter, 2 * quarter)
    normal = spread_flux(wide, flux.astype(F32), insts)
    some(2 * quarter, 3 * quarter)
    lifted = lift_faces(normal, lift, elems)
    some(3 * quarter, elems)
    products = collect()
    return [products[t] + lifted[t * elems : (t + 1) * elems] for t in range(insts)]


def slot_lift(blocks, factors, hot, lift, insts, elems):
    normal = slot_normal(blocks, factors, insts)
    empty = jnp.zeros((FACES * elems, insts * LANE), BF16)
    rows = jnp.concatenate([empty, jnp.concatenate(normal, 1)], 0)
    spots = jnp.dot(hot, rows, preferred_element_type=F32).astype(BF16)
    return lift_faces([spots[:, t * LANE : (t + 1) * LANE] for t in range(insts)], lift, elems)


def base_kernel(slots, state_ref, diag_ref, forcing_ref, entry_ref, pool_ref, flux_ref, source_ref,
                order_ref, spread_ref, lift_ref, spatial_ref, rest_ref, flux_out_ref, hot_ref,
                factor_ref, wide_ref, prod_ref):
    insts, elems, width = state_ref.shape
    hot = source_table(source_ref[...].T, elems, slots)
    flux = flux_order(flux_ref[...], order_ref[...])
    hot_ref[...] = hot
    flux_out_ref[...] = flux
    states = [state_ref[t] for t in range(insts)]
    spatial = local_terms(
        states, diag_ref, wide_ref, prod_ref, pool_ref[...], hot, flux, spread_ref[...],
        lift_ref[...], insts, elems,
    )
    factors = lax.dot_general(hot, flux, (((0,), (0,)), ((), ())), preferred_element_type=F32)
    factor_ref[...] = rotated(factors[FACES * elems :])
    for t in range(insts):
        spatial_ref[t] = spatial[t]
        rest_ref[t] = couple(entry_ref, states, t, 0, insts) - forcing_ref[t].astype(F32)


def last_base_kernel(state_ref, pool_ref, diag_ref, forcing_ref, hot_ref, flux_ref, spread_ref,
                     lift_ref, base_ref, wide_ref, prod_ref):
    insts, elems, width = state_ref.shape
    states = [state_ref[t].astype(BF16) for t in range(insts)]
    spatial = local_terms(
        states, diag_ref, wide_ref, prod_ref, pool_ref[...], hot_ref[...], flux_ref[...],
        spread_ref[...], lift_ref[...], insts, elems,
    )
    for t in range(insts):
        base_ref[t] = spatial[t] - forcing_ref[t].astype(F32)


def message_kernel(ranks, partial_ref, first_ref, base_ref, entry_ref, *refs):
    message_refs, (state_ref, out_ref) = refs[: ranks - 1], refs[ranks - 1 :]
    insts, elems, width = base_ref.shape
    firsts = [[first_ref[t] for t in range(insts)]]
    partials = [[partial_ref[t] for t in range(insts)]]
    for message_ref in message_refs:
        rows = [
            message_ref[i * elems : (i + 1) * elems, 0:width] for i in range(2 * insts)
        ]
        firsts.append(rows[:insts])
        partials.append(rows[insts:])
    states = []
    for k in range(ranks):
        of_rank = []
        for t in range(insts):
            state = partials[k][t].astype(F32)
            for j in range(ranks):
                if j != k:
                    state -= pseudo_step * couple(entry_ref, firsts[j], t, k - j, insts)
            of_rank.append(state.astype(BF16) if k == 0 else state)
        states.append(of_rank)
    for t in range(insts):
        state_ref[t] = states[0][t]
        coupling = base_ref[t]
        for k in range(ranks):
            coupling += couple(entry_ref, states[k], t, -k, insts)
        out_ref[t] = coupling


def received(parts, place, got_refs, order):
    got_refs = {swap: got_refs[i] for i, swap in enumerate(order)}
    arrived = by_offset(
        place, [got_refs[swap][...].astype(F32) for swap in range(len(OFFSETS))]
    )
    for k, offset in enumerate(OFFSETS):
        exists = (place + offset >= 0) & (place + offset < parts)
        arrived[k] = jnp.where(exists, arrived[k], jnp.zeros_like(arrived[k]))
    return jnp.concatenate(arrived, 0)


def step_kernel(parts, place_ref, *refs):
    got_refs, refs = refs[: len(OFFSETS)], refs[len(OFFSETS) :]
    trace_refs, refs = refs[:TRACE_TABLES], refs[TRACE_TABLES:]
    (state_ref, local_ref, rest_ref, hot_ref, factor_ref, lift_ref, send_ref,
     partial_ref, message_ref, next_pool_ref, *out_refs) = refs
    insts, elems, width = state_ref.shape
    place = place_ref[0]
    blocks = received(parts, place, got_refs, FIRST_ORDER)
    lifted = slot_lift(blocks, factor_ref[...], hot_ref[...], lift_ref[...], insts, elems)
    message_ref[...] = jnp.zeros_like(message_ref)
    fresh = []
    for t in range(insts):
        spatial = local_ref[t] + lifted[t * elems : (t + 1) * elems]
        moved = state_ref[t].astype(F32) - pseudo_step * (spatial + rest_ref[t])
        partial_ref[t] = moved
        fresh.append(moved.astype(BF16))
        lean = (moved - pseudo_step * spatial).astype(BF16)
        for i, block in enumerate((state_ref[t], lean)):
            low = (i * insts + t) * elems
            message_ref[low : low + elems, 0:width] = block
    tables_of_traces = [ref[...] for ref in trace_refs]
    pool = trace_pool(jnp.concatenate(fresh, 0), tables_of_traces, insts, elems)
    next_pool_ref[...] = pool
    fill_outgoing(pool, send_ref[0], out_refs, place, elems)


def last_kernel(parts, place_ref, *refs):
    got_refs, refs = refs[: len(OFFSETS)], refs[len(OFFSETS) :]
    (state_ref, base_ref, hot_ref, factor_ref, lift_ref, final_hbm, residual_hbm,
     final_ref, residual_ref, sems) = refs
    insts, elems, width = state_ref.shape
    blocks = received(parts, place_ref[0], got_refs, LAST_ORDER)
    lifted = slot_lift(blocks, factor_ref[...], hot_ref[...], lift_ref[...], insts, elems)
    for t in range(insts):
        residual = base_ref[t] + lifted[t * elems : (t + 1) * elems]
        residual_ref[t] = residual
        final_ref[t] = (state_ref[t].astype(F32) - pseudo_step * residual).astype(BF16)
    copies = [
        pltpu.make_async_copy(residual_ref, residual_hbm, sems.at[0]),
        pltpu.make_async_copy(final_ref, final_hbm, sems.at[1]),
    ]
    for copy in copies:
        copy.start()
    for copy in copies:
        copy.wait()


def on_device(
    initial_state, forcing, diagonal_blocks, flux_jacobian, send_list, source_index, frequency
):
    insts, elems, width = initial_state.shape
    parts = lax.axis_size("dom")
    ranks = lax.axis_size("inst")
    slots, capacity = send_list.shape[1:]
    faces = FACES * elems
    trace_np, lift_np, spectral, second = wide_tables()
    trace_wide = [jnp.asarray(part, BF16) for part in np.split(trace_np, TRACE_TABLES, 1)]
    lift_wide = jnp.asarray(lift_np, BF16)
    place = lax.axis_index("dom").reshape(1)
    sources = source_index.T
    routes = swap_routes(ranks, parts)

    smem = pl.BlockSpec(memory_space=pltpu.SMEM)
    vmem = pl.BlockSpec(memory_space=pltpu.VMEM)
    params = pltpu.CompilerParams(vmem_limit_bytes=VMEM_LIMIT)

    def like(array):
        return jax.ShapeDtypeStruct(array.shape, array.dtype)

    wide_shape = jax.ShapeDtypeStruct(initial_state.shape, F32)
    pool_shape = jax.ShapeDtypeStruct((faces, insts * LANE), BF16)
    out_shapes = [jax.ShapeDtypeStruct((capacity, insts * LANE), BF16)] * slots
    flux_shape = jax.ShapeDtypeStruct((faces, FIELDS * LANE), BF16)
    hot_shape = jax.ShapeDtypeStruct((faces, faces + slots * capacity), BF16)
    factor_shape = jax.ShapeDtypeStruct((slots * capacity, LANE // FPTS * LANE), F32)

    def exchange(outgoing, order):
        return [
            lax.ppermute(outgoing[swap], ("inst", "dom"), routes[swap]) for swap in order
        ]

    entry_shape = jax.ShapeDtypeStruct((NI, width), F32)
    message_shape = jax.ShapeDtypeStruct((2 * insts * elems, pl.cdiv(width, LANE) * LANE), BF16)
    chunks = [pltpu.VMEM((pl.cdiv(width, LANE) * insts * elems, LANE), F32)] * 2
    diag_cost = pl.CostEstimate(
        flops=2 * insts * diagonal_blocks.size, bytes_accessed=2 * diagonal_blocks.size,
        transcendentals=0,
    )
    spread, order = pl.pallas_call(
        table_kernel,
        out_shape=[
            jax.ShapeDtypeStruct((LANE, FIELDS * LANE), BF16),
            jax.ShapeDtypeStruct((FIELDS * FIELDS * FPTS, FIELDS * LANE), BF16),
        ],
        out_specs=[vmem] * 2,
        compiler_params=params,
        cost_estimate=pl.CostEstimate(flops=10**10, bytes_accessed=10**6, transcendentals=0),
        name="tables",
    )()
    freq, _ = lax.optimization_barrier((frequency, spread))
    entries, pool, *outgoing = pl.pallas_call(
        functools.partial(first_kernel, spectral, second),
        out_shape=[entry_shape, pool_shape] + out_shapes,
        in_specs=[smem] * 2 + [vmem] * (3 + TRACE_TABLES),
        out_specs=[vmem] * (2 + len(out_shapes)),
        compiler_params=params,
        cost_estimate=pl.CostEstimate(flops=10**10, bytes_accessed=10**6, transcendentals=0),
        name="first_traces",
    )(place, freq, spread, initial_state, send_list, *trace_wide)
    got = exchange(outgoing, FIRST_ORDER)
    local, rest, flux, hot, factors = pl.pallas_call(
        functools.partial(base_kernel, slots * capacity),
        out_shape=[wide_shape] * 2 + [flux_shape, hot_shape, factor_shape],
        in_specs=[vmem] * 10,
        out_specs=[vmem] * 5,
        scratch_shapes=chunks,
        compiler_params=params,
        cost_estimate=diag_cost,
        name="own_terms",
    )(initial_state, diagonal_blocks, forcing, entries, pool, flux_jacobian, sources, order, spread,
      lift_wide)
    partial, message, pool, *outgoing = pl.pallas_call(
        functools.partial(step_kernel, parts),
        out_shape=[wide_shape, message_shape, pool_shape] + out_shapes,
        in_specs=[smem] + [vmem] * (slots + 7 + TRACE_TABLES),
        out_specs=[vmem] * (3 + len(out_shapes)),
        compiler_params=params,
        name="first_step",
    )(place, *got, *trace_wide, initial_state, local, rest, hot, factors, lift_wide, send_list)
    messages = [
        lax.ppermute(message, "inst", [((i + rank) % ranks, i) for i in range(ranks)])
        for rank in range(1, ranks)
    ]
    got = exchange(outgoing, LAST_ORDER)
    base = pl.pallas_call(
        last_base_kernel,
        out_shape=wide_shape,
        in_specs=[vmem] * 8,
        out_specs=vmem,
        scratch_shapes=chunks,
        compiler_params=params,
        cost_estimate=diag_cost,
        name="last_own_terms",
    )(partial, pool, diagonal_blocks, forcing, hot, flux, spread, lift_wide)
    state, base = pl.pallas_call(
        functools.partial(message_kernel, ranks),
        out_shape=[like(initial_state), wide_shape],
        in_specs=[vmem] * (ranks + 3),
        out_specs=[vmem] * 2,
        compiler_params=params,
        name="message_terms",
    )(partial, initial_state, base, entries, *messages)
    return pl.pallas_call(
        functools.partial(last_kernel, parts),
        out_shape=[like(initial_state), wide_shape],
        in_specs=[smem] + [vmem] * (slots + 5),
        out_specs=[pl.BlockSpec(memory_space=pl.ANY)] * 2,
        scratch_shapes=[
            pltpu.VMEM(initial_state.shape, BF16),
            pltpu.VMEM(initial_state.shape, F32),
            pltpu.SemaphoreType.DMA((2,)),
        ],
        compiler_params=params,
        name="last_step",
    )(place, *got, state, base, hot, factors, lift_wide)


def solution(mesh):
    return jax.shard_map(
        on_device,
        mesh=mesh,
        in_specs=(
            P("inst", "dom", None),
            P("inst", "dom", None),
            P("dom", None, None),
            P("dom", None),
            P("dom", None, None),
            P("dom", None),
            P(),
        ),
        out_specs=(P("inst", "dom", None), P("inst", "dom", None)),
        check_vma=False,
    )
```
